32 devices in a mesh: seq: 8 (over y, x, core), tp: 4 (over z).
Axes of the slice: x: 2, y: 2, z: 4, core: 2. Of those that a mesh axis runs over, the one named last changes fastest.
Arguments:
- hidden_in: bfloat16 [5120, 1152], P('seq'), may hold values from -6 to 6
- cotangent: bfloat16 [5120, 1152], P('seq'), may hold values from -6 to 6
- modulation: bfloat16 [8, 6, 1152], P('seq'), may hold values from -3 to 3
- text_states: bfloat16 [8, 300, 1152], P('seq'), may hold values from -6 to 6
- image_shapes: int32 [8, 2], replicated, may hold values from 8 to 64, as said below
- text_lengths: int32 [8], replicated, may hold values from 75 to 300
- qkv_weight: bfloat16 [1152, 3, 1152], P(None, None, 'tp'), may hold values from -0.1875 to 0.1875
- attn_out_weight: bfloat16 [1152, 1152], P(None, 'tp'), may hold values from -1.75 to 1.75
- cross_q_weight: bfloat16 [1152, 1152], P(None, 'tp'), may hold values from -0.1875 to 0.1875
- cross_kv_weight: bfloat16 [1152, 2, 1152], P(None, None, 'tp'), may hold values from -0.1875 to 0.1875
- cross_out_weight: bfloat16 [1152, 1152], P(None, 'tp'), may hold values from -1.5 to 1.5
- up_weight: bfloat16 [1152, 2, 2880], P(None, None, 'tp'), may hold values from -0.1875 to 0.1875
- conv_weight: bfloat16 [9, 2, 2880], P(None, None, 'tp'), may hold values from -2 to 2
- down_weight: bfloat16 [1152, 2880], P(None, 'tp'), may hold values from -0.3125 to 0.3125
Outputs:
- output: bfloat16 [5120, 1152], P('seq')
- input_grad: float32 [5120, 1152], P('seq')
- modulation_grad: float32 [8, 6, 1152], P('seq')
- qkv_grad: float32 [1152, 3, 1152], P('seq', None, 'tp')
- attn_out_grad: float32 [1152, 1152], P('seq', 'tp')
- cross_q_grad: float32 [1152, 1152], P('seq', 'tp')
- cross_kv_grad: float32 [1152, 2, 1152], P('seq', None, 'tp')
- cross_out_grad: float32 [1152, 1152], P('seq', 'tp')
- up_grad: float32 [1152, 2, 2880], P('seq', None, 'tp')
- conv_grad: float32 [9, 2, 2880], P(None, None, 'tp')
- down_grad: float32 [1152, 2880], P('seq', 'tp')
The draws below stay inside these ranges and needn't reach their ends.
Inputs may be any that keep to these rules, and one draw needn't show every extreme that they name: `image_shapes`: images 2k and 2k + 1 together have exactly 1280 patches and the same width, 32 or 16; a width of 32 comes with heights of 8 to 32, a width of 16 with heights of 16 to 64.
All inputs are finite; a program needn't handle non-finite values.
Results may differ from the reference program's by a relative error of at most 0.02.
Values may be sent and summed in bfloat16 or wider, within the bound.
No kernel may reach another device: no remote copies, remote signals or barrier semaphores. Data moves between devices by JAX's collectives and lax.ppermute only.
A program may use at most 256 MiB of HBM per device.

```python
import math
import jax
import jax.numpy as jnp
from jax import lax

D = 1152
SELF_HEADS = 36
HEAD = 32
CROSS_HEADS = 16
CROSS_HEAD = 72
FF = 2880
CTX = 300
MAXW = 32
TOK_DEV = 640
TOKENS = 5120
IMAGES = 8
SELF_W = 1152
CROSS_W = 1152
HALO = 33


def draw_modulation(key, part):
    factors = jnp.array([0.1, 0.3, 1.0, 0.3, 0.3, 1.0], jnp.float32)
    drawn = jnp.clip(jax.random.normal(key, (IMAGES, 6, D), jnp.float32), -3.0, 3.0)
    return (drawn * factors[None, :, None]).astype(jnp.bfloat16)


def draw_image_shapes(key, part):
    pair_count = IMAGES // 2
    first_key, second_key = jax.random.split(key)
    broad = jax.random.randint(first_key, (pair_count,), 0, 2, jnp.int32)
    broad = broad.at[0].set(1).at[1].set(0)
    lowest = jnp.where(broad == 1, MAXW // 4, MAXW // 2)
    summed = jnp.where(broad == 1, 5 * MAXW // 4, 5 * MAXW // 2)
    spread_draw = jax.random.randint(second_key, (pair_count,), 0, 1 << 20, jnp.int32)
    leading = lowest + spread_draw % (summed - 2 * lowest + 1)
    leading = leading.at[0].set(MAXW // 4).at[1].set(2 * MAXW)
    trailing = summed - leading
    widths = jnp.where(broad == 1, MAXW, MAXW // 2)
    heights = jnp.stack([leading, trailing], axis=1).reshape(-1)
    columns = jnp.repeat(widths, 2)
    return jnp.stack([heights, columns], axis=1).astype(jnp.int32)


def draw_text_lengths(key, part):
    drawn = jax.random.randint(key, (IMAGES,), CTX // 4, CTX + 1, jnp.int32)
    return drawn.at[0].set(CTX)


def raised(values, stream_key, source, target, blocks, factor):
    def block_of(position):
        return (jnp.arange(values.shape[position]) // (values.shape[position] // blocks)).reshape((-1,) + (1,) * (values.ndim - 1 - position))

    one_side = jax.random.permutation(stream_key, blocks)[block_of(target)]
    other_side = (block_of(target) + blocks // 2) % blocks
    return jnp.where((block_of(source) == one_side) | (block_of(source) == other_side), factor * values, values)


def steps_of(rng, shape, shards, least, largest):
    def one(dim, blocks):
        steps = jax.random.uniform(jax.random.fold_in(jax.random.fold_in(rng, 6), dim), (blocks,), jnp.float32, least / len(shards), largest / len(shards))
        return jnp.repeat(jnp.exp(steps), shape[dim] // blocks).reshape((-1,) + (1,) * (len(shape) - dim - 1))

    factor_of = one(*shards[0])
    for cut in shards[1:]:
        factor_of = factor_of * one(*cut)
    return factor_of


def scatter_about(key, dims, deviation, reach, cuts=(), kind=jnp.bfloat16):
    level = steps_of(key, dims, cuts, -0.22, 0.18) if cuts else 1.0
    result = jax.random.normal(key, dims, jnp.float32) * deviation * level
    return jnp.minimum(jnp.maximum(result, -reach), reach).astype(kind)


def bell_draw_with(rng, extent, deviation, reach, pieces, heavy, kind=jnp.bfloat16):
    values = deviation * jax.random.normal(rng, extent, jnp.float32)
    if pieces:
        values = values * steps_of(rng, extent, pieces, -0.22, 0.18)
    return jnp.clip(raised(values, jax.random.fold_in(rng, 3), *heavy), -reach, reach).astype(kind)


def setup_inputs(seed: int = 0) -> dict:
    splits = jax.random.split(jax.random.key(seed), 15)
    return {
        "hidden_in": bell_draw_with(splits[0], (TOKENS, D), 1.0, 6.0, ((0, 8),), (0, 1, 8, 2.0)),
        "cotangent": bell_draw_with(splits[1], (TOKENS, D), 1.0, 6.0, ((0, 8),), (0, 1, 8, 2.0)),
        "modulation": draw_modulation(jax.random.fold_in(splits[14], 71), 0),
        "text_states": scatter_about(splits[3], (IMAGES, CTX, D), 1.0, 6.0, ((0, 8),)),
        "image_shapes": draw_image_shapes(jax.random.fold_in(splits[14], 71), 0),
        "text_lengths": draw_text_lengths(jax.random.fold_in(splits[14], 71), 0),
        "qkv_weight": scatter_about(splits[6], (D, 3, SELF_W), D ** -0.5, 0.1875, ((2, 4),)),
        "attn_out_weight": scatter_about(splits[7], (D, SELF_W), 12 ** -0.5, 1.75, ((1, 4),)),
        "cross_q_weight": scatter_about(splits[8], (D, CROSS_W), D ** -0.5, 0.1875, ((1, 4),)),
        "cross_kv_weight": scatter_about(splits[9], (D, 2, CROSS_W), D ** -0.5, 0.1875, ((2, 4),)),
        "cross_out_weight": scatter_about(splits[10], (D, CROSS_W), 16 ** -0.5, 1.5, ((1, 4),)),
        "up_weight": scatter_about(splits[11], (D, 2, FF), D ** -0.5, 0.1875, ((2, 4),)),
        "conv_weight": scatter_about(splits[12], (9, 2, FF), 9 ** -0.5, 2.0, ((2, 4),)),
        "down_weight": scatter_about(splits[13], (D, FF), (FF // 8) ** -0.5, 0.3125, ((1, 4),)),
    }


@jax.custom_vjp
def low(v):
    return lax.optimization_barrier(v.astype(jnp.bfloat16)).astype(jnp.float32)

@jax.custom_vjp
def low_back(v):
    return v

def low_keep(v):
    return (low(v), None)

def low_pass(kept, grad):
    return (grad,)

def back_keep(v):
    return (v, None)

def back_low(kept, grad):
    return (low(grad),)
low.defvjp(low_keep, low_pass)
low_back.defvjp(back_keep, back_low)
EPSILON = 1e-06
PRECISE = lax.Precision.HIGHEST
MASKED_OUT = -1e+30

def product(left_side, right_side):
    return jnp.dot(left_side, right_side, precision=PRECISE)

def modulated_norm(inputs, shifts, scales):
    inverse = lax.rsqrt(lax.optimization_barrier(jnp.mean(inputs * inputs, axis=-1, keepdims=True)) + EPSILON)
    return inputs * inverse * (1.0 + scales) + shifts

def sequence_block(weights, inputs, mod_pair, text_pair, shape_pair, length_pair):
    qkv_weight, attn_out_weight, cross_q_weight, cross_kv_weight, cross_out_weight, up_weight, conv_weight, down_weight = weights
    seq_tokens = inputs.shape[0]
    places = jnp.arange(seq_tokens, dtype=jnp.int32)
    row_width = shape_pair[0, 1]
    size_first = shape_pair[0, 0] * row_width
    second = places >= size_first
    within = places - jnp.where(second, size_first, 0)
    row_index = within // row_width
    col_index = within % row_width
    height = jnp.where(second, shape_pair[1, 0], shape_pair[0, 0])
    length = jnp.where(second, length_pair[1], length_pair[0])
    second_float = second.astype(jnp.float32)
    image_masks = jnp.stack([1.0 - second_float, second_float])

    def per_token(row_pick):
        return jnp.where(second[:, None], mod_pair[1, row_pick], mod_pair[0, row_pick])
    normed = modulated_norm(inputs, per_token(0), per_token(1))
    projected = low_back(product(low(normed), qkv_weight.reshape(D, 3 * SELF_W)))
    projected = projected.reshape(seq_tokens, 3, SELF_HEADS, HEAD)
    self_queries = low(jax.nn.softplus(projected[:, 0]))
    self_keys = low(jax.nn.softplus(projected[:, 1]))
    self_values = low(projected[:, 2])
    kernels = jnp.einsum('it,tzd,tze->izde', image_masks, self_keys, self_values, precision=PRECISE)
    key_totals = jnp.einsum('it,tzd->izd', image_masks, self_keys, precision=PRECISE)
    numerators = jnp.einsum('tzd,izde->itze', self_queries, kernels, precision=PRECISE)
    denominators = jnp.einsum('tzd,izd->itz', self_queries, key_totals, precision=PRECISE)
    numerator = jnp.where(second[:, None, None], numerators[1], numerators[0])
    denominator = jnp.where(second[:, None], denominators[1], denominators[0]) + 1.0
    attended = low(numerator / denominator[:, :, None]).reshape(seq_tokens, SELF_W)
    attn_branch = low_back(product(attended, attn_out_weight.T))
    after_attn = inputs + per_token(2) * attn_branch
    cross_queries = low(low_back(product(low(after_attn), cross_q_weight)))
    cross_queries = cross_queries.reshape(seq_tokens, CROSS_HEADS, CROSS_HEAD)
    text_kv = low(low_back(jnp.einsum('jsc,cm->jsm', text_pair, cross_kv_weight.reshape(D, 2 * CROSS_W), precision=PRECISE)))
    text_keys = text_kv[:, :, :CROSS_W].reshape(2, CTX, CROSS_HEADS, CROSS_HEAD)
    text_values = text_kv[:, :, CROSS_W:].reshape(2, CTX, CROSS_HEADS, CROSS_HEAD)
    raw_scores = jnp.einsum('tzd,jszd->tzjs', cross_queries, text_keys, precision=PRECISE) * (1.0 / math.sqrt(CROSS_HEAD))
    scores = low_back(jnp.where(second[:, None, None], raw_scores[:, :, 1], raw_scores[:, :, 0]))
    key_live = jnp.arange(CTX, dtype=jnp.int32)[None, :] < length[:, None]
    attn_probs = jax.nn.softmax(jnp.where(key_live[:, None, :], scores, MASKED_OUT), axis=-1)
    probs_pair = low(attn_probs)[:, :, None, :] * image_masks.T[:, None, :, None]
    attended_text = jnp.einsum('tzjs,jszd->tzd', probs_pair, text_values, precision=PRECISE)
    text_mixed = low(low_back(attended_text)).reshape(seq_tokens, CROSS_W)
    cross_branch = low_back(product(text_mixed, cross_out_weight.T))
    after_cross = after_attn + cross_branch
    normed_two = modulated_norm(after_cross, per_token(3), per_token(4))
    up_proj = low_back(product(low(normed_two), up_weight.reshape(D, 2 * FF)))
    activated = low(jax.nn.silu(up_proj))
    padded = jnp.pad(activated, ((HALO, HALO), (0, 0)))
    conv_taps = conv_weight.reshape(9, 2 * FF)
    mixture = jnp.zeros_like(up_proj)
    for tap_index in range(9):
        row_step = tap_index // 3 - 1
        col_step = tap_index % 3 - 1
        offset = (row_step * row_width + col_step + HALO).astype(jnp.int32)
        shifted = lax.dynamic_slice_in_dim(padded, offset, seq_tokens, 0)
        inside = (row_index + row_step >= 0) & (row_index + row_step < height) & (col_index + col_step >= 0) & (col_index + col_step < row_width)
        mixture = mixture + jnp.where(inside[:, None], shifted, 0.0) * conv_taps[tap_index]
    mixture = low_back(mixture)
    hidden = low(mixture[:, :FF] * jax.nn.silu(mixture[:, FF:]))
    ffn_branch = low_back(product(hidden, down_weight.T))
    return after_cross + per_token(5) * ffn_branch

def reference(hidden_in, cotangent, modulation, text_states, image_shapes, text_lengths, qkv_weight, attn_out_weight, cross_q_weight, cross_kv_weight, cross_out_weight, up_weight, conv_weight, down_weight):
    pair_count = IMAGES // 2
    seq_tokens = 2 * TOK_DEV
    inputs_all = hidden_in.astype(jnp.float32).reshape(pair_count, seq_tokens, D)
    text_all = text_states.astype(jnp.float32).reshape(pair_count, 2, CTX, D)
    shape_all = image_shapes.reshape(pair_count, 2, 2)
    length_all = text_lengths.reshape(pair_count, 2)
    weights = tuple((weight.astype(jnp.float32) for weight in (qkv_weight, attn_out_weight, cross_q_weight, cross_kv_weight, cross_out_weight, up_weight, conv_weight, down_weight)))
    block_fn = jax.checkpoint(sequence_block)

    def forward(inputs_given, mod_given, weights_given):
        mod_pairs = mod_given.reshape(pair_count, 2, 6, D)

        def scan_step(carried, sliced):
            return (carried, block_fn(weights_given, *sliced))
        unused, results = lax.scan(scan_step, jnp.zeros((), jnp.float32), (inputs_given, mod_pairs, text_all, shape_all, length_all))
        return results
    results, pullback = jax.vjp(forward, inputs_all, modulation.astype(jnp.float32), weights)
    input_grads, mod_grads, weight_grads = pullback(cotangent.astype(jnp.float32).reshape(pair_count, seq_tokens, D))
    output = results.reshape(TOKENS, D).astype(jnp.bfloat16)
    return (output, input_grads.reshape(TOKENS, D), mod_grads, weight_grads[0], weight_grads[1], weight_grads[2], weight_grads[3], weight_grads[4], weight_grads[5], weight_grads[6], weight_grads[7])
```

```python
import math

import jax
import jax.numpy as jnp
from jax import lax
from jax.sharding import PartitionSpec as P

HEAD = 32
CROSS_HEAD = 72
MAXW = 32


EPSILON = 1e-06
PRECISE = lax.Precision.HIGHEST
MASKED_OUT = -1e30
LOW = jnp.bfloat16
WIDE = jnp.float32


def swapped(block, axis, apart):
    count = lax.axis_size(axis)
    route = [(low, low ^ (1 << apart)) for low in range(count)]
    return lax.ppermute(block, axis, route)


def from_behind(block, step):
    count = lax.axis_size("tp")
    return lax.ppermute(block, "tp", [(k, (k + step) % count) for k in range(count)])


def from_ahead(block, step):
    count = lax.axis_size("tp")
    return lax.ppermute(block, "tp", [(k, (k - step) % count) for k in range(count)])


def bit_of(index, place):
    return (index >> place) & 1


def modulated_norm(inputs, shifts, scales):
    inverse = lax.rsqrt(jnp.mean(inputs * inputs, axis=-1, keepdims=True) + EPSILON)
    return inputs * inverse * (1.0 + scales) + shifts


def glu_product(value_in, gate_in):
    return value_in * jax.nn.silu(gate_in)


def times_transposed(left_side, right_side):
    return lax.dot_general(
        left_side, right_side, (((1,), (1,)), ((), ())), preferred_element_type=WIDE
    )


def over_tokens(left_side, right_side):
    return lax.dot_general(
        left_side, right_side, (((0,), (0,)), ((), ())), preferred_element_type=WIDE
    )


def by_image(second, pair_values):
    return jnp.where(
        second.reshape((-1,) + (1,) * (pair_values.ndim - 2)), pair_values[1], pair_values[0]
    )


def keep_and_send(grid, bit, axis):
    keep = lax.dynamic_index_in_dim(grid, bit, axis, keepdims=False)
    send = lax.dynamic_index_in_dim(grid, 1 - bit, axis, keepdims=False)
    return keep, send


def halved(grid, index, place, axis):
    keep, send = keep_and_send(grid, bit_of(index, place), axis)
    return keep + swapped(send.astype(LOW), "seq", place).astype(WIDE)


def sum_rows(grad):
    count = lax.axis_size("seq")
    index = lax.axis_index("seq")
    places = count.bit_length() - 1
    rows, columns = grad.shape
    own = rows // count
    grid = grad.reshape((2,) * places + (own, columns))
    grid = halved(grid, index, 0, places - 1)
    halves = []
    for part in range(2):
        order = list(range(1, places))
        if part:
            order = order[1:] + order[:1]
        piece = lax.slice_in_dim(
            grid, part * (own // 2), (part + 1) * (own // 2), axis=places - 1
        )
        left = list(range(places - 1, 0, -1))
        for place in order:
            piece = halved(piece, index, place, left.index(place))
            left.remove(place)
        halves.append(piece)
    return jnp.concatenate(halves, axis=0)


def gather_shards(weight, flip):
    index = lax.axis_index("seq")
    rows, columns = weight.shape
    own = rows // 8
    eighth = lax.dynamic_slice_in_dim(weight, (index % 8) * own, own, 0)
    shards = [weight]
    for step in range(1, lax.axis_size("tp")):
        piece = from_behind(eighth, step)[None]
        order = (1, 2) if (step + flip) % 2 else (2, 1)
        grid = piece.reshape(1, 1, 1, own, columns)
        for place in (*order, 0):
            axis = 2 - place
            other = swapped(grid, "seq", place)
            first = bit_of(index, place) == 0
            grid = jnp.where(
                first,
                jnp.concatenate([grid, other], axis=axis),
                jnp.concatenate([other, grid], axis=axis),
            )
        shards.append(grid.reshape(rows, columns))
    return shards


def gather_blocks(block):
    count = lax.axis_size("tp")
    place = lax.axis_index("tp")
    result = jnp.zeros((count,) + block.shape, block.dtype)
    result = lax.dynamic_update_index_in_dim(result, block, place, 0)
    for step in range(1, count):
        result = lax.dynamic_update_index_in_dim(
            result, from_behind(block, step), (place - step) % count, 0
        )
    return result.reshape((count * block.shape[0],) + block.shape[1:])


def token_block(values, place):
    count = lax.axis_size("tp")
    size = values.shape[0] // count
    return lax.dynamic_slice_in_dim(values, (place % count) * size, size, 0)


def scatter_product(left_side, right_side):
    count = lax.axis_size("tp")
    place = lax.axis_index("tp")
    sent = [
        from_behind(
            times_transposed(token_block(left_side, place + step), right_side).astype(LOW), step
        )
        for step in range(1, count)
    ]
    total = times_transposed(token_block(left_side, place), right_side)
    for piece in sent:
        total = total + piece.astype(WIDE)
    return total


def same_everywhere(block):
    pair = block + swapped(block, "tp", 0)
    return pair + swapped(pair, "tp", 1)


def shards(
    hidden_in,
    cotangent,
    modulation,
    text_states,
    image_shapes,
    text_lengths,
    qkv_weight,
    attn_out_weight,
    cross_q_weight,
    cross_kv_weight,
    cross_out_weight,
    up_weight,
    conv_weight,
    down_weight,
):
    tokens_here, model_width = hidden_in.shape
    context = text_states.shape[1]
    self_cols = qkv_weight.shape[2]
    cross_cols = cross_q_weight.shape[1]
    ffn_cols = up_weight.shape[2]
    self_heads = self_cols // HEAD
    cross_heads = cross_cols // CROSS_HEAD
    score_scale = 1.0 / math.sqrt(CROSS_HEAD)
    rim_depth = MAXW + 1
    tp_count = lax.axis_size("tp")
    tp_index = lax.axis_index("tp")
    block_size = tokens_here // tp_count
    seq_index = lax.axis_index("seq")
    first_half = seq_index % 2 == 0
    pair_index = seq_index // 2
    pair_shapes = lax.dynamic_slice_in_dim(image_shapes, 2 * pair_index, 2, 0)
    pair_lengths = lax.dynamic_slice_in_dim(text_lengths, 2 * pair_index, 2, 0)
    row_width = pair_shapes[0, 1]
    size_first = pair_shapes[0, 0] * row_width
    places = jnp.arange(tokens_here, dtype=jnp.int32) + jnp.where(first_half, 0, tokens_here)
    second = places >= size_first
    within = places - jnp.where(second, size_first, 0)
    row_index = within // row_width
    col_index = within % row_width
    height = jnp.where(second, pair_shapes[1, 0], pair_shapes[0, 0])
    second_float = second.astype(WIDE)
    image_masks = jnp.stack([1.0 - second_float, second_float])
    mask_low = image_masks.astype(LOW)
    block_second = token_block(second, tp_index)
    block_float = block_second.astype(WIDE)[:, None]

    def inside(row_step, col_step):
        return (
            (row_index + row_step >= 0)
            & (row_index + row_step < height)
            & (col_index + col_step >= 0)
            & (col_index + col_step < row_width)
        )

    text_rows = text_states[0]
    kv_own = jnp.dot(
        text_rows,
        cross_kv_weight.reshape(model_width, 2 * cross_cols),
        preferred_element_type=WIDE,
    ).astype(LOW)
    mod_own = modulation[0]
    mod_other = swapped(mod_own, "seq", 0)
    mod_pair = jnp.where(
        first_half, jnp.stack([mod_own, mod_other]), jnp.stack([mod_other, mod_own])
    ).astype(WIDE)

    out_shards = gather_shards(attn_out_weight, 0)
    query_shards = gather_shards(cross_q_weight, 1)
    kv_shards = jnp.stack([kv_own] + [from_behind(kv_own, step) for step in range(1, tp_count)])
    cross_shards = gather_shards(cross_out_weight, 0)
    kv_other = swapped(kv_shards, "seq", 0)
    kv_pair = jnp.where(
        first_half,
        jnp.stack([kv_shards, kv_other], axis=1),
        jnp.stack([kv_other, kv_shards], axis=1),
    )

    def per_token(row_pick):
        return jnp.where(second[:, None], mod_pair[1, row_pick], mod_pair[0, row_pick])

    def per_block(row_pick):
        return jnp.where(block_second[:, None], mod_pair[1, row_pick], mod_pair[0, row_pick])

    def image_sums(member):
        late = jnp.sum(member * block_float, axis=0)
        return jnp.stack([jnp.sum(member * (1.0 - block_float), axis=0), late])

    inputs = hidden_in.astype(WIDE)
    gate_ffn = per_token(5)
    normed_low = modulated_norm(inputs, per_token(0), per_token(1)).astype(LOW)
    qkv_flat = qkv_weight.reshape(model_width, 3 * self_cols)
    projected = jnp.dot(normed_low, qkv_flat, preferred_element_type=WIDE).reshape(
        tokens_here, 3, self_heads, HEAD
    )
    self_queries = jax.nn.softplus(projected[:, 0]).astype(LOW)
    self_keys = jax.nn.softplus(projected[:, 1]).astype(LOW)
    self_values = projected[:, 2].astype(LOW)
    masked_keys = self_keys[None] * mask_low[:, :, None, None]
    kernel_part = jnp.einsum(
        "itzd,tze->izde", masked_keys, self_values, preferred_element_type=WIDE
    )
    total_part = jnp.einsum("it,tzd->izd", mask_low, self_keys, preferred_element_type=WIDE)
    kernel_other, total_other = swapped((kernel_part, total_part), "seq", 0)
    kernels = kernel_part + kernel_other
    key_totals = total_part + total_other
    queries_wide = self_queries.astype(WIDE)
    numerators = jnp.einsum("tzd,izde->itze", queries_wide, kernels, precision=PRECISE)
    denominators = jnp.einsum("tzd,izd->itz", queries_wide, key_totals, precision=PRECISE)
    numerator = by_image(second, numerators)
    denominator = by_image(second, denominators) + 1.0
    attended = numerator / denominator[:, :, None]
    attended_low = attended.reshape(tokens_here, self_cols).astype(LOW)

    block_inputs = token_block(hidden_in, tp_index).astype(WIDE)
    block_upstream = token_block(cotangent, tp_index).astype(WIDE)
    attended_blocks = [token_block(attended_low, tp_index)] + [
        from_behind(token_block(attended_low, tp_index + step), step)
        for step in range(1, tp_count)
    ]
    attn_branch = sum(
        times_transposed(block, shard) for block, shard in zip(attended_blocks, out_shards)
    )
    gate_attn = per_block(2)
    after_attn = block_inputs + gate_attn * attn_branch
    after_low = after_attn.astype(LOW)
    query_low = [
        jnp.dot(after_low, shard, preferred_element_type=WIDE).astype(LOW)
        for shard in query_shards
    ]
    heads_all = tp_count * cross_heads
    cross_queries = (
        jnp.stack(query_low)
        .reshape(tp_count, block_size, cross_heads, CROSS_HEAD)
        .transpose(0, 2, 1, 3)
        .reshape(heads_all, block_size, CROSS_HEAD)
    )
    text_kv = (
        kv_pair.reshape(tp_count, 2 * context, 2, cross_heads, CROSS_HEAD)
        .transpose(2, 0, 3, 1, 4)
        .reshape(2, heads_all, 2 * context, CROSS_HEAD)
    )
    text_keys, text_values = text_kv[0], text_kv[1]
    key_place = jnp.arange(2 * context, dtype=jnp.int32)
    key_second = key_place >= context
    key_within = key_place - jnp.where(key_second, context, 0)
    key_length = jnp.where(key_second, pair_lengths[1], pair_lengths[0])
    key_live = (key_within < key_length)[None, :] & (key_second[None, :] == block_second[:, None])
    scores = (
        jnp.einsum("ztd,zsd->zts", cross_queries, text_keys, preferred_element_type=WIDE)
        * score_scale
    )
    masked = jnp.where(key_live[None], scores, MASKED_OUT)
    row_max = jnp.max(masked, axis=-1, keepdims=True)
    exp_scores = jnp.exp(masked - row_max)
    attn_probs = exp_scores / jnp.sum(exp_scores, axis=-1, keepdims=True)
    probs_low = attn_probs.astype(LOW)
    attended_text = jnp.einsum(
        "zts,zsd->ztd", probs_low, text_values, preferred_element_type=WIDE
    ).astype(LOW)

    def to_shards(heads):
        return (
            heads.reshape(tp_count, cross_heads, block_size, CROSS_HEAD)
            .transpose(0, 2, 1, 3)
            .reshape(tp_count, block_size, cross_cols)
        )

    text_low = to_shards(attended_text)
    cross_branch = sum(
        times_transposed(text_low[step], cross_shards[step]) for step in range(tp_count)
    )
    after_cross = after_attn + cross_branch
    normed_two, norm_two_back = jax.vjp(modulated_norm, after_cross, per_block(3), per_block(4))
    normed_two_low = gather_blocks(normed_two.astype(LOW))
    up_flat = up_weight.reshape(model_width, 2 * ffn_cols)
    up_proj = jnp.dot(normed_two_low, up_flat, preferred_element_type=WIDE)
    activated = jax.nn.silu(up_proj).astype(LOW)
    conv_taps = conv_weight.reshape(9, 2 * ffn_cols).astype(WIDE)
    rim_in = swapped(jnp.where(first_half, activated[-rim_depth:], activated[:rim_depth]), "seq", 0)
    zero_rim = jnp.zeros_like(rim_in)
    padded = jnp.concatenate(
        [
            jnp.where(first_half, zero_rim, rim_in),
            activated,
            jnp.where(first_half, rim_in, zero_rim),
        ],
        axis=0,
    )
    mixture = jnp.zeros_like(up_proj)
    for tap_index in range(9):
        row_step = tap_index // 3 - 1
        col_step = tap_index % 3 - 1
        offset = row_step * row_width + col_step
        shifted = lax.dynamic_slice_in_dim(padded, rim_depth + offset, tokens_here, 0)
        mixture = (
            mixture
            + jnp.where(inside(row_step, col_step)[:, None], shifted.astype(WIDE), 0.0)
            * conv_taps[tap_index]
        )
    hidden, gating_back = jax.vjp(glu_product, mixture[:, :ffn_cols], mixture[:, ffn_cols:])
    hidden_low = hidden.astype(LOW)
    upstream = cotangent.astype(WIDE)
    grad_ffn = (upstream * gate_ffn).astype(LOW)
    grad_hidden = jnp.dot(grad_ffn, down_weight, preferred_element_type=WIDE)
    grad_value, grad_gating = gating_back(grad_hidden)
    grad_mixture = jnp.concatenate([grad_value, grad_gating], axis=1).astype(LOW)
    rim_back = swapped(
        jnp.where(first_half, grad_mixture[-rim_depth:], grad_mixture[:rim_depth]), "seq", 0
    )
    ffn_branch = scatter_product(hidden_low, down_weight)
    output_block = (after_cross + per_block(5) * ffn_branch).astype(LOW)
    down_part = over_tokens(grad_ffn, hidden_low)
    grad_padded = jnp.concatenate(
        [
            jnp.where(first_half, zero_rim, rim_back),
            grad_mixture,
            jnp.where(first_half, rim_back, zero_rim),
        ],
        axis=0,
    )
    grad_mix_wide = grad_mixture.astype(WIDE)
    grad_activated = jnp.zeros_like(up_proj)
    tap_grads = []
    for tap_index in range(9):
        row_step = tap_index // 3 - 1
        col_step = tap_index % 3 - 1
        offset = row_step * row_width + col_step
        source = lax.dynamic_slice_in_dim(grad_padded, rim_depth - offset, tokens_here, 0)
        grad_activated = (
            grad_activated
            + jnp.where(inside(-row_step, -col_step)[:, None], source.astype(WIDE), 0.0)
            * conv_taps[tap_index]
        )
        shifted = lax.dynamic_slice_in_dim(padded, rim_depth + offset, tokens_here, 0)
        tap_grads.append(
            jnp.sum(
                jnp.where(inside(row_step, col_step)[:, None], shifted.astype(WIDE), 0.0)
                * grad_mix_wide,
                axis=0,
            )
        )
    conv_sum = jnp.stack(tap_grads)
    sigmoid_up = jax.nn.sigmoid(up_proj)
    grad_up_low = (grad_activated * sigmoid_up * (1.0 + up_proj * (1.0 - sigmoid_up))).astype(LOW)
    grad_norm_two = scatter_product(grad_up_low, up_flat)
    up_part = over_tokens(normed_two_low, grad_up_low)

    grad_cross_in, grad_shift_ffn, grad_scale_ffn = norm_two_back(grad_norm_two)
    grad_after_cross = block_upstream + grad_cross_in
    grad_cross = grad_after_cross.astype(LOW)
    cross_out_part = [over_tokens(grad_cross, text_low[step]) for step in range(tp_count)]
    grad_text = jnp.stack(
        [
            jnp.dot(grad_cross, shard, preferred_element_type=WIDE).astype(LOW)
            for shard in cross_shards
        ]
    )

    def to_heads(blocks):
        return (
            blocks.reshape(tp_count, block_size, cross_heads, CROSS_HEAD)
            .transpose(0, 2, 1, 3)
            .reshape(heads_all, block_size, CROSS_HEAD)
        )

    grad_text_heads = to_heads(grad_text)
    grad_probs = jnp.einsum(
        "ztd,zsd->zts", grad_text_heads, text_values, preferred_element_type=WIDE
    )
    grad_values = jnp.einsum(
        "zts,ztd->zsd", probs_low, grad_text_heads, preferred_element_type=WIDE
    )
    grad_scores = (
        attn_probs * (grad_probs - jnp.sum(attn_probs * grad_probs, axis=-1, keepdims=True))
    ).astype(LOW)
    grad_queries = (
        jnp.einsum("zts,zsd->ztd", grad_scores, text_keys, preferred_element_type=WIDE)
        * score_scale
    )
    grad_keys = (
        jnp.einsum("zts,ztd->zsd", grad_scores, cross_queries, preferred_element_type=WIDE)
        * score_scale
    )
    grad_query_low = to_shards(grad_queries.astype(LOW))
    cross_q_part = [over_tokens(after_low, grad_query_low[step]) for step in range(tp_count)]
    grad_after_attn = grad_after_cross + sum(
        times_transposed(grad_query_low[step], query_shards[step]) for step in range(tp_count)
    )

    grad_gate_attn = grad_after_attn * attn_branch
    grad_attn = (grad_after_attn * gate_attn).astype(LOW)
    grad_attended_blocks = [
        jnp.dot(grad_attn, shard, preferred_element_type=WIDE).astype(LOW) for shard in out_shards
    ]
    attn_out_part = [over_tokens(grad_attn, block) for block in attended_blocks]
    grad_attended = jnp.zeros((tp_count, block_size, self_cols), LOW)
    for step in range(tp_count):
        piece = grad_attended_blocks[step]
        if step:
            piece = from_ahead(piece, step)
        grad_attended = lax.dynamic_update_index_in_dim(
            grad_attended, piece, (tp_index + step) % tp_count, 0
        )
    grad_attended = grad_attended.reshape(tokens_here, self_heads, HEAD).astype(WIDE)
    grad_numer = grad_attended / denominator[:, :, None]
    grad_denom = -jnp.sum(grad_attended * attended, axis=-1) / denominator
    grad_kernel_part = jnp.einsum(
        "it,tzd,tze->izde", image_masks, queries_wide, grad_numer, precision=PRECISE
    )
    grad_total_part = jnp.einsum(
        "it,tzd,tz->izd", image_masks, queries_wide, grad_denom, precision=PRECISE
    )
    kernel_back_other, total_back_other = swapped((grad_kernel_part, grad_total_part), "seq", 0)
    grad_kernels = grad_kernel_part + kernel_back_other
    grad_totals = grad_total_part + total_back_other
    grad_q_pair = (
        jnp.einsum("tze,izde->itzd", grad_numer, kernels, precision=PRECISE)
        + grad_denom[None, :, :, None] * key_totals[:, None]
    )
    values_wide = self_values.astype(WIDE)
    keys_wide = self_keys.astype(WIDE)
    grad_k_pair = (
        jnp.einsum("tze,izde->itzd", values_wide, grad_kernels, precision=PRECISE)
        + grad_totals[:, None]
    )
    grad_v_pair = jnp.einsum("tzd,izde->itze", keys_wide, grad_kernels, precision=PRECISE)
    grad_q_self = jax.nn.sigmoid(projected[:, 0]) * by_image(second, grad_q_pair)
    grad_k_self = jax.nn.sigmoid(projected[:, 1]) * by_image(second, grad_k_pair)
    grad_v_self = by_image(second, grad_v_pair)
    grad_projected = (
        jnp.stack([grad_q_self, grad_k_self, grad_v_self], axis=1)
        .reshape(tokens_here, 3 * self_cols)
        .astype(LOW)
    )
    grad_normed = scatter_product(grad_projected, qkv_flat)
    qkv_part = over_tokens(normed_low, grad_projected)
    normed_unused, norm_back = jax.vjp(modulated_norm, block_inputs, per_block(0), per_block(1))
    grad_inputs_norm, grad_shift_attn, grad_scale_attn = norm_back(grad_normed)
    input_grad = gather_blocks((grad_after_attn + grad_inputs_norm).astype(LOW)).astype(WIDE)
    output = gather_blocks(output_block)

    early_sums = jnp.stack(
        [
            image_sums(member)
            for member in (
                grad_gate_attn,
                grad_shift_ffn,
                grad_scale_ffn,
                block_upstream * ffn_branch,
            )
        ],
        axis=1,
    )
    late_sums = jnp.stack(
        [image_sums(member) for member in (grad_shift_attn, grad_scale_attn)], axis=1
    )

    def image_total(pair_sums):
        own = jnp.where(first_half, pair_sums[0], pair_sums[1])
        other = jnp.where(first_half, pair_sums[1], pair_sums[0])
        return same_everywhere(own + swapped(other, "seq", 0))

    modulation_grad = jnp.concatenate([image_total(late_sums), image_total(early_sums)], axis=0)

    grad_kv = (
        jnp.stack([grad_keys, grad_values])
        .reshape(2, tp_count, cross_heads, 2, context, CROSS_HEAD)
        .transpose(3, 1, 4, 0, 2, 5)
        .reshape(2, tp_count, context, 2 * cross_cols)
    )
    grad_kv_keep = jnp.where(first_half, grad_kv[0], grad_kv[1])
    grad_kv_send = jnp.where(first_half, grad_kv[1], grad_kv[0]).astype(LOW)
    grad_kv_image = grad_kv_keep + swapped(grad_kv_send, "seq", 0).astype(WIDE)
    grad_kv_own = grad_kv_image[0] + sum(
        from_ahead(grad_kv_image[step].astype(LOW), step).astype(WIDE)
        for step in range(1, tp_count)
    )
    ckv_part = over_tokens(text_rows, grad_kv_own.astype(LOW))

    def own_columns(rows):
        total = rows[:, 0]
        for step in range(1, tp_count):
            total = total + from_ahead(rows[:, step].astype(LOW), step).astype(WIDE)
        return total

    def sum_square(parts):
        rows = sum_rows(jnp.concatenate(parts, axis=1))
        return own_columns(rows.reshape(rows.shape[0], tp_count, -1))

    for place in range(lax.axis_size("seq").bit_length() - 1):
        conv_sum = conv_sum + swapped(conv_sum, "seq", place)
    down_grad = sum_rows(down_part)
    up_grad = sum_rows(up_part)
    cross_out_grad = sum_square(cross_out_part)
    cross_q_grad = sum_square(cross_q_part)
    ckv_grad = sum_rows(ckv_part)
    attn_out_grad = sum_square(attn_out_part)
    qkv_grad = sum_rows(qkv_part)
    return (
        output,
        input_grad,
        modulation_grad[None],
        qkv_grad.reshape(-1, 3, self_cols),
        attn_out_grad,
        cross_q_grad,
        ckv_grad.reshape(-1, 2, cross_cols),
        cross_out_grad,
        up_grad.reshape(-1, 2, ffn_cols),
        conv_sum.reshape(9, 2, ffn_cols),
        down_grad,
    )


def solution(mesh):
    placed = (
        P("seq", None),
        P("seq", None),
        P("seq", None, None),
        P("seq", None, None),
        P(),
        P(),
        P(None, None, "tp"),
        P(None, "tp"),
        P(None, "tp"),
        P(None, None, "tp"),
        P(None, "tp"),
        P(None, None, "tp"),
        P(None, None, "tp"),
        P(None, "tp"),
    )
    return jax.shard_map(
        shards,
        mesh=mesh,
        in_specs=placed,
        out_specs=(
            P("seq", None),
            P("seq", None),
            P("seq", None, None),
            P("seq", None, "tp"),
            P("seq", "tp"),
            P("seq", "tp"),
            P("seq", None, "tp"),
            P("seq", "tp"),
            P("seq", None, "tp"),
            P(None, None, "tp"),
            P("seq", "tp"),
        ),
        check_vma=False,
    )
```

```python
import functools
import math

import jax
import jax.numpy as jnp
from jax import lax
from jax.experimental import pallas as pl
from jax.experimental.pallas import tpu as pltpu
from jax.sharding import PartitionSpec as P

HEAD = 32
CROSS_HEAD = 72
MAXW = 32
LANES = 128
GRANT = 56 * 1024 * 1024

EPSILON = 1e-06
MASKED_OUT = -1e30
LOW = jnp.bfloat16
WIDE = jnp.float32

FIRST, CUT, SIDE, WIDTH, OWN_LENGTH, OTHER_LENGTH, BLOCK_FIRST, SEQ_TOKENS, TP_PLACE, ROW_PLACE = range(10)


def swapped(block, axis, apart):
    count = lax.axis_size(axis)
    route = [(low, low ^ (1 << apart)) for low in range(count)]
    return lax.ppermute(block, axis, route)


def from_behind(block, step):
    count = lax.axis_size("tp")
    return lax.ppermute(block, "tp", [(k, (k + step) % count) for k in range(count)])


def from_ahead(block, step):
    count = lax.axis_size("tp")
    return lax.ppermute(block, "tp", [(k, (k - step) % count) for k in range(count)])


def dot(left, right):
    return jnp.dot(left, right, preferred_element_type=WIDE)


def times_transposed(left, right):
    return lax.dot_general(left, right, (((1,), (1,)), ((), ())), preferred_element_type=WIDE)


def over_tokens(left, right):
    return lax.dot_general(left, right, (((0,), (0,)), ((), ())), preferred_element_type=WIDE)


def split(wide):
    high = wide.astype(LOW)
    return high, (wide - high.astype(WIDE)).astype(LOW)


def call(body, name, outs, arrays, *, grid=None, in_specs=None, out_specs=None, scratch=(), flops=0, table=None):
    shapes = tuple(jax.ShapeDtypeStruct(*out) for out in outs)
    size = sum(math.prod(a.shape) * a.dtype.itemsize for a in (*arrays, *shapes))
    whole = pl.BlockSpec(memory_space=pltpu.VMEM)
    return pl.pallas_call(
        body,
        out_shape=shapes,
        grid_spec=pltpu.PrefetchScalarGridSpec(
            num_scalar_prefetch=1,
            grid=grid or (1,),
            in_specs=in_specs or [whole] * len(arrays),
            out_specs=out_specs or [whole] * len(shapes),
            scratch_shapes=list(scratch),
        ),
        compiler_params=pltpu.CompilerParams(vmem_limit_bytes=GRANT),
        cost_estimate=pl.CostEstimate(flops=0, bytes_accessed=size // 100, transcendentals=0),
        name=name,
    )(table, *arrays)


def own_image(table, start, rows):
    place = start + lax.broadcasted_iota(jnp.int32, (rows, 1), 0)
    return (place >= table[CUT]).astype(jnp.int32) == table[SIDE]


def pick(own, own_rows, other_rows, row):
    return jnp.where(
        own, own_rows[row : row + 1, :].astype(WIDE), other_rows[row : row + 1, :].astype(WIDE)
    )


def inverse_size(wide):
    return lax.rsqrt(jnp.mean(wide * wide, axis=-1, keepdims=True) + EPSILON)


def both_sums(own, values):
    mine = jnp.sum(jnp.where(own, values, 0.0), axis=0, keepdims=True)
    return mine, jnp.sum(jnp.where(own, 0.0, values), axis=0, keepdims=True)


def same_head(rows, columns):
    row_head = lax.broadcasted_iota(jnp.int32, (rows, columns), 0) // HEAD
    return row_head == lax.broadcasted_iota(jnp.int32, (rows, columns), 1) // HEAD


def fold(square):
    size = square.shape[1]
    total = None
    for low in range(0, size, LANES):
        part = square[:, low : min(low + LANES, size)]
        if part.shape[1] < LANES:
            part = jnp.concatenate(
                [part, jnp.zeros((part.shape[0], LANES - part.shape[1]), part.dtype)], axis=1
            )
        total = part if total is None else total + part
    return total


def unfold(folded):
    size = folded.shape[0]
    parts = [folded[:, : min(LANES, size - low)] for low in range(0, size, LANES)]
    return jnp.where(same_head(size, size), jnp.concatenate(parts, axis=1), 0.0)


def packed(square, totals):
    keep = same_head(square.shape[0], square.shape[1])
    return fold(jnp.where(keep, square, 0.0)) + pltpu.roll(
        fold(jnp.where(keep, totals, 0.0)), HEAD, 1
    )


def unpacked(folded):
    return unfold(folded), unfold(pltpu.roll(folded, LANES - HEAD, 1))


def log_exp(wide):
    return jnp.maximum(wide, 0.0) + jnp.log1p(jnp.exp(-jnp.abs(wide)))


def logistic(wide):
    return 1.0 / (1.0 + jnp.exp(-wide))


def self_project_body(table, x, mod_own, mod_other, weight, normed, raw, q, k, v, own_out, other_out, squares, totals):
    step = pl.program_id(0)
    rows, columns = q.shape
    own = own_image(table, table[FIRST] + step * rows, rows)
    wide = x[...].astype(WIDE)
    low = (
        wide * inverse_size(wide) * (1.0 + pick(own, mod_own, mod_other, 1))
        + pick(own, mod_own, mod_other, 0)
    ).astype(LOW)
    normed[...] = low
    out = dot(low, weight[...])
    raw[...] = out[:, : 2 * columns]
    q[...] = log_exp(out[:, :columns]).astype(LOW)
    keys = log_exp(out[:, columns : 2 * columns]).astype(LOW)
    values = out[:, 2 * columns :].astype(LOW)
    k[...] = keys
    v[...] = values

    @pl.when(step == 0)
    def _():
        squares[...] = jnp.zeros_like(squares)
        totals[...] = jnp.zeros_like(totals)

    ones = jnp.ones((rows, columns), LOW)
    for image in range(2):
        zero = jnp.zeros_like(keys)
        masked = jnp.where(own, keys, zero) if image == 0 else jnp.where(own, zero, keys)
        squares[image] += over_tokens(masked, values)
        totals[image] += over_tokens(masked, ones)

    @pl.when(step == pl.num_programs(0) - 1)
    def _():
        own_out[...] = packed(squares[0], totals[0])
        other_out[...] = packed(squares[1], totals[1])


def self_project(table, x, mod_own, mod_other, weight, columns):
    tokens, width = x.shape
    rows = 128
    row = lambda c: pl.BlockSpec((rows, c), lambda i, t: (i, 0))
    fixed = lambda *s: pl.BlockSpec(s, lambda i, t: (0,) * len(s))
    return call(
        self_project_body,
        "self_project",
        [((tokens, width), LOW), ((tokens, 2 * columns), WIDE)]
        + [((tokens, columns), LOW)] * 3
        + [((columns, LANES), WIDE)] * 2,
        (x, mod_own, mod_other, weight),
        grid=(tokens // rows,),
        in_specs=[row(width), fixed(*mod_own.shape), fixed(*mod_own.shape), fixed(*weight.shape)],
        out_specs=[row(width), row(2 * columns)]
        + [row(columns)] * 3
        + [fixed(columns, LANES)] * 2,
        scratch=[pltpu.VMEM((2, columns, columns), WIDE)] * 2,
        flops=4 * tokens * width * 3 * columns,
        table=table,
    )


def keep_squares(kernels, key_totals, own_fold, other_fold):
    for image, folded in enumerate((own_fold, other_fold)):
        square, total = unpacked(folded[...])
        kernels[image, 0], kernels[image, 1] = split(square)
        key_totals[image, 0], key_totals[image, 1] = split(total)


def self_attend_body(table, q, own_fold, other_fold, attended, wide_out, denominator, kernels, key_totals):
    step = pl.program_id(0)
    rows = q.shape[0]

    @pl.when(step == 0)
    def _():
        keep_squares(kernels, key_totals, own_fold, other_fold)

    own = own_image(table, table[FIRST] + step * rows, rows)
    queries = q[...]

    def both(pair):
        own_part = dot(queries, pair[0, 0]) + dot(queries, pair[0, 1])
        return jnp.where(own, own_part, dot(queries, pair[1, 0]) + dot(queries, pair[1, 1]))

    under = both(key_totals) + 1.0
    out = both(kernels) / under
    attended[...] = out.astype(LOW)
    wide_out[...] = out
    denominator[...] = under


def self_attend(table, q, own_fold, other_fold):
    tokens, columns = q.shape
    rows = 128
    row = pl.BlockSpec((rows, columns), lambda i, t: (i, 0))
    fixed = pl.BlockSpec((columns, LANES), lambda i, t: (0, 0))
    return call(
        self_attend_body,
        "self_attend",
        [((tokens, columns), LOW), ((tokens, columns), WIDE), ((tokens, columns), WIDE)],
        (q, own_fold, other_fold),
        grid=(tokens // rows,),
        in_specs=[row, fixed, fixed],
        out_specs=[row, row, row],
        scratch=[pltpu.VMEM((2, 2, columns, columns), LOW)] * 2,
        flops=16 * tokens * columns * columns,
        table=table,
    )


def self_back_body(table, grad, q, wide_out, denominator, own_fold, other_fold, grad_q, own_out, other_out, kernels, key_totals, squares, totals):
    step = pl.program_id(0)
    rows, columns = q.shape

    @pl.when(step == 0)
    def _():
        keep_squares(kernels, key_totals, own_fold, other_fold)
        squares[...] = jnp.zeros_like(squares)
        totals[...] = jnp.zeros_like(totals)

    place = lax.rem(table[TP_PLACE] + step, pl.num_programs(0))
    own = own_image(table, table[FIRST] + place * rows, rows)
    wide = grad[0].astype(WIDE)
    over = 1.0 / denominator[...]
    numer_high, numer_low = split(wide * over)
    ones = jnp.where(same_head(columns, columns), 1.0, 0.0).astype(LOW)
    high, low = split(wide * wide_out[...])
    denom = -(dot(high, ones) + dot(low, ones)) * over
    denom_high, denom_low = split(denom)

    def back(image):
        square, total = kernels[image, 0], key_totals[image, 0]
        through = (
            times_transposed(numer_high, square)
            + times_transposed(numer_low, square)
            + times_transposed(numer_high, kernels[image, 1])
        )
        totals_part = (
            times_transposed(denom_high, total)
            + times_transposed(denom_low, total)
            + times_transposed(denom_high, key_totals[image, 1])
        )
        return through + totals_part * (1.0 / HEAD)

    grad_q[...] = jnp.where(own, back(0), back(1))
    queries = q[...]
    zero = jnp.zeros_like(queries)
    for image in range(2):
        masked = jnp.where(own, queries, zero) if image == 0 else jnp.where(own, zero, queries)
        squares[image] += over_tokens(masked, numer_high) + over_tokens(masked, numer_low)
        totals[image] += over_tokens(masked, denom_high) + over_tokens(masked, denom_low)

    @pl.when(step == pl.num_programs(0) - 1)
    def _():
        own_out[...] = packed(squares[0], totals[0])
        other_out[...] = packed(squares[1], totals[1])


def self_back(table, grad, q, wide_out, denominator, own_fold, other_fold):
    count, rows, columns = grad.shape
    tokens = q.shape[0]
    turn = lambda i, t: (lax.rem(t[TP_PLACE] + i, count), 0)
    row = pl.BlockSpec((rows, columns), turn)
    fixed = pl.BlockSpec((columns, LANES), lambda i, t: (0, 0))
    return call(
        self_back_body,
        "self_back",
        [((tokens, columns), WIDE)] + [((columns, LANES), WIDE)] * 2,
        (grad, q, wide_out, denominator, own_fold, other_fold),
        grid=(count,),
        in_specs=[pl.BlockSpec((1, rows, columns), lambda i, t: (i, 0, 0)), row, row, row, fixed, fixed],
        out_specs=[row, fixed, fixed],
        scratch=[pltpu.VMEM((2, 2, columns, columns), LOW)] * 2
        + [pltpu.VMEM((2, columns, columns), WIDE)] * 2,
        flops=48 * tokens * columns * columns,
        table=table,
    )


def self_project_back_body(table, grad_q, k, v, raw, own_fold, other_fold, grad_out, kernels, key_totals):
    step = pl.program_id(0)
    rows, columns = k.shape

    @pl.when(step == 0)
    def _():
        keep_squares(kernels, key_totals, own_fold, other_fold)

    own = own_image(table, table[FIRST] + step * rows, rows)
    keys, values = k[...], v[...]
    ones = jnp.ones((16, columns), LOW)

    def grad_k(image):
        total = times_transposed(ones, key_totals[image, 0]) + times_transposed(
            ones, key_totals[image, 1]
        )
        return (
            times_transposed(values, kernels[image, 0])
            + times_transposed(values, kernels[image, 1])
            + total[:1] * (1.0 / HEAD)
        )

    def grad_v(image):
        return dot(keys, kernels[image, 0]) + dot(keys, kernels[image, 1])

    given = raw[...]
    q_part = grad_q[...] * logistic(given[:, :columns])
    k_part = jnp.where(own, grad_k(0), grad_k(1)) * logistic(given[:, columns:])
    v_part = jnp.where(own, grad_v(0), grad_v(1))
    grad_out[...] = jnp.concatenate([q_part, k_part, v_part], axis=1).astype(LOW)


def self_project_back(table, grad_q, k, v, raw, own_fold, other_fold):
    tokens, columns = k.shape
    rows = 128
    row = lambda c: pl.BlockSpec((rows, c), lambda i, t: (i, 0))
    fixed = pl.BlockSpec((columns, LANES), lambda i, t: (0, 0))
    return call(
        self_project_back_body,
        "self_project_back",
        [((tokens, 3 * columns), LOW)],
        (grad_q, k, v, raw, own_fold, other_fold),
        grid=(tokens // rows,),
        in_specs=[row(columns), row(columns), row(columns), row(2 * columns), fixed, fixed],
        out_specs=[row(3 * columns)],
        scratch=[pltpu.VMEM((2, 2, columns, columns), LOW)] * 2,
        flops=16 * tokens * columns * columns,
        table=table,
    )[0]


def live_keys(table, own, keys):
    place = lax.broadcasted_iota(jnp.int32, (1, keys), 1)
    return place < jnp.where(own, table[OWN_LENGTH], table[OTHER_LENGTH])


def shard_of(first, rest, step, offset=0):
    return first[...] if step == 0 else rest[offset + step - 1]


def middle_body(table, att, x, mod_own, mod_other, out_first, query_first, cross_first, rest, kv_own, kv_other, branch, after_low, queries_out, probs_out, text_out, after_cross, normed):
    count, rows, columns = att.shape
    keys = kv_own.shape[1]
    heads = columns // CROSS_HEAD
    own = own_image(table, table[BLOCK_FIRST], rows)
    y1 = jnp.zeros((rows, x.shape[1]), WIDE)
    for step in range(count):
        y1 += times_transposed(att[step], shard_of(out_first, rest, step))
    branch[...] = y1
    x1 = x[...].astype(WIDE) + pick(own, mod_own, mod_other, 2) * y1
    x1_low = x1.astype(LOW)
    after_low[...] = x1_low
    live = live_keys(table, own, keys)
    yc = jnp.zeros_like(x1)
    for step in range(count):
        queries = dot(x1_low, shard_of(query_first, rest, step, count - 1)).astype(LOW)
        queries_out[step] = queries
        mine, theirs = kv_own[step], kv_other[step]
        parts = []
        for head in range(heads):
            lanes = slice(head * CROSS_HEAD, (head + 1) * CROSS_HEAD)
            wide_lanes = slice(columns + head * CROSS_HEAD, columns + (head + 1) * CROSS_HEAD)
            q = queries[:, lanes]
            scores = jnp.where(
                own, times_transposed(q, mine[:, lanes]), times_transposed(q, theirs[:, lanes])
            ) * (1.0 / math.sqrt(CROSS_HEAD))
            scores = jnp.where(live, scores, MASKED_OUT)
            raised = jnp.exp(scores - jnp.max(scores, axis=-1, keepdims=True))
            probs = raised / jnp.sum(raised, axis=-1, keepdims=True)
            probs_out[step * heads + head] = probs
            low = probs.astype(LOW)
            parts.append(
                jnp.where(own, dot(low, mine[:, wide_lanes]), dot(low, theirs[:, wide_lanes]))
            )
        text = jnp.concatenate(parts, axis=1).astype(LOW)
        text_out[step] = text
        yc += times_transposed(text, shard_of(cross_first, rest, step, 2 * count - 2))
    x2 = x1 + yc
    after_cross[...] = x2
    normed[...] = (
        x2 * inverse_size(x2) * (1.0 + pick(own, mod_own, mod_other, 4))
        + pick(own, mod_own, mod_other, 3)
    ).astype(LOW)


def middle_back_body(table, grad_rows, up_weight, grad_1, grad_2, grad_3, x2_in, upstream, branch, mod_own, mod_other, out_first, query_first, cross_first, rest, kv_own, kv_other, probs_in, queries_in, cross_grad, query_grad, attn_grad, attended_grad, after_grad, sums, kv_own_grad, kv_other_grad):
    count, rows, columns = queries_in.shape
    keys = kv_own.shape[1]
    heads = columns // CROSS_HEAD
    scale = 1.0 / math.sqrt(CROSS_HEAD)
    own = own_image(table, table[BLOCK_FIRST], rows)
    grad = (
        times_transposed(grad_rows[...], up_weight[...])
        + grad_1[...].astype(WIDE)
        + grad_2[...].astype(WIDE)
        + grad_3[...].astype(WIDE)
    )
    x2 = x2_in[...]
    inverse = inverse_size(x2)
    xh = x2 * inverse
    sums[0:1], sums[1:2] = both_sums(own, grad)
    sums[2:3], sums[3:4] = both_sums(own, grad * xh)
    e = grad * (1.0 + pick(own, mod_own, mod_other, 4))
    dx2 = upstream[...].astype(WIDE) + inverse * (
        e - xh * jnp.mean(e * xh, axis=-1, keepdims=True)
    )
    dyc = dx2.astype(LOW)
    cross_grad[...] = dyc
    dx1 = dx2
    for step in range(count):
        doc = dot(dyc, shard_of(cross_first, rest, step, 2 * count - 2)).astype(LOW)
        mine, theirs = kv_own[step], kv_other[step]
        queries = queries_in[step]
        query_parts = []
        key_parts = ([], [])
        value_parts = ([], [])
        for head in range(heads):
            lanes = slice(head * CROSS_HEAD, (head + 1) * CROSS_HEAD)
            wide_lanes = slice(columns + head * CROSS_HEAD, columns + (head + 1) * CROSS_HEAD)
            do, q = doc[:, lanes], queries[:, lanes]
            probs = probs_in[step * heads + head]
            dp = jnp.where(
                own,
                times_transposed(do, mine[:, wide_lanes]),
                times_transposed(do, theirs[:, wide_lanes]),
            )
            ds = (probs * (dp - jnp.sum(probs * dp, axis=-1, keepdims=True))).astype(LOW)
            low = probs.astype(LOW)
            zero = jnp.zeros_like(ds)
            query_parts.append(
                jnp.where(own, dot(ds, mine[:, lanes]), dot(ds, theirs[:, lanes])) * scale
            )
            for image in range(2):
                mask = (lambda a: jnp.where(own, a, zero)) if image == 0 else (
                    lambda a: jnp.where(own, zero, a)
                )
                key_parts[image].append(over_tokens(mask(ds), q) * scale)
                value_parts[image].append(over_tokens(mask(low), do))
        dqc = jnp.concatenate(query_parts, axis=1).astype(LOW)
        query_grad[step] = dqc
        kv_own_grad[step] = jnp.concatenate(key_parts[0] + value_parts[0], axis=1).astype(LOW)
        kv_other_grad[step] = jnp.concatenate(key_parts[1] + value_parts[1], axis=1).astype(LOW)
        dx1 = dx1 + times_transposed(dqc, shard_of(query_first, rest, step, count - 1))
    after_grad[...] = dx1
    sums[4:5], sums[5:6] = both_sums(own, dx1 * branch[...])
    sums[6:8] = jnp.zeros((2, sums.shape[1]), WIDE)
    dy1 = (dx1 * pick(own, mod_own, mod_other, 2)).astype(LOW)
    attn_grad[...] = dy1
    for step in range(count):
        attended_grad[step] = dot(dy1, shard_of(out_first, rest, step)).astype(LOW)


def first_norm_back_body(table, grad_rows, weight, grad_1, grad_2, grad_3, after_grad, x, mod_own, mod_other, input_grad, sums):
    rows = x.shape[0]
    own = own_image(table, table[BLOCK_FIRST], rows)
    grad = (
        times_transposed(grad_rows[...], weight[...])
        + grad_1[...].astype(WIDE)
        + grad_2[...].astype(WIDE)
        + grad_3[...].astype(WIDE)
    )
    wide = x[...].astype(WIDE)
    inverse = inverse_size(wide)
    xh = wide * inverse
    sums[0:1], sums[1:2] = both_sums(own, grad)
    sums[2:3], sums[3:4] = both_sums(own, grad * xh)
    sums[4:8] = jnp.zeros((4, sums.shape[1]), WIDE)
    e = grad * (1.0 + pick(own, mod_own, mod_other, 1))
    input_grad[...] = (
        after_grad[...] + inverse * (e - xh * jnp.mean(e * xh, axis=-1, keepdims=True))
    ).astype(LOW)


def output_body(table, hidden_rows, weight, branch_1, branch_2, branch_3, x2, upstream, mod_own, mod_other, output, sums):
    rows = x2.shape[0]
    own = own_image(table, table[BLOCK_FIRST], rows)
    branch = (
        times_transposed(hidden_rows[...], weight[...])
        + branch_1[...].astype(WIDE)
        + branch_2[...].astype(WIDE)
        + branch_3[...].astype(WIDE)
    )
    sums[0:1], sums[1:2] = both_sums(own, upstream[...].astype(WIDE) * branch)
    sums[2:8] = jnp.zeros((6, sums.shape[1]), WIDE)
    output[...] = (x2[...] + pick(own, mod_own, mod_other, 5) * branch).astype(LOW)


def up_body(table, x, weight, wide_out, low_out, ordered):
    block = x[0]
    up = dot(block, weight[...])
    ordered[...] = block
    wide_out[...] = up
    low_out[...] = (up * logistic(up)).astype(LOW)


def up_project(table, blocks, weight):
    count, rows, width = blocks.shape
    columns = weight.shape[1]
    turn = lambda i, t: (lax.rem(t[TP_PLACE] + count - i, count), 0)
    return call(
        up_body,
        "up_project",
        [((count * rows, columns), WIDE), ((count * rows, columns), LOW), ((count * rows, width), LOW)],
        (blocks, weight),
        grid=(count,),
        in_specs=[
            pl.BlockSpec((1, rows, width), lambda i, t: (i, 0, 0)),
            pl.BlockSpec(weight.shape, lambda i, t: (0, 0)),
        ],
        out_specs=[pl.BlockSpec((rows, columns), turn)] * 2 + [pl.BlockSpec((rows, width), turn)],
        flops=2 * count * rows * width * columns,
        table=table,
    )


def fill(padded, block, rim):
    tokens = block.shape[0]
    edge = rim[...].astype(WIDE)
    padded[0:MAXW, :] = edge
    padded[MAXW : MAXW + tokens, :] = block.astype(WIDE)
    padded[MAXW + tokens : 2 * MAXW + tokens, :] = edge


def fill_masks(table, masks):
    tokens = masks.shape[1]
    place = table[FIRST] + lax.broadcasted_iota(jnp.int32, (tokens, LANES), 0)
    width = table[WIDTH]
    cut = table[CUT]
    late = place >= cut
    start = jnp.where(late, cut, 0)
    end = jnp.where(late, table[SEQ_TOKENS], cut)
    column = lax.bitwise_and(place, width - 1)
    one, none = jnp.ones((tokens, LANES), WIDE), jnp.zeros((tokens, LANES), WIDE)
    masks[0] = jnp.where(place - width >= start, one, none)
    masks[1] = jnp.where(place + width < end, one, none)
    masks[2] = jnp.where(column > 0, one, none)
    masks[3] = jnp.where(column < width - 1, one, none)


CHUNK = 64


def three_rows(table, padded, masks, low):
    width = table[WIDTH]
    above = padded[pl.ds(pl.multiple_of(MAXW + low - width, 16), CHUNK), :]
    below = padded[pl.ds(pl.multiple_of(MAXW + low + width, 16), CHUNK), :]
    own = padded[pl.ds(pl.multiple_of(MAXW + low, 16), CHUNK), :]
    rows = pl.ds(pl.multiple_of(low, 16), CHUNK)
    return above * masks[0, rows, :], own, below * masks[1, rows, :]


def nine_taps(rows, taps, left_mask, right_mask):
    mixed = [sum(rows[a] * taps[a][b] for a in range(3)) for b in range(3)]
    return (
        mixed[1]
        + left_mask * pltpu.roll(mixed[0], 1, 0)
        + right_mask * pltpu.roll(mixed[2], CHUNK - 1, 0)
    )


def taps_of(taps, flip):
    read = lambda a, b: taps[3 * a + b : 3 * a + b + 1, :]
    return [[read(2 - a, 2 - b) if flip else read(a, b) for b in range(3)] for a in range(3)]


def mix_body(table, value, gate, value_rim, gate_rim, value_taps, gate_taps, grad_hidden, hidden, grads, value_pad, gate_pad, masks):
    @pl.when(pl.program_id(0) == 0)
    def _():
        fill_masks(table, masks)

    fill(value_pad, value[...], value_rim)
    fill(gate_pad, gate[...], gate_rim)
    value_weights, gate_weights = taps_of(value_taps, False), taps_of(gate_taps, False)

    @pl.loop(0, value.shape[0] // CHUNK)
    def _(index):
        low = index * CHUNK
        rows = pl.ds(pl.multiple_of(low, CHUNK), CHUNK)
        left, right = masks[2, rows, :], masks[3, rows, :]
        mv = nine_taps(three_rows(table, value_pad, masks, low), value_weights, left, right)
        mg = nine_taps(three_rows(table, gate_pad, masks, low), gate_weights, left, right)
        sigma = logistic(mg)
        gated = mg * sigma
        hidden[rows, :] = (mv * gated).astype(LOW)
        dh = grad_hidden[rows, :]
        grads[0, rows, :] = (dh * gated).astype(LOW)
        grads[1, rows, :] = (dh * mv * (sigma * (1.0 + mg * (1.0 - sigma)))).astype(LOW)


def mix(table, activated, rim, taps, grad_hidden):
    tokens, wide = activated.shape
    columns = wide // 2
    tiles = columns // LANES
    block = lambda r, shift: pl.BlockSpec((r, LANES), lambda i, t: (0, i + shift))
    pad = pltpu.VMEM((tokens + 2 * MAXW, LANES), WIDE)
    return call(
        mix_body,
        "mix",
        [((tokens, columns), LOW), ((2, tokens, columns), LOW)],
        (activated, activated, rim, rim, taps, taps, grad_hidden),
        grid=(tiles,),
        in_specs=[
            block(tokens, 0),
            block(tokens, tiles),
            block(MAXW, 0),
            block(MAXW, tiles),
            block(taps.shape[0], 0),
            block(taps.shape[0], tiles),
            block(tokens, 0),
        ],
        out_specs=[
            block(tokens, 0),
            pl.BlockSpec((2, tokens, LANES), lambda i, t: (0, 0, i)),
        ],
        scratch=[pad, pad, pltpu.VMEM((4, tokens, LANES), WIDE)],
        flops=6000 * tokens * columns // 2,
        table=table,
    )


def mix_back_body(table, grads, grads_rim, activated, rim, taps, up, grad_up, tap_grads, grad_pad, act_pad, masks):
    @pl.when(pl.program_id(0) == 0)
    def _():
        fill_masks(table, masks)

    fill(grad_pad, grads[0], grads_rim.at[0])
    fill(act_pad, activated[...], rim)
    weights = taps_of(taps, True)

    def step(index, sums):
        low = index * CHUNK
        rows = pl.ds(pl.multiple_of(low, CHUNK), CHUNK)
        left, right = masks[2, rows, :], masks[3, rows, :]
        mine = three_rows(table, grad_pad, masks, low)
        dact = nine_taps(mine, weights, left, right)
        given = up[rows, :]
        sigma = logistic(given)
        grad_up[rows, :] = (dact * (sigma * (1.0 + given * (1.0 - sigma)))).astype(LOW)
        acts = three_rows(table, act_pad, masks, low)
        turned = (
            right * pltpu.roll(mine[1], CHUNK - 1, 0),
            mine[1],
            left * pltpu.roll(mine[1], 1, 0),
        )
        return tuple(
            sums[3 * a + b]
            + jnp.sum((acts[a] * turned[b]).reshape(CHUNK // 8, 8, LANES), axis=0)
            for a in range(3)
            for b in range(3)
        )

    zero = jnp.zeros((8, LANES), WIDE)
    sums = lax.fori_loop(0, activated.shape[0] // CHUNK, step, (zero,) * 9)
    for tap in range(9):
        tap_grads[tap : tap + 1, :] = jnp.sum(sums[tap], axis=0, keepdims=True)
    tap_grads[9:16, :] = jnp.zeros((7, LANES), WIDE)


def mix_back(table, grads, grads_rim, activated, rim, taps, up):
    tokens, wide = activated.shape
    columns = wide // 2
    tiles = columns // LANES
    block = lambda r: pl.BlockSpec((r, LANES), lambda i, t: (0, i))
    half = lambda r: pl.BlockSpec(
        (1, r, LANES), lambda i, t: (lax.div(i, tiles), 0, lax.rem(i, tiles))
    )
    pad = pltpu.VMEM((tokens + 2 * MAXW, LANES), WIDE)
    return call(
        mix_back_body,
        "mix_back",
        [((tokens, wide), LOW), ((16, wide), WIDE)],
        (grads, grads_rim, activated, rim, taps, up),
        grid=(2 * tiles,),
        in_specs=[half(tokens), half(MAXW), block(tokens), block(MAXW), block(taps.shape[0]), block(tokens)],
        out_specs=[block(tokens), block(16)],
        scratch=[pad, pad, pltpu.VMEM((4, tokens, LANES), WIDE)],
        flops=6000 * tokens * columns,
        table=table,
    )


def eighths_body(table, *refs):
    for place, ref in enumerate(refs[:-1]):
        refs[-1][place] = ref[...]


def order_body(table, *refs):
    pieces, out = refs[:-1], refs[-1]
    units, rows = pieces[0].shape[0], pieces[0].shape[1]
    weights = 3
    for place, piece in enumerate(pieces):
        block = lax.bitwise_xor(table[ROW_PLACE], place)
        for unit in range(units):
            target = (unit % weights) * (units // weights) + unit // weights
            out[target, pl.ds(pl.multiple_of(block * rows, 16), rows), :] = piece[unit]


def after(value, *others):
    return lax.optimization_barrier((value, others))[0]


def fetch_eighths(weights):
    rows, columns = weights[0].shape
    own = rows // 8
    eighth = call(
        eighths_body,
        "eighths",
        [((len(weights), own, columns), weights[0].dtype)],
        weights,
        in_specs=[pl.BlockSpec((own, columns), lambda i, t: (t[0], 0))] * len(weights),
        out_specs=[pl.BlockSpec((len(weights), own, columns), lambda i, t: (0, 0, 0))],
        table=(lax.axis_index("seq") % 8).reshape(1).astype(jnp.int32),
    )[0]
    return [from_behind(eighth, step) for step in range(1, lax.axis_size("tp"))]


def share_eighths(table, fetched, ready):
    count = lax.axis_size("seq")
    far = lambda flip: lax.ppermute(fetched, "seq", [(k, k ^ flip) for k in range(count)])
    even = [fetched] + after([far(2), far(4), far(6)], *ready)
    pieces = []
    for piece in even:
        pieces += [piece, swapped(piece, "seq", 0)]
    units, rows, columns = fetched.shape
    return call(
        order_body, "order", [((units, 8 * rows, columns), fetched.dtype)], pieces, table=table
    )[0]


def token_block(values, place):
    count = lax.axis_size("tp")
    size = values.shape[0] // count
    return lax.dynamic_slice_in_dim(values, (place % count) * size, size, 0)


def placed_blocks(blocks):
    count = len(blocks)
    place = lax.axis_index("tp")
    result = jnp.zeros((count,) + blocks[0].shape, blocks[0].dtype)
    for step in range(count):
        result = lax.dynamic_update_index_in_dim(result, blocks[step], (place - step) % count, 0)
    return result.reshape((count * blocks[0].shape[0],) + blocks[0].shape[1:])


def all_blocks(block):
    return [block] + [from_behind(block, step) for step in range(1, lax.axis_size("tp"))]


def products_body(table, left, right, *outs):
    count = len(outs) + 1
    rows = left.shape[0] // count
    for step, out in enumerate(outs):
        low = lax.rem(table[TP_PLACE] + step + 1, count) * rows
        block = left[pl.ds(pl.multiple_of(low, 16), rows), :]
        out[...] = times_transposed(block, right[...]).astype(LOW)


def products_to_send(table, left, right):
    count = lax.axis_size("tp")
    shape = (left.shape[0] // count, right.shape[0])
    return list(
        call(products_body, "products", [(shape, LOW)] * (count - 1), (left, right), table=table)
    )


def own_rows(left):
    count = lax.axis_size("tp")
    return pl.BlockSpec((left.shape[0] // count, left.shape[1]), lambda i, t: (t[TP_PLACE], 0))


def sent_ahead(products):
    return [from_behind(product, step + 1) for step, product in enumerate(products)]


def same_everywhere(block):
    pair = block + swapped(block, "tp", 0)
    return pair + swapped(pair, "tp", 1)


def sum_rows(grad):
    return lax.optimization_barrier(
        lax.psum_scatter(grad.astype(LOW), "seq", scatter_dimension=0, tiled=True)
    )


def square_body(table, dyc, text, x1, dqc, dy1, att, out):
    parts = [
        over_tokens(left[...], right[0]) for left, right in ((dyc, text), (x1, dqc), (dy1, att))
    ]
    rest = out.shape[1] - sum(part.shape[1] for part in parts)
    if rest:
        parts.append(jnp.zeros((out.shape[0], rest), WIDE))
    out[...] = jnp.concatenate(parts, axis=1).astype(LOW)


def square_parts(table, lefts, rights):
    rows, width = lefts[0].shape
    count, _, columns = rights[0].shape
    block = -(-3 * columns // LANES) * LANES
    whole = pl.BlockSpec((rows, width), lambda i, t: (0, 0))
    one = pl.BlockSpec((1, rows, columns), lambda i, t: (i, 0, 0))
    return call(
        square_body,
        "square_parts",
        [((width, count * block), LOW)],
        [array for pair in zip(lefts, rights) for array in pair],
        grid=(count,),
        in_specs=[whole, one] * 3,
        out_specs=[pl.BlockSpec((width, block), lambda i, t: (0, i))],
        flops=8 * rows * width * count * block,
        table=table,
    )[0]


def ffn_body(table, grad_ffn, hidden, normed, grad_up, out):
    step = pl.program_id(0)

    @pl.when(step == 0)
    def _():
        out[...] = over_tokens(grad_ffn[...], hidden[...]).astype(LOW)

    @pl.when(step > 0)
    def _():
        out[...] = over_tokens(normed[...], grad_up[...]).astype(LOW)


def ffn_parts_of(table, grad_ffn, hidden, normed, grad_up):
    tokens, width = normed.shape
    columns = hidden.shape[1]
    whole = pl.BlockSpec((tokens, width), lambda i, t: (0, 0))
    return call(
        ffn_body,
        "ffn_parts",
        [((width, 3 * columns), LOW)],
        (grad_ffn, hidden, normed, grad_up),
        grid=(3,),
        in_specs=[
            whole,
            pl.BlockSpec((tokens, columns), lambda i, t: (0, 0)),
            whole,
            pl.BlockSpec((tokens, columns), lambda i, t: (0, jnp.maximum(i - 1, 0))),
        ],
        out_specs=[pl.BlockSpec((width, columns), lambda i, t: (0, i))],
        table=table,
    )[0]


def late_body(table, normed, grad_projected, text, kv_grad, out):
    first = over_tokens(normed[...], grad_projected[...]).astype(LOW)
    second = over_tokens(text[...], kv_grad[...]).astype(LOW)
    out[...] = jnp.concatenate([first, second], axis=1)


def shards(
    hidden_in,
    cotangent,
    modulation,
    text_states,
    image_shapes,
    text_lengths,
    qkv_weight,
    attn_out_weight,
    cross_q_weight,
    cross_kv_weight,
    cross_out_weight,
    up_weight,
    conv_weight,
    down_weight,
):
    tokens_here, width = hidden_in.shape
    context = text_states.shape[1]
    keys = -(-context // 16) * 16
    self_cols = qkv_weight.shape[2]
    cross_cols = cross_q_weight.shape[1]
    ffn_cols = up_weight.shape[2]
    ffn_pad = -(-ffn_cols // LANES) * LANES
    count = lax.axis_size("tp")
    tp_index = lax.axis_index("tp")
    block_size = tokens_here // count
    seq_index = lax.axis_index("seq")
    side = seq_index % 2
    first_half = side == 0
    pair = seq_index - side
    pair_shapes = lax.dynamic_slice_in_dim(image_shapes, pair, 2, 0)
    row_width = pair_shapes[0, 1]
    lengths = lax.dynamic_slice_in_dim(text_lengths, pair, 2, 0)
    first_place = side * tokens_here
    table = jnp.stack(
        [
            first_place,
            pair_shapes[0, 0] * row_width,
            side,
            row_width,
            jnp.where(first_half, lengths[0], lengths[1]),
            jnp.where(first_half, lengths[1], lengths[0]),
            first_place + tp_index * block_size,
            jnp.int32(2 * tokens_here),
            tp_index,
            seq_index % 8,
        ]
    ).astype(jnp.int32)

    mod_own = modulation[0]
    mod_other = swapped(mod_own, "seq", 0).astype(WIDE)
    mod_own = mod_own.astype(WIDE)
    fetched = jnp.concatenate(fetch_eighths([attn_out_weight, cross_q_weight, cross_out_weight]))
    qkv_flat = qkv_weight.reshape(width, 3 * self_cols)
    normed_low, raw, q, k, v, part_own, part_other = self_project(
        table, hidden_in, mod_own, mod_other, qkv_flat, self_cols
    )
    theirs = swapped(jnp.stack([part_own, part_other]), "seq", 0)
    fetched = after(fetched, q)
    text_rows = jnp.pad(text_states[0], ((0, keys - context), (0, 0)))
    kv_here = dot(
        after(text_rows, fetched), cross_kv_weight.reshape(width, 2 * cross_cols)
    ).astype(LOW)
    kernel_own, kernel_other = part_own + theirs[1], part_other + theirs[0]
    attended, attended_wide, denominator = self_attend(
        table, after(q, kv_here), kernel_own, kernel_other
    )

    x_block = token_block(hidden_in, tp_index)
    up_block = token_block(cotangent, tp_index)
    up_flat = jnp.pad(after(up_weight, attended), ((0, 0), (0, 0), (0, ffn_pad - ffn_cols))).reshape(
        width, 2 * ffn_pad
    )
    down_flat = jnp.pad(after(down_weight, attended), ((0, 0), (0, ffn_pad - ffn_cols)))
    taps = (
        jnp.pad(conv_weight, ((0, 7), (0, 0), (0, ffn_pad - ffn_cols)))
        .reshape(16, 2 * ffn_pad)
        .astype(WIDE)
    )
    gate_rows = jnp.where(
        (first_place + jnp.arange(tokens_here, dtype=jnp.int32) >= table[CUT])[:, None] == (side == 1),
        mod_own[5:6],
        mod_other[5:6],
    )
    grad_ffn = (cotangent.astype(WIDE) * gate_rows).astype(LOW)
    grad_hidden = dot(grad_ffn, down_flat)
    ready = (up_flat, taps, grad_hidden)
    kv_own = jnp.stack(after(all_blocks(kv_here), *ready))
    kv_other = swapped(kv_own, "seq", 0)
    rest = share_eighths(table, fetched, ready)
    attended_blocks = jnp.stack(
        [token_block(attended, tp_index)]
        + [from_behind(token_block(attended, tp_index + step), step) for step in range(1, count)]
    )
    all_heads = count * cross_cols // CROSS_HEAD
    weights = (attn_out_weight, cross_q_weight, cross_out_weight, rest)
    branch, after_low, queries, probs, text_low, after_cross, normed_two = call(
        middle_body,
        "middle",
        [
            ((block_size, width), WIDE),
            ((block_size, width), LOW),
            ((count, block_size, cross_cols), LOW),
            ((all_heads, block_size, keys), WIDE),
            ((count, block_size, cross_cols), LOW),
            ((block_size, width), WIDE),
            ((block_size, width), LOW),
        ],
        (attended_blocks, x_block, mod_own, mod_other, *weights, kv_own, kv_other),
        flops=60 * block_size * width * width,
        table=table,
    )

    blocks_two = jnp.stack(all_blocks(normed_two))
    up_wide, activated, normed_two_low = up_project(table, blocks_two, up_flat)
    rim = swapped(jnp.where(first_half, activated[-MAXW:], activated[:MAXW]), "seq", 0)
    hidden, grads = mix(table, activated, rim, taps, grad_hidden)
    grads_rim = swapped(jnp.where(first_half, grads[:, -MAXW:], grads[:, :MAXW]), "seq", 0)
    whole = pl.BlockSpec(memory_space=pltpu.VMEM)
    branch_sent = products_to_send(table, hidden, down_flat)
    grad_up, tap_part = mix_back(
        table, grads, grads_rim, activated, rim, taps, after(up_wide, branch_sent)
    )
    branch_parts = sent_ahead(branch_sent)
    norm_two_sent = products_to_send(table, grad_up, up_flat)
    grad_norm_two = sent_ahead(after(norm_two_sent, branch_parts))
    ffn_parts = ffn_parts_of(
        table, grad_ffn, after(hidden, norm_two_sent), normed_two_low, grad_up
    )
    ffn_rows = sum_rows(after(ffn_parts, grad_norm_two))
    output_block, output_sums = call(
        output_body,
        "output",
        [((block_size, width), LOW), ((8, width), WIDE)],
        (
            hidden,
            down_flat,
            *branch_parts,
            after_cross,
            up_block,
            mod_own,
            mod_other,
        ),
        in_specs=[own_rows(hidden)] + [whole] * 8,
        table=table,
    )
    output_blocks = all_blocks(output_block)

    (
        cross_grad,
        query_grad,
        attn_grad,
        attended_grad,
        after_grad,
        middle_sums,
        kv_own_grad,
        kv_other_grad,
    ) = call(
        middle_back_body,
        "middle_back",
        [
            ((block_size, width), LOW),
            ((count, block_size, cross_cols), LOW),
            ((block_size, width), LOW),
            ((count, block_size, self_cols), LOW),
            ((block_size, width), WIDE),
            ((8, width), WIDE),
            ((count, keys, 2 * cross_cols), LOW),
            ((count, keys, 2 * cross_cols), LOW),
        ],
        (
            after(grad_up, ffn_parts, output_block),
            up_flat,
            *grad_norm_two,
            after_cross,
            up_block,
            branch,
            mod_own,
            mod_other,
            *weights,
            kv_own,
            kv_other,
            probs,
            queries,
        ),
        in_specs=[own_rows(grad_up)] + [whole] * 17,
        flops=120 * block_size * width * width,
        table=table,
    )

    grad_blocks = jnp.stack(
        [attended_grad[0]] + [from_ahead(attended_grad[step], step) for step in range(1, count)]
    )
    squares = square_parts(
        table,
        (cross_grad, after_low, attn_grad),
        (text_low, query_grad, after(attended_blocks, attended_grad, output_blocks)),
    )
    square_rows = sum_rows(after(squares, grad_blocks))
    kv_total = kv_own_grad.astype(WIDE) + swapped(kv_other_grad, "seq", 0).astype(WIDE)
    kv_sent = [kv_total[step].astype(LOW) for step in range(1, count)]
    grad_blocks = after(grad_blocks, squares, kv_sent, ffn_rows)
    grad_q, back_own, back_other = self_back(
        table, grad_blocks, q, attended_wide, denominator, kernel_own, kernel_other
    )
    back_theirs = swapped(jnp.stack([back_own, back_other]), "seq", 0)
    kv_grad = kv_total[0]
    for step in range(1, count):
        kv_grad = kv_grad + from_ahead(kv_sent[step - 1], step).astype(WIDE)
    kv_grad = kv_grad.astype(LOW)
    grad_projected = self_project_back(
        table,
        grad_q,
        k,
        v,
        raw,
        back_own + back_theirs[1],
        back_other + back_theirs[0],
    )
    normed_sent = products_to_send(table, grad_projected, qkv_flat)
    grad_normed = sent_ahead(normed_sent)
    grad_projected = after(grad_projected, normed_sent)
    late_parts = call(
        late_body,
        "late_parts",
        [((width, 3 * self_cols + 2 * cross_cols), LOW)],
        (normed_low, grad_projected, text_rows, kv_grad),
        flops=4 * tokens_here * width * 5 * self_cols,
        table=table,
    )[0]
    late_rows = sum_rows(after(late_parts, square_rows, grad_normed))
    def image_total(sums, amount):
        pairs = sums[: 2 * amount].reshape(amount, 2, width)
        return same_everywhere(pairs[:, 0] + swapped(pairs[:, 1], "seq", 0))

    early = image_total(
        after(jnp.concatenate([middle_sums[:6], output_sums[:2]]), normed_sent), 4
    )
    conv_sum = after(tap_part[:9], normed_sent)
    for place in range(lax.axis_size("seq").bit_length() - 1):
        conv_sum = conv_sum + swapped(conv_sum, "seq", place)
    input_block, first_sums = call(
        first_norm_back_body,
        "first_norm_back",
        [((block_size, width), LOW), ((8, width), WIDE)],
        (
            after(grad_projected, late_parts, square_rows, early, conv_sum),
            qkv_flat,
            *grad_normed,
            after_grad,
            x_block,
            mod_own,
            mod_other,
        ),
        in_specs=[own_rows(grad_projected)] + [whole] * 8,
        table=table,
    )
    input_grad = placed_blocks(all_blocks(input_block)).astype(WIDE)
    output = placed_blocks(output_blocks)

    late = image_total(first_sums, 2)
    modulation_grad = jnp.stack([late[0], late[1], early[2], early[0], early[1], early[3]])

    block = square_rows.shape[1] // count
    square_grads = square_rows[:, : 3 * self_cols].astype(WIDE)
    for step in range(1, count):
        piece = square_rows[:, step * block : step * block + 3 * self_cols]
        square_grads = square_grads + from_ahead(piece, step).astype(WIDE)
    late_rows = late_rows.astype(WIDE)

    return (
        output,
        input_grad,
        modulation_grad[None],
        late_rows[:, : 3 * self_cols].reshape(-1, 3, self_cols),
        square_grads[:, 2 * self_cols :],
        square_grads[:, self_cols : 2 * self_cols],
        late_rows[:, 3 * self_cols :].reshape(-1, 2, cross_cols),
        square_grads[:, :self_cols],
        ffn_rows[:, ffn_pad:].astype(WIDE).reshape(-1, 2, ffn_pad)[:, :, :ffn_cols],
        conv_sum.reshape(9, 2, ffn_pad)[:, :, :ffn_cols],
        ffn_rows[:, :ffn_cols].astype(WIDE),
    )


def solution(mesh):
    placed = (
        P("seq", None),
        P("seq", None),
        P("seq", None, None),
        P("seq", None, None),
        P(),
        P(),
        P(None, None, "tp"),
        P(None, "tp"),
        P(None, "tp"),
        P(None, None, "tp"),
        P(None, "tp"),
        P(None, None, "tp"),
        P(None, None, "tp"),
        P(None, "tp"),
    )
    return jax.shard_map(
        shards,
        mesh=mesh,
        in_specs=placed,
        out_specs=(
            P("seq", None),
            P("seq", None),
            P("seq", None, None),
            P("seq", None, "tp"),
            P("seq", "tp"),
            P("seq", "tp"),
            P("seq", None, "tp"),
            P("seq", "tp"),
            P("seq", None, "tp"),
            P(None, None, "tp"),
            P("seq", "tp"),
        ),
        check_vma=False,
    )
```

```python
import functools
import math

import jax
import jax.numpy as jnp
from jax import lax
from jax.experimental import pallas as pl
from jax.experimental.pallas import tpu as pltpu
from jax.sharding import PartitionSpec as P

HEAD = 32
CROSS_HEAD = 72
MAXW = 32
LANES = 128
GRANT = 56 * 1024 * 1024

EPSILON = 1e-06
MASKED_OUT = -1e30
LOW = jnp.bfloat16
WIDE = jnp.float32

FIRST, CUT, SIDE, WIDTH, OWN_LENGTH, OTHER_LENGTH, BLOCK_FIRST, SEQ_TOKENS, TP_PLACE, ROW_PLACE = range(10)


def swapped(block, axis, apart):
    count = lax.axis_size(axis)
    route = [(low, low ^ (1 << apart)) for low in range(count)]
    return lax.ppermute(block, axis, route)


def from_behind(block, step):
    count = lax.axis_size("tp")
    return lax.ppermute(block, "tp", [(k, (k + step) % count) for k in range(count)])


def exchanged(blocks):
    return lax.all_to_all(blocks, "tp", 0, 0, tiled=True)


def dot(left, right):
    return jnp.dot(left, right, preferred_element_type=WIDE)


def times_transposed(left, right):
    return lax.dot_general(left, right, (((1,), (1,)), ((), ())), preferred_element_type=WIDE)


def over_tokens(left, right):
    return lax.dot_general(left, right, (((0,), (0,)), ((), ())), preferred_element_type=WIDE)


def split(wide):
    high = wide.astype(LOW)
    return high, (wide - high.astype(WIDE)).astype(LOW)


def call(body, name, outs, arrays, *, grid=None, in_specs=None, out_specs=None, scratch=(), flops=0, table=None):
    shapes = tuple(jax.ShapeDtypeStruct(*out) for out in outs)
    size = sum(math.prod(a.shape) * a.dtype.itemsize for a in (*arrays, *shapes))
    whole = pl.BlockSpec(memory_space=pltpu.VMEM)
    return pl.pallas_call(
        body,
        out_shape=shapes,
        grid_spec=pltpu.PrefetchScalarGridSpec(
            num_scalar_prefetch=1,
            grid=grid or (1,),
            in_specs=in_specs or [whole] * len(arrays),
            out_specs=out_specs or [whole] * len(shapes),
            scratch_shapes=list(scratch),
        ),
        compiler_params=pltpu.CompilerParams(vmem_limit_bytes=GRANT),
        cost_estimate=pl.CostEstimate(flops=0, bytes_accessed=size // 100, transcendentals=0),
        name=name,
    )(table, *arrays)


def own_image(table, start, rows):
    place = start + lax.broadcasted_iota(jnp.int32, (rows, 1), 0)
    return (place >= table[CUT]).astype(jnp.int32) == table[SIDE]


def pick(own, own_rows, other_rows, row):
    return jnp.where(
        own, own_rows[row : row + 1, :].astype(WIDE), other_rows[row : row + 1, :].astype(WIDE)
    )


def inverse_size(wide):
    return lax.rsqrt(jnp.mean(wide * wide, axis=-1, keepdims=True) + EPSILON)


def both_sums(own, values):
    mine = jnp.sum(jnp.where(own, values, 0.0), axis=0, keepdims=True)
    return mine, jnp.sum(jnp.where(own, 0.0, values), axis=0, keepdims=True)


def same_head(rows, columns):
    row_head = lax.broadcasted_iota(jnp.int32, (rows, columns), 0) // HEAD
    return row_head == lax.broadcasted_iota(jnp.int32, (rows, columns), 1) // HEAD


def fold(square):
    size = square.shape[1]
    total = None
    for low in range(0, size, LANES):
        part = square[:, low : min(low + LANES, size)]
        if part.shape[1] < LANES:
            part = jnp.concatenate(
                [part, jnp.zeros((part.shape[0], LANES - part.shape[1]), part.dtype)], axis=1
            )
        total = part if total is None else total + part
    return total


def unfold(folded):
    size = folded.shape[0]
    parts = [folded[:, : min(LANES, size - low)] for low in range(0, size, LANES)]
    return jnp.where(same_head(size, size), jnp.concatenate(parts, axis=1), 0.0)


def packed(square, totals):
    keep = same_head(square.shape[0], square.shape[1])
    return fold(jnp.where(keep, square, 0.0)) + pltpu.roll(
        fold(jnp.where(keep, totals, 0.0)), HEAD, 1
    )


def unpacked(folded):
    return unfold(folded), unfold(pltpu.roll(folded, LANES - HEAD, 1))


def log_exp(wide):
    return jnp.maximum(wide, 0.0) + jnp.log1p(jnp.exp(-jnp.abs(wide)))


def logistic(wide):
    return 1.0 / (1.0 + jnp.exp(-wide))


def self_project_body(table, x, mod_own, mod_other, weight, normed, raw, q, k, v, own_out, other_out, squares, totals):
    step = pl.program_id(0)
    rows, columns = q.shape
    own = own_image(table, table[FIRST] + step * rows, rows)
    wide = x[...].astype(WIDE)
    low = (
        wide * inverse_size(wide) * (1.0 + pick(own, mod_own, mod_other, 1))
        + pick(own, mod_own, mod_other, 0)
    ).astype(LOW)
    normed[...] = low
    out = times_transposed(low, weight[...])
    raw[...] = out[:, : 2 * columns]
    q[...] = log_exp(out[:, :columns]).astype(LOW)
    keys = log_exp(out[:, columns : 2 * columns]).astype(LOW)
    values = out[:, 2 * columns :].astype(LOW)
    k[...] = keys
    v[...] = values

    @pl.when(step == 0)
    def _():
        squares[...] = jnp.zeros_like(squares)
        totals[...] = jnp.zeros_like(totals)

    ones = jnp.ones((rows, columns), LOW)
    for image in range(2):
        zero = jnp.zeros_like(keys)
        masked = jnp.where(own, keys, zero) if image == 0 else jnp.where(own, zero, keys)
        squares[image] += over_tokens(masked, values)
        totals[image] += over_tokens(masked, ones)

    @pl.when(step == pl.num_programs(0) - 1)
    def _():
        own_out[...] = packed(squares[0], totals[0])
        other_out[...] = packed(squares[1], totals[1])


def self_project(table, x, mod_own, mod_other, weight, columns):
    tokens, width = x.shape
    rows = 128
    row = lambda c: pl.BlockSpec((rows, c), lambda i, t: (i, 0))
    fixed = lambda *s: pl.BlockSpec(s, lambda i, t: (0,) * len(s))
    return call(
        self_project_body,
        "self_project",
        [((tokens, width), LOW), ((tokens, 2 * columns), WIDE)]
        + [((tokens, columns), LOW)] * 3
        + [((columns, LANES), WIDE)] * 2,
        (x, mod_own, mod_other, weight),
        grid=(tokens // rows,),
        in_specs=[row(width), fixed(*mod_own.shape), fixed(*mod_own.shape), fixed(*weight.shape)],
        out_specs=[row(width), row(2 * columns)]
        + [row(columns)] * 3
        + [fixed(columns, LANES)] * 2,
        scratch=[pltpu.VMEM((2, columns, columns), WIDE)] * 2,
        flops=4 * tokens * width * 3 * columns,
        table=table,
    )


def keep_squares(kernels, key_totals, own_fold, other_fold):
    for image, folded in enumerate((own_fold, other_fold)):
        square, total = unpacked(folded[...])
        kernels[image, 0], kernels[image, 1] = split(square)
        key_totals[image, 0], key_totals[image, 1] = split(total)


def self_attend_body(table, q, own_fold, other_fold, attended, wide_out, denominator, kernels, key_totals):
    step = pl.program_id(0)
    rows = q.shape[0]

    @pl.when(step == 0)
    def _():
        keep_squares(kernels, key_totals, own_fold, other_fold)

    own = own_image(table, table[FIRST] + step * rows, rows)
    queries = q[...]

    def both(pair):
        own_part = dot(queries, pair[0, 0]) + dot(queries, pair[0, 1])
        return jnp.where(own, own_part, dot(queries, pair[1, 0]) + dot(queries, pair[1, 1]))

    under = both(key_totals) + 1.0
    out = both(kernels) / under
    attended[...] = out.astype(LOW)
    wide_out[...] = out
    denominator[...] = under


def self_attend(table, q, own_fold, other_fold):
    tokens, columns = q.shape
    rows = 128
    row = pl.BlockSpec((rows, columns), lambda i, t: (i, 0))
    fixed = pl.BlockSpec((columns, LANES), lambda i, t: (0, 0))
    return call(
        self_attend_body,
        "self_attend",
        [((tokens, columns), LOW), ((tokens, columns), WIDE), ((tokens, columns), WIDE)],
        (q, own_fold, other_fold),
        grid=(tokens // rows,),
        in_specs=[row, fixed, fixed],
        out_specs=[row, row, row],
        scratch=[pltpu.VMEM((2, 2, columns, columns), LOW)] * 2,
        flops=16 * tokens * columns * columns,
        table=table,
    )


def self_back_body(table, grad, q, wide_out, denominator, own_fold, other_fold, grad_q, own_out, other_out, kernels, key_totals, squares, totals):
    step = pl.program_id(0)
    rows, columns = q.shape

    @pl.when(step == 0)
    def _():
        keep_squares(kernels, key_totals, own_fold, other_fold)
        squares[...] = jnp.zeros_like(squares)
        totals[...] = jnp.zeros_like(totals)

    own = own_image(table, table[FIRST] + step * rows, rows)
    wide = grad[0].astype(WIDE)
    over = 1.0 / denominator[...]
    numer_high, numer_low = split(wide * over)
    ones = jnp.where(same_head(columns, columns), 1.0, 0.0).astype(LOW)
    high, low = split(wide * wide_out[...])
    denom = -(dot(high, ones) + dot(low, ones)) * over
    denom_high, denom_low = split(denom)

    def back(image):
        square, total = kernels[image, 0], key_totals[image, 0]
        through = (
            times_transposed(numer_high, square)
            + times_transposed(numer_low, square)
            + times_transposed(numer_high, kernels[image, 1])
        )
        totals_part = (
            times_transposed(denom_high, total)
            + times_transposed(denom_low, total)
            + times_transposed(denom_high, key_totals[image, 1])
        )
        return through + totals_part * (1.0 / HEAD)

    grad_q[...] = jnp.where(own, back(0), back(1))
    queries = q[...]
    zero = jnp.zeros_like(queries)
    for image in range(2):
        masked = jnp.where(own, queries, zero) if image == 0 else jnp.where(own, zero, queries)
        squares[image] += over_tokens(masked, numer_high) + over_tokens(masked, numer_low)
        totals[image] += over_tokens(masked, denom_high) + over_tokens(masked, denom_low)

    @pl.when(step == pl.num_programs(0) - 1)
    def _():
        own_out[...] = packed(squares[0], totals[0])
        other_out[...] = packed(squares[1], totals[1])


def self_back(table, grad, q, wide_out, denominator, own_fold, other_fold):
    count, rows, columns = grad.shape
    tokens = q.shape[0]
    row = pl.BlockSpec((rows, columns), lambda i, t: (i, 0))
    fixed = pl.BlockSpec((columns, LANES), lambda i, t: (0, 0))
    return call(
        self_back_body,
        "self_back",
        [((tokens, columns), WIDE)] + [((columns, LANES), WIDE)] * 2,
        (grad, q, wide_out, denominator, own_fold, other_fold),
        grid=(count,),
        in_specs=[pl.BlockSpec((1, rows, columns), lambda i, t: (i, 0, 0)), row, row, row, fixed, fixed],
        out_specs=[row, fixed, fixed],
        scratch=[pltpu.VMEM((2, 2, columns, columns), LOW)] * 2
        + [pltpu.VMEM((2, columns, columns), WIDE)] * 2,
        flops=48 * tokens * columns * columns,
        table=table,
    )


def self_project_back_body(table, grad_q, k, v, raw, own_fold, other_fold, grad_out, kernels, key_totals):
    step = pl.program_id(0)
    rows, columns = k.shape

    @pl.when(step == 0)
    def _():
        keep_squares(kernels, key_totals, own_fold, other_fold)

    own = own_image(table, table[FIRST] + step * rows, rows)
    keys, values = k[...], v[...]
    ones = jnp.ones((16, columns), LOW)

    def grad_k(image):
        total = times_transposed(ones, key_totals[image, 0]) + times_transposed(
            ones, key_totals[image, 1]
        )
        return (
            times_transposed(values, kernels[image, 0])
            + times_transposed(values, kernels[image, 1])
            + total[:1] * (1.0 / HEAD)
        )

    def grad_v(image):
        return dot(keys, kernels[image, 0]) + dot(keys, kernels[image, 1])

    given = raw[...]
    q_part = grad_q[...] * logistic(given[:, :columns])
    k_part = jnp.where(own, grad_k(0), grad_k(1)) * logistic(given[:, columns:])
    v_part = jnp.where(own, grad_v(0), grad_v(1))
    grad_out[...] = jnp.concatenate([q_part, k_part, v_part], axis=1).astype(LOW)


def self_project_back(table, grad_q, k, v, raw, own_fold, other_fold):
    tokens, columns = k.shape
    rows = 128
    row = lambda c: pl.BlockSpec((rows, c), lambda i, t: (i, 0))
    fixed = pl.BlockSpec((columns, LANES), lambda i, t: (0, 0))
    return call(
        self_project_back_body,
        "self_project_back",
        [((tokens, 3 * columns), LOW)],
        (grad_q, k, v, raw, own_fold, other_fold),
        grid=(tokens // rows,),
        in_specs=[row(columns), row(columns), row(columns), row(2 * columns), fixed, fixed],
        out_specs=[row(3 * columns)],
        scratch=[pltpu.VMEM((2, 2, columns, columns), LOW)] * 2,
        flops=16 * tokens * columns * columns,
        table=table,
    )[0]


def live_keys(table, own, keys):
    place = lax.broadcasted_iota(jnp.int32, (1, keys), 1)
    return place < jnp.where(own, table[OWN_LENGTH], table[OTHER_LENGTH])


def shard_of(first, rest, step, which):
    rows = first.shape[0]
    return first[...] if step == 0 else rest[step - 1, which * rows : (which + 1) * rows, :]


def middle_body(table, att, x, mod_own, mod_other, out_first, query_first, cross_first, *refs):
    pieces, (kv_own, kv_other) = refs[:8], refs[8:10]
    branch, after_low, queries_out, probs_out, text_out, after_cross, normed, rest = refs[10:]
    put_in_order(table, pieces, rest)
    count, rows, columns = att.shape
    keys = kv_own.shape[1]
    heads = columns // CROSS_HEAD
    own = own_image(table, table[BLOCK_FIRST], rows)
    y1 = jnp.zeros((rows, x.shape[1]), WIDE)
    for step in range(count):
        y1 += dot(att[turned(table, step, count)], shard_of(out_first, rest, step, 0))
    branch[...] = y1
    x1 = x[...].astype(WIDE) + pick(own, mod_own, mod_other, 2) * y1
    x1_low = x1.astype(LOW)
    after_low[...] = x1_low
    live = live_keys(table, own, keys)
    yc = jnp.zeros_like(x1)
    for step in range(count):
        queries = times_transposed(x1_low, shard_of(query_first, rest, step, 1)).astype(LOW)
        queries_out[step] = queries
        place = turned(table, step, count)
        mine, theirs = kv_own[place], kv_other[place]
        parts = []
        for head in range(heads):
            lanes = slice(head * CROSS_HEAD, (head + 1) * CROSS_HEAD)
            wide_lanes = slice(columns + head * CROSS_HEAD, columns + (head + 1) * CROSS_HEAD)
            q = queries[:, lanes]
            scores = jnp.where(
                own, times_transposed(q, mine[:, lanes]), times_transposed(q, theirs[:, lanes])
            ) * (1.0 / math.sqrt(CROSS_HEAD))
            scores = jnp.where(live, scores, MASKED_OUT)
            raised = jnp.exp(scores - jnp.max(scores, axis=-1, keepdims=True))
            probs = raised / jnp.sum(raised, axis=-1, keepdims=True)
            probs_out[step * heads + head] = probs
            low = probs.astype(LOW)
            parts.append(
                jnp.where(own, dot(low, mine[:, wide_lanes]), dot(low, theirs[:, wide_lanes]))
            )
        text = jnp.concatenate(parts, axis=1).astype(LOW)
        text_out[step] = text
        yc += dot(text, shard_of(cross_first, rest, step, 2))
    x2 = x1 + yc
    after_cross[...] = x2
    normed[...] = (
        x2 * inverse_size(x2) * (1.0 + pick(own, mod_own, mod_other, 4))
        + pick(own, mod_own, mod_other, 3)
    ).astype(LOW)


def middle_back_body(table, grads, x2_in, upstream, branch, mod_own, mod_other, out_first, query_first, cross_first, rest, kv_own, kv_other, probs_in, queries_in, cross_grad, query_grad, attn_grad, attended_grad, after_grad, sums, kv_own_grad, kv_other_grad):
    count, rows, columns = queries_in.shape
    keys = kv_own.shape[1]
    heads = columns // CROSS_HEAD
    scale = 1.0 / math.sqrt(CROSS_HEAD)
    own = own_image(table, table[BLOCK_FIRST], rows)
    grad = total(grads)
    x2 = x2_in[...]
    inverse = inverse_size(x2)
    xh = x2 * inverse
    sums[0:1], sums[1:2] = both_sums(own, grad)
    sums[2:3], sums[3:4] = both_sums(own, grad * xh)
    e = grad * (1.0 + pick(own, mod_own, mod_other, 4))
    dx2 = upstream[...].astype(WIDE) + inverse * (
        e - xh * jnp.mean(e * xh, axis=-1, keepdims=True)
    )
    dyc = dx2.astype(LOW)
    cross_grad[...] = dyc
    dx1 = dx2
    for step in range(count):
        doc = times_transposed(dyc, shard_of(cross_first, rest, step, 2)).astype(LOW)
        place = turned(table, step, count)
        mine, theirs = kv_own[place], kv_other[place]
        queries = queries_in[step]
        query_parts = []
        key_parts = ([], [])
        value_parts = ([], [])
        for head in range(heads):
            lanes = slice(head * CROSS_HEAD, (head + 1) * CROSS_HEAD)
            wide_lanes = slice(columns + head * CROSS_HEAD, columns + (head + 1) * CROSS_HEAD)
            do, q = doc[:, lanes], queries[:, lanes]
            probs = probs_in[step * heads + head]
            dp = jnp.where(
                own,
                times_transposed(do, mine[:, wide_lanes]),
                times_transposed(do, theirs[:, wide_lanes]),
            )
            ds = (probs * (dp - jnp.sum(probs * dp, axis=-1, keepdims=True))).astype(LOW)
            low = probs.astype(LOW)
            zero = jnp.zeros_like(ds)
            query_parts.append(
                jnp.where(own, dot(ds, mine[:, lanes]), dot(ds, theirs[:, lanes])) * scale
            )
            for image in range(2):
                mask = (lambda a: jnp.where(own, a, zero)) if image == 0 else (
                    lambda a: jnp.where(own, zero, a)
                )
                key_parts[image].append(over_tokens(mask(ds), q) * scale)
                value_parts[image].append(over_tokens(mask(low), do))
        dqc = jnp.concatenate(query_parts, axis=1).astype(LOW)
        query_grad[step] = dqc
        kv_own_grad[place] = jnp.concatenate(key_parts[0] + value_parts[0], axis=1).astype(LOW)
        kv_other_grad[place] = jnp.concatenate(key_parts[1] + value_parts[1], axis=1).astype(LOW)
        dx1 = dx1 + dot(dqc, shard_of(query_first, rest, step, 1))
    after_grad[...] = dx1
    sums[4:5], sums[5:6] = both_sums(own, dx1 * branch[...])
    sums[6:8] = jnp.zeros((2, sums.shape[1]), WIDE)
    dy1 = (dx1 * pick(own, mod_own, mod_other, 2)).astype(LOW)
    attn_grad[...] = dy1
    for step in range(count):
        attended_grad[turned(table, step, count)] = times_transposed(
            dy1, shard_of(out_first, rest, step, 0)
        ).astype(LOW)


def first_norm_back_body(table, grads, after_grad, x, mod_own, mod_other, input_grad, sums):
    rows = x.shape[0]
    own = own_image(table, table[BLOCK_FIRST], rows)
    grad = total(grads)
    wide = x[...].astype(WIDE)
    inverse = inverse_size(wide)
    xh = wide * inverse
    sums[0:1], sums[1:2] = both_sums(own, grad)
    sums[2:3], sums[3:4] = both_sums(own, grad * xh)
    sums[4:8] = jnp.zeros((4, sums.shape[1]), WIDE)
    e = grad * (1.0 + pick(own, mod_own, mod_other, 1))
    input_grad[...] = (
        after_grad[...] + inverse * (e - xh * jnp.mean(e * xh, axis=-1, keepdims=True))
    ).astype(LOW)


def output_body(table, branches, x2, upstream, mod_own, mod_other, output, sums):
    rows = x2.shape[0]
    own = own_image(table, table[BLOCK_FIRST], rows)
    branch = total(branches)
    sums[0:1], sums[1:2] = both_sums(own, upstream[...].astype(WIDE) * branch)
    sums[2:8] = jnp.zeros((6, sums.shape[1]), WIDE)
    output[...] = (x2[...] + pick(own, mod_own, mod_other, 5) * branch).astype(LOW)


def up_body(table, *refs):
    blocks, weight, (wide_out, low_out, ordered) = refs[:-4], refs[-4], refs[-3:]
    step = pl.program_id(0)
    for place, ref in enumerate(blocks):

        @pl.when(step == place)
        def _():
            ordered[...] = ref[...]

    up = times_transposed(ordered[...], weight[...])
    wide_out[...] = up
    low_out[...] = (up * logistic(up)).astype(LOW)


def up_project(table, blocks, weight):
    count = len(blocks)
    rows, width = blocks[0].shape
    columns = weight.shape[0]
    turn = lambda i, t: (turned(t, i, count), 0)
    whole = lambda a: pl.BlockSpec(a.shape, lambda i, t: (0, 0))
    return call(
        up_body,
        "up_project",
        [((count * rows, columns), WIDE), ((count * rows, columns), LOW), ((count * rows, width), LOW)],
        (*blocks, weight),
        grid=(count,),
        in_specs=[whole(array) for array in (*blocks, weight)],
        out_specs=[pl.BlockSpec((rows, columns), turn)] * 2 + [pl.BlockSpec((rows, width), turn)],
        table=table,
    )


def fill(padded, block, rim):
    tokens = block.shape[0]
    edge = rim[...].astype(WIDE)
    padded[0:MAXW, :] = edge
    padded[MAXW : MAXW + tokens, :] = block.astype(WIDE)
    padded[MAXW + tokens : 2 * MAXW + tokens, :] = edge


def fill_masks(table, masks):
    tokens = masks.shape[1]
    place = table[FIRST] + lax.broadcasted_iota(jnp.int32, (tokens, LANES), 0)
    width = table[WIDTH]
    cut = table[CUT]
    late = place >= cut
    start = jnp.where(late, cut, 0)
    end = jnp.where(late, table[SEQ_TOKENS], cut)
    column = lax.bitwise_and(place, width - 1)
    one, none = jnp.ones((tokens, LANES), WIDE), jnp.zeros((tokens, LANES), WIDE)
    masks[0] = jnp.where(place - width >= start, one, none)
    masks[1] = jnp.where(place + width < end, one, none)
    masks[2] = jnp.where(column > 0, one, none)
    masks[3] = jnp.where(column < width - 1, one, none)


CHUNK = 64


def three_rows(table, padded, masks, low):
    width = table[WIDTH]
    above = padded[pl.ds(pl.multiple_of(MAXW + low - width, 16), CHUNK), :]
    below = padded[pl.ds(pl.multiple_of(MAXW + low + width, 16), CHUNK), :]
    own = padded[pl.ds(pl.multiple_of(MAXW + low, 16), CHUNK), :]
    rows = pl.ds(pl.multiple_of(low, 16), CHUNK)
    return above * masks[0, rows, :], own, below * masks[1, rows, :]


def nine_taps(rows, taps, left_mask, right_mask):
    mixed = [sum(rows[a] * taps[a][b] for a in range(3)) for b in range(3)]
    return (
        mixed[1]
        + left_mask * pltpu.roll(mixed[0], 1, 0)
        + right_mask * pltpu.roll(mixed[2], CHUNK - 1, 0)
    )


def taps_of(taps, flip):
    read = lambda a, b: taps[3 * a + b : 3 * a + b + 1, :]
    return [[read(2 - a, 2 - b) if flip else read(a, b) for b in range(3)] for a in range(3)]


def mix_body(table, value, gate, value_rim, gate_rim, value_taps, gate_taps, grad_hidden, hidden, grads, value_pad, gate_pad, masks):
    @pl.when(pl.program_id(0) == 0)
    def _():
        fill_masks(table, masks)

    fill(value_pad, value[...], value_rim)
    fill(gate_pad, gate[...], gate_rim)
    value_weights, gate_weights = taps_of(value_taps, False), taps_of(gate_taps, False)

    @pl.loop(0, value.shape[0] // CHUNK)
    def _(index):
        low = index * CHUNK
        rows = pl.ds(pl.multiple_of(low, CHUNK), CHUNK)
        left, right = masks[2, rows, :], masks[3, rows, :]
        mv = nine_taps(three_rows(table, value_pad, masks, low), value_weights, left, right)
        mg = nine_taps(three_rows(table, gate_pad, masks, low), gate_weights, left, right)
        sigma = logistic(mg)
        gated = mg * sigma
        hidden[rows, :] = (mv * gated).astype(LOW)
        dh = grad_hidden[rows, :]
        grads[0, rows, :] = (dh * gated).astype(LOW)
        grads[1, rows, :] = (dh * mv * (sigma * (1.0 + mg * (1.0 - sigma)))).astype(LOW)


def mix(table, activated, rim, taps, grad_hidden):
    tokens, wide = activated.shape
    columns = wide // 2
    tiles = columns // LANES
    block = lambda r, shift: pl.BlockSpec((r, LANES), lambda i, t: (0, i + shift))
    pad = pltpu.VMEM((tokens + 2 * MAXW, LANES), WIDE)
    return call(
        mix_body,
        "mix",
        [((tokens, columns), LOW), ((2, tokens, columns), LOW)],
        (activated, activated, rim, rim, taps, taps, grad_hidden),
        grid=(tiles,),
        in_specs=[
            block(tokens, 0),
            block(tokens, tiles),
            block(MAXW, 0),
            block(MAXW, tiles),
            block(taps.shape[0], 0),
            block(taps.shape[0], tiles),
            block(tokens, 0),
        ],
        out_specs=[
            block(tokens, 0),
            pl.BlockSpec((2, tokens, LANES), lambda i, t: (0, 0, i)),
        ],
        scratch=[pad, pad, pltpu.VMEM((4, tokens, LANES), WIDE)],
        flops=6000 * tokens * columns // 2,
        table=table,
    )


def mix_back_body(table, grads, grads_rim, activated, rim, taps, up, grad_up, tap_grads, grad_pad, act_pad, masks):
    @pl.when(pl.program_id(0) == 0)
    def _():
        fill_masks(table, masks)

    fill(grad_pad, grads[0], grads_rim.at[0])
    fill(act_pad, activated[...], rim)
    weights = taps_of(taps, True)

    def step(index, sums):
        low = index * CHUNK
        rows = pl.ds(pl.multiple_of(low, CHUNK), CHUNK)
        left, right = masks[2, rows, :], masks[3, rows, :]
        mine = three_rows(table, grad_pad, masks, low)
        dact = nine_taps(mine, weights, left, right)
        given = up[rows, :]
        sigma = logistic(given)
        grad_up[rows, :] = (dact * (sigma * (1.0 + given * (1.0 - sigma)))).astype(LOW)
        acts = three_rows(table, act_pad, masks, low)
        turned = (
            right * pltpu.roll(mine[1], CHUNK - 1, 0),
            mine[1],
            left * pltpu.roll(mine[1], 1, 0),
        )
        return tuple(
            sums[3 * a + b]
            + jnp.sum((acts[a] * turned[b]).reshape(CHUNK // 8, 8, LANES), axis=0)
            for a in range(3)
            for b in range(3)
        )

    zero = jnp.zeros((8, LANES), WIDE)
    sums = lax.fori_loop(0, activated.shape[0] // CHUNK, step, (zero,) * 9)
    for tap in range(9):
        tap_grads[tap : tap + 1, :] = jnp.sum(sums[tap], axis=0, keepdims=True)
    tap_grads[9:16, :] = jnp.zeros((7, LANES), WIDE)


def mix_back(table, grads, grads_rim, activated, rim, taps, up):
    tokens, wide = activated.shape
    columns = wide // 2
    tiles = columns // LANES
    block = lambda r: pl.BlockSpec((r, LANES), lambda i, t: (0, i))
    half = lambda r: pl.BlockSpec(
        (1, r, LANES), lambda i, t: (lax.div(i, tiles), 0, lax.rem(i, tiles))
    )
    pad = pltpu.VMEM((tokens + 2 * MAXW, LANES), WIDE)
    return call(
        mix_back_body,
        "mix_back",
        [((tokens, wide), LOW), ((16, wide), WIDE)],
        (grads, grads_rim, activated, rim, taps, up),
        grid=(2 * tiles,),
        in_specs=[half(tokens), half(MAXW), block(tokens), block(MAXW), block(taps.shape[0]), block(tokens)],
        out_specs=[block(tokens), block(16)],
        scratch=[pad, pad, pltpu.VMEM((4, tokens, LANES), WIDE)],
        flops=6000 * tokens * columns,
        table=table,
    )


def eighth_body(table, *refs):
    weights, out, joined = refs[:-2], refs[-2], refs[-1]
    low = 0
    for weight in weights:
        joined[low : low + weight.shape[0], :] = weight[...]
        low += weight.shape[0]
    rows = out.shape[0]
    out[...] = joined[pl.ds(pl.multiple_of(table[0] * rows, 16), rows), :]


def put_in_order(table, pieces, out):
    steps, rows = pieces[0].shape[0], pieces[0].shape[1]
    for place, piece in enumerate(pieces):
        block = lax.bitwise_xor(table[ROW_PLACE], place)
        for step in range(steps):
            out[step, pl.ds(pl.multiple_of(block * rows, 16), rows), :] = piece[step]


def after(value, *others):
    return lax.optimization_barrier((value, others))[0]


def fetch_eighths(weights):
    columns = weights[0].shape[1]
    rows = -(-sum(weight.shape[0] for weight in weights) // LANES) * 16
    eighth = call(
        eighth_body,
        "eighth",
        [((rows, columns), weights[0].dtype)],
        weights,
        scratch=[pltpu.VMEM((8 * rows, columns), weights[0].dtype)],
        table=(lax.axis_index("seq") % 8).reshape(1).astype(jnp.int32),
    )[0]
    return jnp.stack([from_behind(eighth, step) for step in range(1, lax.axis_size("tp"))])


def share_eighths(fetched, ready):
    count = lax.axis_size("seq")
    far = lambda flip: lax.ppermute(fetched, "seq", [(k, k ^ flip) for k in range(count)])
    pieces = []
    for piece in [fetched] + after([far(2), far(4), far(6)], *ready):
        pieces += [piece, swapped(piece, "seq", 0)]
    return pieces


def token_block(values, place):
    count = lax.axis_size("tp")
    size = values.shape[0] // count
    return lax.dynamic_slice_in_dim(values, (place % count) * size, size, 0)


def placed_blocks(blocks):
    count = len(blocks)
    place = lax.axis_index("tp")
    result = jnp.zeros((count,) + blocks[0].shape, blocks[0].dtype)
    for step in range(count):
        result = lax.dynamic_update_index_in_dim(result, blocks[step], (place - step) % count, 0)
    return result.reshape((count * blocks[0].shape[0],) + blocks[0].shape[1:])


def all_blocks(block):
    return [block] + [from_behind(block, step) for step in range(1, lax.axis_size("tp"))]


def product_body(table, left, right, out):
    out[0] = dot(left[...], right[...]).astype(LOW)


def product(table, left, right):
    count = lax.axis_size("tp")
    rows, columns = left.shape[0] // count, left.shape[1]
    return call(
        product_body,
        "product",
        [((count, rows, right.shape[1]), LOW)],
        (left, right),
        grid=(count,),
        in_specs=[
            pl.BlockSpec((rows, columns), lambda i, t: (i, 0)),
            pl.BlockSpec(right.shape, lambda i, t: (0, 0)),
        ],
        out_specs=[pl.BlockSpec((1, rows, right.shape[1]), lambda i, t: (i, 0, 0))],
        table=table,
    )[0]


def total(parts):
    result = parts[0].astype(WIDE)
    for place in range(1, parts.shape[0]):
        result += parts[place].astype(WIDE)
    return result


def turned(table, step, count):
    return lax.rem(table[TP_PLACE] + count - step, count)


def same_everywhere(block):
    count = lax.axis_size("tp")
    flipped = lambda flip: lax.ppermute(block, "tp", [(k, k ^ flip) for k in range(count)])
    return (block + flipped(1)) + (flipped(2) + flipped(3))


def sum_rows(grad):
    return lax.optimization_barrier(
        lax.psum_scatter(grad.astype(LOW), "seq", scatter_dimension=0, tiled=True)
    )


def square_body(table, dyc, text, x1, dqc, dy1, att, out):
    parts = [
        over_tokens(left[...], right[0]) for left, right in ((dyc, text), (x1, dqc), (dy1, att))
    ]
    rest = out.shape[1] - sum(part.shape[1] for part in parts)
    if rest:
        parts.append(jnp.zeros((out.shape[0], rest), WIDE))
    out[...] = jnp.concatenate(parts, axis=1).astype(LOW)


def square_parts(table, lefts, rights):
    rows, width = lefts[0].shape
    count, _, columns = rights[0].shape
    block = -(-3 * columns // LANES) * LANES
    whole = pl.BlockSpec((rows, width), lambda i, t: (0, 0))
    one = pl.BlockSpec((1, rows, columns), lambda i, t: (turned(t, i, count), 0, 0))
    still = pl.BlockSpec((1, rows, columns), lambda i, t: (i, 0, 0))
    return call(
        square_body,
        "square_parts",
        [((width, count * block), LOW)],
        [array for pair in zip(lefts, rights) for array in pair],
        grid=(count,),
        in_specs=[whole, one, whole, one, whole, still],
        out_specs=[pl.BlockSpec((width, block), lambda i, t: (0, i))],
        flops=8 * rows * width * count * block,
        table=table,
    )[0]


def ffn_body(table, grad_ffn, hidden, normed, grad_up, out):
    step = pl.program_id(0)

    @pl.when(step == 0)
    def _():
        out[...] = over_tokens(grad_ffn[...], hidden[...]).astype(LOW)

    @pl.when(step > 0)
    def _():
        out[...] = over_tokens(normed[...], grad_up[...]).astype(LOW)


def ffn_parts_of(table, grad_ffn, hidden, normed, grad_up):
    tokens, width = normed.shape
    columns = hidden.shape[1]
    whole = pl.BlockSpec((tokens, width), lambda i, t: (0, 0))
    return call(
        ffn_body,
        "ffn_parts",
        [((width, 3 * columns), LOW)],
        (grad_ffn, hidden, normed, grad_up),
        grid=(3,),
        in_specs=[
            whole,
            pl.BlockSpec((tokens, columns), lambda i, t: (0, 0)),
            whole,
            pl.BlockSpec((tokens, columns), lambda i, t: (0, jnp.maximum(i - 1, 0))),
        ],
        out_specs=[pl.BlockSpec((width, columns), lambda i, t: (0, i))],
        table=table,
    )[0]


def late_body(table, normed, grad_projected, text, kv_grads, out):
    first = over_tokens(normed[...], grad_projected[...]).astype(LOW)
    second = over_tokens(text[...], total(kv_grads).astype(LOW)).astype(LOW)
    out[...] = jnp.concatenate([first, second], axis=1)


def shards(
    hidden_in,
    cotangent,
    modulation,
    text_states,
    image_shapes,
    text_lengths,
    qkv_weight,
    attn_out_weight,
    cross_q_weight,
    cross_kv_weight,
    cross_out_weight,
    up_weight,
    conv_weight,
    down_weight,
):
    tokens_here, width = hidden_in.shape
    context = text_states.shape[1]
    keys = -(-context // 16) * 16
    self_cols = qkv_weight.shape[2]
    cross_cols = cross_q_weight.shape[1]
    ffn_cols = up_weight.shape[2]
    ffn_pad = -(-ffn_cols // LANES) * LANES
    count = lax.axis_size("tp")
    tp_index = lax.axis_index("tp")
    block_size = tokens_here // count
    seq_index = lax.axis_index("seq")
    side = seq_index % 2
    first_half = side == 0
    pair = seq_index - side
    pair_shapes = lax.dynamic_slice_in_dim(image_shapes, pair, 2, 0)
    row_width = pair_shapes[0, 1]
    lengths = lax.dynamic_slice_in_dim(text_lengths, pair, 2, 0)
    first_place = side * tokens_here
    table = jnp.stack(
        [
            first_place,
            pair_shapes[0, 0] * row_width,
            side,
            row_width,
            jnp.where(first_half, lengths[0], lengths[1]),
            jnp.where(first_half, lengths[1], lengths[0]),
            first_place + tp_index * block_size,
            jnp.int32(2 * tokens_here),
            tp_index,
            seq_index % 8,
        ]
    ).astype(jnp.int32)

    mod_own = modulation[0]
    mod_other = swapped(mod_own, "seq", 0).astype(WIDE)
    mod_own = mod_own.astype(WIDE)
    weights = [attn_out_weight.T, cross_q_weight.T, cross_out_weight.T]
    fetched = fetch_eighths(weights)
    qkv_flat = qkv_weight.transpose(1, 2, 0).reshape(3 * self_cols, width)
    text_rows = jnp.pad(text_states[0], ((0, keys - context), (0, 0)))
    kv_here = times_transposed(
        text_rows, cross_kv_weight.transpose(1, 2, 0).reshape(2 * cross_cols, width)
    ).astype(LOW)
    kv_sent_first = jnp.broadcast_to(kv_here[None], (count,) + kv_here.shape)
    normed_low, raw, q, k, v, part_own, part_other = self_project(
        table, after(hidden_in, kv_sent_first), mod_own, mod_other, qkv_flat, self_cols
    )
    theirs = swapped(jnp.stack([part_own, part_other]), "seq", 0)
    fetched = after(fetched, q)
    kernel_own, kernel_other = part_own + theirs[1], part_other + theirs[0]
    attended, attended_wide, denominator = self_attend(
        table, after(q, kv_here), kernel_own, kernel_other
    )

    x_block = token_block(hidden_in, tp_index)
    up_block = token_block(cotangent, tp_index)
    up_flat = jnp.pad(
        after(up_weight.transpose(1, 2, 0), attended), ((0, 0), (0, ffn_pad - ffn_cols), (0, 0))
    ).reshape(2 * ffn_pad, width)
    down_flat = jnp.pad(after(down_weight.T, attended), ((0, ffn_pad - ffn_cols), (0, 0)))
    taps = (
        jnp.pad(conv_weight, ((0, 7), (0, 0), (0, ffn_pad - ffn_cols)))
        .reshape(16, 2 * ffn_pad)
        .astype(WIDE)
    )
    gate_rows = jnp.where(
        (first_place + jnp.arange(tokens_here, dtype=jnp.int32) >= table[CUT])[:, None] == (side == 1),
        mod_own[5:6],
        mod_other[5:6],
    )
    grad_ffn = (cotangent.astype(WIDE) * gate_rows).astype(LOW)
    grad_hidden = times_transposed(grad_ffn, down_flat)
    ready = (up_flat, taps, grad_hidden)
    split_tokens = lambda values: values.reshape(count, block_size, values.shape[1])
    kv_own = exchanged(kv_sent_first)
    attended_blocks = exchanged(after(split_tokens(attended), kv_own))
    kv_own = after(kv_own, *ready)
    kv_other = swapped(kv_own, "seq", 0)
    pieces = share_eighths(fetched, ready)
    all_heads = count * cross_cols // CROSS_HEAD
    branch, after_low, queries, probs, text_low, after_cross, normed_two, rest = call(
        middle_body,
        "middle",
        [
            ((block_size, width), WIDE),
            ((block_size, width), LOW),
            ((count, block_size, cross_cols), LOW),
            ((all_heads, block_size, keys), WIDE),
            ((count, block_size, cross_cols), LOW),
            ((block_size, width), WIDE),
            ((block_size, width), LOW),
            ((count - 1, 8 * fetched.shape[1], width), LOW),
        ],
        (attended_blocks, x_block, mod_own, mod_other, *weights, *pieces, kv_own, kv_other),
        flops=60 * block_size * width * width,
        table=table,
    )

    up_wide, activated, normed_two_low = up_project(table, all_blocks(normed_two), up_flat)
    rim = swapped(jnp.where(first_half, activated[-MAXW:], activated[:MAXW]), "seq", 0)
    hidden, grads = mix(table, activated, rim, taps, grad_hidden)
    grads_rim = swapped(jnp.where(first_half, grads[:, -MAXW:], grads[:, :MAXW]), "seq", 0)
    branch_sent = product(table, hidden, down_flat)
    grad_up, tap_part = mix_back(
        table, grads, grads_rim, activated, rim, taps, after(up_wide, branch_sent)
    )
    branches = exchanged(branch_sent)
    norm_two_sent = product(table, grad_up, up_flat)
    grad_norm_two = exchanged(after(norm_two_sent, branches))
    ffn_parts = ffn_parts_of(
        table, grad_ffn, after(hidden, norm_two_sent), normed_two_low, grad_up
    )
    ffn_rows = sum_rows(after(ffn_parts, grad_norm_two))
    output_block, output_sums = call(
        output_body,
        "output",
        [((block_size, width), LOW), ((8, width), WIDE)],
        (branches, after_cross, up_block, mod_own, mod_other),
        table=table,
    )
    output_blocks = all_blocks(output_block)

    (
        cross_grad,
        query_grad,
        attn_grad,
        attended_grad,
        after_grad,
        middle_sums,
        kv_own_grad,
        kv_other_grad,
    ) = call(
        middle_back_body,
        "middle_back",
        [
            ((block_size, width), LOW),
            ((count, block_size, cross_cols), LOW),
            ((block_size, width), LOW),
            ((count, block_size, self_cols), LOW),
            ((block_size, width), WIDE),
            ((8, width), WIDE),
            ((count, keys, 2 * cross_cols), LOW),
            ((count, keys, 2 * cross_cols), LOW),
        ],
        (
            after(grad_norm_two, ffn_parts, output_block),
            after_cross,
            up_block,
            branch,
            mod_own,
            mod_other,
            *weights,
            rest,
            kv_own,
            kv_other,
            probs,
            queries,
        ),
        flops=120 * block_size * width * width,
        table=table,
    )

    grad_blocks = exchanged(after(attended_grad, output_blocks))
    squares = square_parts(
        table,
        (cross_grad, after_low, attn_grad),
        (text_low, query_grad, after(attended_blocks, attended_grad)),
    )
    square_rows = sum_rows(after(squares, grad_blocks))
    kv_sent = (
        kv_own_grad.astype(WIDE) + swapped(kv_other_grad, "seq", 0).astype(WIDE)
    ).astype(LOW)
    kv_sent = after(kv_sent, grad_blocks)
    kv_parts = exchanged(kv_sent)
    grad_blocks = after(grad_blocks, squares, kv_sent, ffn_rows)
    grad_q, back_own, back_other = self_back(
        table, grad_blocks, q, attended_wide, denominator, kernel_own, kernel_other
    )
    back_theirs = swapped(jnp.stack([back_own, back_other]), "seq", 0)
    grad_projected = self_project_back(
        table,
        grad_q,
        k,
        v,
        raw,
        back_own + back_theirs[1],
        back_other + back_theirs[0],
    )
    normed_sent = product(table, grad_projected, qkv_flat)
    grad_normed = exchanged(after(normed_sent, kv_parts))
    late_parts = call(
        late_body,
        "late_parts",
        [((width, 3 * self_cols + 2 * cross_cols), LOW)],
        (normed_low, after(grad_projected, normed_sent), text_rows, kv_parts),
        table=table,
    )[0]
    late_rows = sum_rows(after(late_parts, square_rows, grad_normed))
    conv_sum = after(tap_part[:9], normed_sent)
    for place in range(lax.axis_size("seq").bit_length() - 1):
        conv_sum = conv_sum + swapped(conv_sum, "seq", place)
    input_block, first_sums = call(
        first_norm_back_body,
        "first_norm_back",
        [((block_size, width), LOW), ((8, width), WIDE)],
        (
            after(grad_normed, late_parts, square_rows),
            after_grad,
            x_block,
            mod_own,
            mod_other,
        ),
        table=table,
    )
    square_sent = square_rows.reshape(square_rows.shape[0], count, -1).transpose(1, 0, 2)
    square_grads = total(exchanged(after(square_sent, grad_normed)))[:, : 3 * self_cols]
    input_blocks = all_blocks(input_block)
    input_grad = placed_blocks(input_blocks).astype(WIDE)
    output = placed_blocks(output_blocks)

    pairs = jnp.concatenate([first_sums[:4], middle_sums[4:6], middle_sums[:4], output_sums[:2]])
    pairs = pairs.reshape(6, 2, width)
    modulation_grad = same_everywhere(
        after(pairs[:, 0] + swapped(pairs[:, 1], "seq", 0), input_blocks)
    )

    late_rows = late_rows.astype(WIDE)

    return (
        output,
        input_grad,
        modulation_grad[None],
        late_rows[:, : 3 * self_cols].reshape(-1, 3, self_cols),
        square_grads[:, 2 * self_cols :],
        square_grads[:, self_cols : 2 * self_cols],
        late_rows[:, 3 * self_cols :].reshape(-1, 2, cross_cols),
        square_grads[:, :self_cols],
        ffn_rows[:, ffn_pad:].astype(WIDE).reshape(-1, 2, ffn_pad)[:, :, :ffn_cols],
        conv_sum.reshape(9, 2, ffn_pad)[:, :, :ffn_cols],
        ffn_rows[:, :ffn_cols].astype(WIDE),
    )


def solution(mesh):
    placed = (
        P("seq", None),
        P("seq", None),
        P("seq", None, None),
        P("seq", None, None),
        P(),
        P(),
        P(None, None, "tp"),
        P(None, "tp"),
        P(None, "tp"),
        P(None, None, "tp"),
        P(None, "tp"),
        P(None, None, "tp"),
        P(None, None, "tp"),
        P(None, "tp"),
    )
    return jax.shard_map(
        shards,
        mesh=mesh,
        in_specs=placed,
        out_specs=(
            P("seq", None),
            P("seq", None),
            P("seq", None, None),
            P("seq", None, "tp"),
            P("seq", "tp"),
            P("seq", "tp"),
            P("seq", None, "tp"),
            P("seq", "tp"),
            P("seq", None, "tp"),
            P(None, None, "tp"),
            P("seq", "tp"),
        ),
        check_vma=False,
    )
```

```python
import functools
import math

import jax
import jax.numpy as jnp
from jax import lax
from jax.experimental import pallas as pl
from jax.experimental.pallas import tpu as pltpu
from jax.sharding import PartitionSpec as P

HEAD = 32
CROSS_HEAD = 72
MAXW = 32
LANES = 128
GRANT = 56 * 1024 * 1024

EPSILON = 1e-06
MASKED_OUT = -1e30
LOW = jnp.bfloat16
WIDE = jnp.float32

FIRST, CUT, SIDE, WIDTH, OWN_LENGTH, OTHER_LENGTH, BLOCK_FIRST, SEQ_TOKENS, TP_PLACE, ROW_PLACE = range(10)


def swapped(block, axis, apart):
    count = lax.axis_size(axis)
    route = [(low, low ^ (1 << apart)) for low in range(count)]
    return lax.ppermute(block, axis, route)


def from_behind(block, step):
    count = lax.axis_size("tp")
    return lax.ppermute(block, "tp", [(k, (k + step) % count) for k in range(count)])


def exchanged(blocks):
    return lax.all_to_all(blocks, "tp", 0, 0, tiled=True)


def dot(left, right):
    return jnp.dot(left, right, preferred_element_type=WIDE)


def times_transposed(left, right):
    return lax.dot_general(left, right, (((1,), (1,)), ((), ())), preferred_element_type=WIDE)


def over_tokens(left, right):
    return lax.dot_general(left, right, (((0,), (0,)), ((), ())), preferred_element_type=WIDE)


def split(wide):
    high = wide.astype(LOW)
    return high, (wide - high.astype(WIDE)).astype(LOW)


def call(body, name, outs, arrays, *, grid=None, in_specs=None, out_specs=None, scratch=(), flops=0, table=None):
    shapes = tuple(jax.ShapeDtypeStruct(*out) for out in outs)
    size = sum(math.prod(a.shape) * a.dtype.itemsize for a in (*arrays, *shapes))
    whole = pl.BlockSpec(memory_space=pltpu.VMEM)
    return pl.pallas_call(
        body,
        out_shape=shapes,
        grid_spec=pltpu.PrefetchScalarGridSpec(
            num_scalar_prefetch=1,
            grid=grid or (1,),
            in_specs=in_specs or [whole] * len(arrays),
            out_specs=out_specs or [whole] * len(shapes),
            scratch_shapes=list(scratch),
        ),
        compiler_params=pltpu.CompilerParams(vmem_limit_bytes=GRANT),
        cost_estimate=pl.CostEstimate(flops=0, bytes_accessed=size // 100, transcendentals=0),
        name=name,
    )(table, *arrays)


def own_image(table, start, rows):
    place = start + lax.broadcasted_iota(jnp.int32, (rows, 1), 0)
    return (place >= table[CUT]).astype(jnp.int32) == table[SIDE]


def pick(own, own_rows, other_rows, row):
    return jnp.where(
        own, own_rows[row : row + 1, :].astype(WIDE), other_rows[row : row + 1, :].astype(WIDE)
    )


def inverse_size(wide):
    return lax.rsqrt(jnp.mean(wide * wide, axis=-1, keepdims=True) + EPSILON)


def both_sums(own, values):
    mine = jnp.sum(jnp.where(own, values, 0.0), axis=0, keepdims=True)
    return mine, jnp.sum(jnp.where(own, 0.0, values), axis=0, keepdims=True)


def same_head(rows, columns):
    row_head = lax.broadcasted_iota(jnp.int32, (rows, columns), 0) // HEAD
    return row_head == lax.broadcasted_iota(jnp.int32, (rows, columns), 1) // HEAD


def fold(square):
    size = square.shape[1]
    total = None
    for low in range(0, size, LANES):
        part = square[:, low : min(low + LANES, size)]
        if part.shape[1] < LANES:
            part = jnp.concatenate(
                [part, jnp.zeros((part.shape[0], LANES - part.shape[1]), part.dtype)], axis=1
            )
        total = part if total is None else total + part
    return total


def unfold(folded):
    size = folded.shape[0]
    parts = [folded[:, : min(LANES, size - low)] for low in range(0, size, LANES)]
    return jnp.where(same_head(size, size), jnp.concatenate(parts, axis=1), 0.0)


def packed(square, totals):
    keep = same_head(square.shape[0], square.shape[1])
    return fold(jnp.where(keep, square, 0.0)) + pltpu.roll(
        fold(jnp.where(keep, totals, 0.0)), HEAD, 1
    )


def unpacked(folded):
    return unfold(folded), unfold(pltpu.roll(folded, LANES - HEAD, 1))


def log_exp(wide):
    return jnp.maximum(wide, 0.0) + jnp.log1p(jnp.exp(-jnp.abs(wide)))


def logistic(wide):
    return 0.5 + 0.5 * jnp.tanh(0.5 * wide)


def self_project_body(table, x, mod_own, mod_other, weight, normed, raw, q, k, v, own_out, other_out, squares, totals):
    step = pl.program_id(0)
    rows, columns = q.shape
    own = own_image(table, table[FIRST] + step * rows, rows)
    wide = x[...].astype(WIDE)
    low = (
        wide * inverse_size(wide) * (1.0 + pick(own, mod_own, mod_other, 1))
        + pick(own, mod_own, mod_other, 0)
    ).astype(LOW)
    normed[...] = low
    out = times_transposed(low, weight[...])
    raw[...] = out[:, : 2 * columns]
    q[...] = log_exp(out[:, :columns]).astype(LOW)
    keys = log_exp(out[:, columns : 2 * columns]).astype(LOW)
    values = out[:, 2 * columns :].astype(LOW)
    k[...] = keys
    v[...] = values

    @pl.when(step == 0)
    def _():
        squares[...] = jnp.zeros_like(squares)
        totals[...] = jnp.zeros_like(totals)

    ones = jnp.ones((rows, columns), LOW)
    for image in range(2):
        zero = jnp.zeros_like(keys)
        masked = jnp.where(own, keys, zero) if image == 0 else jnp.where(own, zero, keys)
        squares[image] += over_tokens(masked, values)
        totals[image] += over_tokens(masked, ones)

    @pl.when(step == pl.num_programs(0) - 1)
    def _():
        own_out[...] = packed(squares[0], totals[0])
        other_out[...] = packed(squares[1], totals[1])


def self_project(table, x, mod_own, mod_other, weight, columns):
    tokens, width = x.shape
    rows = 128
    row = lambda c: pl.BlockSpec((rows, c), lambda i, t: (i, 0))
    fixed = lambda *s: pl.BlockSpec(s, lambda i, t: (0,) * len(s))
    return call(
        self_project_body,
        "self_project",
        [((tokens, width), LOW), ((tokens, 2 * columns), WIDE)]
        + [((tokens, columns), LOW)] * 3
        + [((columns, LANES), WIDE)] * 2,
        (x, mod_own, mod_other, weight),
        grid=(tokens // rows,),
        in_specs=[row(width), fixed(*mod_own.shape), fixed(*mod_own.shape), fixed(*weight.shape)],
        out_specs=[row(width), row(2 * columns)]
        + [row(columns)] * 3
        + [fixed(columns, LANES)] * 2,
        scratch=[pltpu.VMEM((2, columns, columns), WIDE)] * 2,
        flops=4 * tokens * width * 3 * columns,
        table=table,
    )


def keep_squares(kernels, key_totals, own_fold, other_fold):
    for image, folded in enumerate((own_fold, other_fold)):
        square, total = unpacked(folded[...])
        kernels[image, 0], kernels[image, 1] = split(square)
        key_totals[image, 0], key_totals[image, 1] = split(total)


def self_attend_body(table, q, own_fold, other_fold, attended, wide_out, denominator, kernels, key_totals):
    step = pl.program_id(0)
    rows = q.shape[0]

    @pl.when(step == 0)
    def _():
        keep_squares(kernels, key_totals, own_fold, other_fold)

    own = own_image(table, table[FIRST] + step * rows, rows)
    queries = q[...]

    def both(pair):
        own_part = dot(queries, pair[0, 0]) + dot(queries, pair[0, 1])
        return jnp.where(own, own_part, dot(queries, pair[1, 0]) + dot(queries, pair[1, 1]))

    under = both(key_totals) + 1.0
    out = both(kernels) / under
    attended[...] = out.astype(LOW)
    wide_out[...] = out
    denominator[...] = under


def self_attend(table, q, own_fold, other_fold):
    tokens, columns = q.shape
    rows = 128
    row = pl.BlockSpec((rows, columns), lambda i, t: (i, 0))
    fixed = pl.BlockSpec((columns, LANES), lambda i, t: (0, 0))
    return call(
        self_attend_body,
        "self_attend",
        [((tokens, columns), LOW), ((tokens, columns), WIDE), ((tokens, columns), WIDE)],
        (q, own_fold, other_fold),
        grid=(tokens // rows,),
        in_specs=[row, fixed, fixed],
        out_specs=[row, row, row],
        scratch=[pltpu.VMEM((2, 2, columns, columns), LOW)] * 2,
        flops=16 * tokens * columns * columns,
        table=table,
    )


def self_back_body(table, grad, q, wide_out, denominator, own_fold, other_fold, grad_q, own_out, other_out, kernels, key_totals, squares, totals):
    step = pl.program_id(0)
    rows, columns = q.shape

    @pl.when(step == 0)
    def _():
        keep_squares(kernels, key_totals, own_fold, other_fold)
        squares[...] = jnp.zeros_like(squares)
        totals[...] = jnp.zeros_like(totals)

    own = own_image(table, table[FIRST] + step * rows, rows)
    wide = grad[0].astype(WIDE)
    over = 1.0 / denominator[...]
    numer_high, numer_low = split(wide * over)
    ones = jnp.where(same_head(columns, columns), 1.0, 0.0).astype(LOW)
    high, low = split(wide * wide_out[...])
    denom = -(dot(high, ones) + dot(low, ones)) * over
    denom_high, denom_low = split(denom)

    def back(image):
        square, total = kernels[image, 0], key_totals[image, 0]
        through = (
            times_transposed(numer_high, square)
            + times_transposed(numer_low, square)
            + times_transposed(numer_high, kernels[image, 1])
        )
        totals_part = (
            times_transposed(denom_high, total)
            + times_transposed(denom_low, total)
            + times_transposed(denom_high, key_totals[image, 1])
        )
        return through + totals_part * (1.0 / HEAD)

    grad_q[...] = jnp.where(own, back(0), back(1))
    queries = q[...]
    zero = jnp.zeros_like(queries)
    for image in range(2):
        masked = jnp.where(own, queries, zero) if image == 0 else jnp.where(own, zero, queries)
        squares[image] += over_tokens(masked, numer_high) + over_tokens(masked, numer_low)
        totals[image] += over_tokens(masked, denom_high) + over_tokens(masked, denom_low)

    @pl.when(step == pl.num_programs(0) - 1)
    def _():
        own_out[...] = packed(squares[0], totals[0])
        other_out[...] = packed(squares[1], totals[1])


def self_back(table, grad, q, wide_out, denominator, own_fold, other_fold):
    count, rows, columns = grad.shape
    tokens = q.shape[0]
    row = pl.BlockSpec((rows, columns), lambda i, t: (i, 0))
    fixed = pl.BlockSpec((columns, LANES), lambda i, t: (0, 0))
    return call(
        self_back_body,
        "self_back",
        [((tokens, columns), WIDE)] + [((columns, LANES), WIDE)] * 2,
        (grad, q, wide_out, denominator, own_fold, other_fold),
        grid=(count,),
        in_specs=[pl.BlockSpec((1, rows, columns), lambda i, t: (i, 0, 0)), row, row, row, fixed, fixed],
        out_specs=[row, fixed, fixed],
        scratch=[pltpu.VMEM((2, 2, columns, columns), LOW)] * 2
        + [pltpu.VMEM((2, columns, columns), WIDE)] * 2,
        flops=48 * tokens * columns * columns,
        table=table,
    )


def self_project_back_body(table, grad_q, k, v, raw, own_fold, other_fold, grad_out, kernels, key_totals):
    step = pl.program_id(0)
    rows, columns = k.shape

    @pl.when(step == 0)
    def _():
        keep_squares(kernels, key_totals, own_fold, other_fold)

    own = own_image(table, table[FIRST] + step * rows, rows)
    keys, values = k[...], v[...]
    ones = jnp.ones((16, columns), LOW)

    def grad_k(image):
        total = times_transposed(ones, key_totals[image, 0]) + times_transposed(
            ones, key_totals[image, 1]
        )
        return (
            times_transposed(values, kernels[image, 0])
            + times_transposed(values, kernels[image, 1])
            + total[:1] * (1.0 / HEAD)
        )

    def grad_v(image):
        return dot(keys, kernels[image, 0]) + dot(keys, kernels[image, 1])

    given = raw[...]
    q_part = grad_q[...] * logistic(given[:, :columns])
    k_part = jnp.where(own, grad_k(0), grad_k(1)) * logistic(given[:, columns:])
    v_part = jnp.where(own, grad_v(0), grad_v(1))
    grad_out[...] = jnp.concatenate([q_part, k_part, v_part], axis=1).astype(LOW)


def self_project_back(table, grad_q, k, v, raw, own_fold, other_fold):
    tokens, columns = k.shape
    rows = 128
    row = lambda c: pl.BlockSpec((rows, c), lambda i, t: (i, 0))
    fixed = pl.BlockSpec((columns, LANES), lambda i, t: (0, 0))
    return call(
        self_project_back_body,
        "self_project_back",
        [((tokens, 3 * columns), LOW)],
        (grad_q, k, v, raw, own_fold, other_fold),
        grid=(tokens // rows,),
        in_specs=[row(columns), row(columns), row(columns), row(2 * columns), fixed, fixed],
        out_specs=[row(3 * columns)],
        scratch=[pltpu.VMEM((2, 2, columns, columns), LOW)] * 2,
        flops=16 * tokens * columns * columns,
        table=table,
    )[0]


def live_keys(table, own, keys):
    place = lax.broadcasted_iota(jnp.int32, (1, keys), 1)
    return place < jnp.where(own, table[OWN_LENGTH], table[OTHER_LENGTH])


def shard_of(first, rest, step, which):
    rows = first.shape[0]
    return first[...] if step == 0 else rest[step - 1, which * rows : (which + 1) * rows, :]


def middle_body(table, att, x, mod_own, mod_other, out_first, query_first, cross_first, *refs):
    pieces, (kv_own, kv_other) = refs[:8], refs[8:10]
    branch, after_low, queries_out, probs_out, text_out, after_cross, normed, rest = refs[10:]
    put_in_order(table, pieces, rest)
    count, rows, columns = att.shape
    keys = kv_own.shape[1]
    heads = columns // CROSS_HEAD
    own = own_image(table, table[BLOCK_FIRST], rows)
    y1 = jnp.zeros((rows, x.shape[1]), WIDE)
    for step in range(count):
        y1 += dot(att[turned(table, step, count)], shard_of(out_first, rest, step, 0))
    branch[...] = y1
    x1 = x[...].astype(WIDE) + pick(own, mod_own, mod_other, 2) * y1
    x1_low = x1.astype(LOW)
    after_low[...] = x1_low
    live = live_keys(table, own, keys)
    yc = jnp.zeros_like(x1)
    for step in range(count):
        queries = times_transposed(x1_low, shard_of(query_first, rest, step, 1)).astype(LOW)
        queries_out[step] = queries
        place = turned(table, step, count)
        mine, theirs = kv_own[place], kv_other[place]
        parts = []
        for head in range(heads):
            lanes = slice(head * CROSS_HEAD, (head + 1) * CROSS_HEAD)
            wide_lanes = slice(columns + head * CROSS_HEAD, columns + (head + 1) * CROSS_HEAD)
            q = queries[:, lanes]
            scores = jnp.where(
                own, times_transposed(q, mine[:, lanes]), times_transposed(q, theirs[:, lanes])
            ) * (1.0 / math.sqrt(CROSS_HEAD))
            scores = jnp.where(live, scores, MASKED_OUT)
            raised = jnp.exp(scores - jnp.max(scores, axis=-1, keepdims=True))
            probs = raised / jnp.sum(raised, axis=-1, keepdims=True)
            probs_out[step * heads + head] = probs
            low = probs.astype(LOW)
            parts.append(
                jnp.where(own, dot(low, mine[:, wide_lanes]), dot(low, theirs[:, wide_lanes]))
            )
        text = jnp.concatenate(parts, axis=1).astype(LOW)
        text_out[step] = text
        yc += dot(text, shard_of(cross_first, rest, step, 2))
    x2 = x1 + yc
    after_cross[...] = x2
    normed[...] = (
        x2 * inverse_size(x2) * (1.0 + pick(own, mod_own, mod_other, 4))
        + pick(own, mod_own, mod_other, 3)
    ).astype(LOW)


def middle_back_body(table, grad_own, grad_1, grad_2, grad_3, x2_in, upstream, branch, mod_own, mod_other, out_first, query_first, cross_first, rest, kv_own, kv_other, probs_in, queries_in, cross_grad, query_grad, attn_grad, attended_grad, after_grad, sums, kv_own_grad, kv_other_grad):
    count, rows, columns = queries_in.shape
    keys = kv_own.shape[1]
    heads = columns // CROSS_HEAD
    scale = 1.0 / math.sqrt(CROSS_HEAD)
    own = own_image(table, table[BLOCK_FIRST], rows)
    grad = with_own(grad_own, grad_1, grad_2, grad_3)
    x2 = x2_in[...]
    inverse = inverse_size(x2)
    xh = x2 * inverse
    sums[0:1], sums[1:2] = both_sums(own, grad)
    sums[2:3], sums[3:4] = both_sums(own, grad * xh)
    e = grad * (1.0 + pick(own, mod_own, mod_other, 4))
    dx2 = upstream[...].astype(WIDE) + inverse * (
        e - xh * jnp.mean(e * xh, axis=-1, keepdims=True)
    )
    dyc = dx2.astype(LOW)
    cross_grad[...] = dyc
    dx1 = dx2
    for step in range(count):
        doc = times_transposed(dyc, shard_of(cross_first, rest, step, 2)).astype(LOW)
        place = turned(table, step, count)
        mine, theirs = kv_own[place], kv_other[place]
        queries = queries_in[step]
        query_parts = []
        key_parts = ([], [])
        value_parts = ([], [])
        for head in range(heads):
            lanes = slice(head * CROSS_HEAD, (head + 1) * CROSS_HEAD)
            wide_lanes = slice(columns + head * CROSS_HEAD, columns + (head + 1) * CROSS_HEAD)
            do, q = doc[:, lanes], queries[:, lanes]
            probs = probs_in[step * heads + head]
            dp = jnp.where(
                own,
                times_transposed(do, mine[:, wide_lanes]),
                times_transposed(do, theirs[:, wide_lanes]),
            )
            ds = (probs * (dp - jnp.sum(probs * dp, axis=-1, keepdims=True))).astype(LOW)
            low = probs.astype(LOW)
            zero = jnp.zeros_like(ds)
            query_parts.append(
                jnp.where(own, dot(ds, mine[:, lanes]), dot(ds, theirs[:, lanes])) * scale
            )
            for image in range(2):
                mask = (lambda a: jnp.where(own, a, zero)) if image == 0 else (
                    lambda a: jnp.where(own, zero, a)
                )
                key_parts[image].append(over_tokens(mask(ds), q) * scale)
                value_parts[image].append(over_tokens(mask(low), do))
        dqc = jnp.concatenate(query_parts, axis=1).astype(LOW)
        query_grad[step] = dqc
        kv_own_grad[place] = jnp.concatenate(key_parts[0] + value_parts[0], axis=1).astype(LOW)
        kv_other_grad[place] = jnp.concatenate(key_parts[1] + value_parts[1], axis=1).astype(LOW)
        dx1 = dx1 + dot(dqc, shard_of(query_first, rest, step, 1))
    after_grad[...] = dx1
    sums[4:5], sums[5:6] = both_sums(own, dx1 * branch[...])
    sums[6:8] = jnp.zeros((2, sums.shape[1]), WIDE)
    dy1 = (dx1 * pick(own, mod_own, mod_other, 2)).astype(LOW)
    attn_grad[...] = dy1
    for step in range(count):
        attended_grad[turned(table, step, count)] = times_transposed(
            dy1, shard_of(out_first, rest, step, 0)
        ).astype(LOW)


def first_norm_back_body(table, grad_own, grad_1, grad_2, grad_3, after_grad, x, mod_own, mod_other, input_grad, sums):
    rows = x.shape[0]
    own = own_image(table, table[BLOCK_FIRST], rows)
    grad = with_own(grad_own, grad_1, grad_2, grad_3)
    wide = x[...].astype(WIDE)
    inverse = inverse_size(wide)
    xh = wide * inverse
    sums[0:1], sums[1:2] = both_sums(own, grad)
    sums[2:3], sums[3:4] = both_sums(own, grad * xh)
    sums[4:8] = jnp.zeros((4, sums.shape[1]), WIDE)
    e = grad * (1.0 + pick(own, mod_own, mod_other, 1))
    input_grad[...] = (
        after_grad[...] + inverse * (e - xh * jnp.mean(e * xh, axis=-1, keepdims=True))
    ).astype(LOW)


def output_body(table, branches, x2, upstream, mod_own, mod_other, output, sums):
    rows = x2.shape[0]
    own = own_image(table, table[BLOCK_FIRST], rows)
    branch = total(branches)
    sums[0:1], sums[1:2] = both_sums(own, upstream[...].astype(WIDE) * branch)
    sums[2:8] = jnp.zeros((6, sums.shape[1]), WIDE)
    output[...] = (x2[...] + pick(own, mod_own, mod_other, 5) * branch).astype(LOW)


def up_body(table, *refs):
    blocks, weight, (wide_out, low_out, ordered) = refs[:-4], refs[-4], refs[-3:]
    rows = blocks[0].shape[0]

    @pl.when(pl.program_id(0) == 0)
    def _():
        for step, block in enumerate(blocks):
            low = turned(table, step, len(blocks)) * rows
            ordered[pl.ds(pl.multiple_of(low, 16), rows), :] = block[...]

    up = times_transposed(ordered[...], weight[...])
    wide_out[...] = up
    low_out[...] = (up * logistic(up)).astype(LOW)


def up_project(table, blocks, weight):
    rows, width = blocks[0].shape
    tokens = len(blocks) * rows
    columns = 3 * LANES
    whole = lambda *shape: pl.BlockSpec(shape, lambda i, t: (0, 0))
    column = pl.BlockSpec((tokens, columns), lambda i, t: (0, i))
    return call(
        up_body,
        "up_project",
        [((tokens, weight.shape[0]), WIDE), ((tokens, weight.shape[0]), LOW), ((tokens, width), LOW)],
        (*blocks, weight),
        grid=(weight.shape[0] // columns,),
        in_specs=[whole(rows, width)] * len(blocks)
        + [pl.BlockSpec((columns, width), lambda i, t: (i, 0))],
        out_specs=[column, column, whole(tokens, width)],
        table=table,
    )


def fill(padded, block, rim):
    tokens = block.shape[0]
    edge = rim[...].astype(WIDE)
    padded[0:MAXW, :] = edge
    padded[MAXW : MAXW + tokens, :] = block.astype(WIDE)
    padded[MAXW + tokens : 2 * MAXW + tokens, :] = edge


def fill_masks(table, masks):
    tokens = masks.shape[1]
    place = table[FIRST] + lax.broadcasted_iota(jnp.int32, (tokens, LANES), 0)
    width = table[WIDTH]
    cut = table[CUT]
    late = place >= cut
    start = jnp.where(late, cut, 0)
    end = jnp.where(late, table[SEQ_TOKENS], cut)
    column = lax.bitwise_and(place, width - 1)
    one, none = jnp.ones((tokens, LANES), WIDE), jnp.zeros((tokens, LANES), WIDE)
    masks[0] = jnp.where(place - width >= start, one, none)
    masks[1] = jnp.where(place + width < end, one, none)
    masks[2] = jnp.where(column > 0, one, none)
    masks[3] = jnp.where(column < width - 1, one, none)


CHUNK = 64


def three_rows(table, padded, masks, low):
    width = table[WIDTH]
    above = padded[pl.ds(pl.multiple_of(MAXW + low - width, 16), CHUNK), :]
    below = padded[pl.ds(pl.multiple_of(MAXW + low + width, 16), CHUNK), :]
    own = padded[pl.ds(pl.multiple_of(MAXW + low, 16), CHUNK), :]
    rows = pl.ds(pl.multiple_of(low, 16), CHUNK)
    return above * masks[0, rows, :], own, below * masks[1, rows, :]


def nine_taps(rows, taps, left_mask, right_mask):
    mixed = [sum(rows[a] * taps[a][b] for a in range(3)) for b in range(3)]
    return (
        mixed[1]
        + left_mask * pltpu.roll(mixed[0], 1, 0)
        + right_mask * pltpu.roll(mixed[2], CHUNK - 1, 0)
    )


def taps_of(taps, flip):
    read = lambda a, b: taps[3 * a + b : 3 * a + b + 1, :]
    return [[read(2 - a, 2 - b) if flip else read(a, b) for b in range(3)] for a in range(3)]


def mix_body(table, value, gate, value_rim, gate_rim, value_taps, gate_taps, grad_hidden, hidden, grads, value_pad, gate_pad, masks):
    @pl.when(pl.program_id(0) == 0)
    def _():
        fill_masks(table, masks)

    fill(value_pad, value[...], value_rim)
    fill(gate_pad, gate[...], gate_rim)
    value_weights, gate_weights = taps_of(value_taps, False), taps_of(gate_taps, False)

    @pl.loop(0, value.shape[0] // CHUNK)
    def _(index):
        low = index * CHUNK
        rows = pl.ds(pl.multiple_of(low, CHUNK), CHUNK)
        left, right = masks[2, rows, :], masks[3, rows, :]
        mv = nine_taps(three_rows(table, value_pad, masks, low), value_weights, left, right)
        mg = nine_taps(three_rows(table, gate_pad, masks, low), gate_weights, left, right)
        sigma = logistic(mg)
        gated = mg * sigma
        hidden[rows, :] = (mv * gated).astype(LOW)
        dh = grad_hidden[rows, :]
        grads[0, rows, :] = (dh * gated).astype(LOW)
        grads[1, rows, :] = (dh * mv * (sigma * (1.0 + mg * (1.0 - sigma)))).astype(LOW)


def mix(table, activated, rim, taps, grad_hidden):
    tokens, wide = activated.shape
    columns = wide // 2
    tiles = columns // LANES
    block = lambda r, shift: pl.BlockSpec((r, LANES), lambda i, t: (0, i + shift))
    pad = pltpu.VMEM((tokens + 2 * MAXW, LANES), WIDE)
    return call(
        mix_body,
        "mix",
        [((tokens, columns), LOW), ((2, tokens, columns), LOW)],
        (activated, activated, rim, rim, taps, taps, grad_hidden),
        grid=(tiles,),
        in_specs=[
            block(tokens, 0),
            block(tokens, tiles),
            block(MAXW, 0),
            block(MAXW, tiles),
            block(taps.shape[0], 0),
            block(taps.shape[0], tiles),
            block(tokens, 0),
        ],
        out_specs=[
            block(tokens, 0),
            pl.BlockSpec((2, tokens, LANES), lambda i, t: (0, 0, i)),
        ],
        scratch=[pad, pad, pltpu.VMEM((4, tokens, LANES), WIDE)],
        flops=6000 * tokens * columns // 2,
        table=table,
    )


def mix_back_body(table, grads, grads_rim, activated, rim, taps, up, grad_up, tap_grads, grad_pad, act_pad, masks):
    @pl.when(pl.program_id(0) == 0)
    def _():
        fill_masks(table, masks)

    fill(grad_pad, grads[0], grads_rim.at[0])
    fill(act_pad, activated[...], rim)
    weights = taps_of(taps, True)

    def step(index, sums):
        low = index * CHUNK
        rows = pl.ds(pl.multiple_of(low, CHUNK), CHUNK)
        left, right = masks[2, rows, :], masks[3, rows, :]
        mine = three_rows(table, grad_pad, masks, low)
        dact = nine_taps(mine, weights, left, right)
        given = up[rows, :]
        sigma = logistic(given)
        grad_up[rows, :] = (dact * (sigma * (1.0 + given * (1.0 - sigma)))).astype(LOW)
        acts = three_rows(table, act_pad, masks, low)
        turned = (
            right * pltpu.roll(mine[1], CHUNK - 1, 0),
            mine[1],
            left * pltpu.roll(mine[1], 1, 0),
        )
        return tuple(
            sums[3 * a + b]
            + jnp.sum((acts[a] * turned[b]).reshape(CHUNK // 8, 8, LANES), axis=0)
            for a in range(3)
            for b in range(3)
        )

    zero = jnp.zeros((8, LANES), WIDE)
    sums = lax.fori_loop(0, activated.shape[0] // CHUNK, step, (zero,) * 9)
    for tap in range(9):
        tap_grads[tap : tap + 1, :] = jnp.sum(sums[tap], axis=0, keepdims=True)
    tap_grads[9:16, :] = jnp.zeros((7, LANES), WIDE)


def mix_back(table, grads, grads_rim, activated, rim, taps, up):
    tokens, wide = activated.shape
    columns = wide // 2
    tiles = columns // LANES
    block = lambda r: pl.BlockSpec((r, LANES), lambda i, t: (0, i))
    half = lambda r: pl.BlockSpec(
        (1, r, LANES), lambda i, t: (lax.div(i, tiles), 0, lax.rem(i, tiles))
    )
    pad = pltpu.VMEM((tokens + 2 * MAXW, LANES), WIDE)
    return call(
        mix_back_body,
        "mix_back",
        [((tokens, wide), LOW), ((16, wide), WIDE)],
        (grads, grads_rim, activated, rim, taps, up),
        grid=(2 * tiles,),
        in_specs=[half(tokens), half(MAXW), block(tokens), block(MAXW), block(taps.shape[0]), block(tokens)],
        out_specs=[block(tokens), block(16)],
        scratch=[pad, pad, pltpu.VMEM((4, tokens, LANES), WIDE)],
        flops=6000 * tokens * columns,
        table=table,
    )


def eighth_body(table, *refs):
    weights, out, joined = refs[:-2], refs[-2], refs[-1]
    low = 0
    for weight in weights:
        joined[low : low + weight.shape[0], :] = weight[...]
        low += weight.shape[0]
    rows = out.shape[0]
    out[...] = joined[pl.ds(pl.multiple_of(table[0] * rows, 16), rows), :]


def put_in_order(table, pieces, out):
    steps, rows = pieces[0].shape[0], pieces[0].shape[1]
    for place, piece in enumerate(pieces):
        block = lax.bitwise_xor(table[ROW_PLACE], place)
        for step in range(steps):
            out[step, pl.ds(pl.multiple_of(block * rows, 16), rows), :] = piece[step]


def after(value, *others):
    return lax.optimization_barrier((value, others))[0]


def fetch_eighths(weights):
    columns = weights[0].shape[1]
    rows = -(-sum(weight.shape[0] for weight in weights) // LANES) * 16
    eighth = call(
        eighth_body,
        "eighth",
        [((rows, columns), weights[0].dtype)],
        weights,
        scratch=[pltpu.VMEM((8 * rows, columns), weights[0].dtype)],
        table=(lax.axis_index("seq") % 8).reshape(1).astype(jnp.int32),
    )[0]
    return jnp.stack([from_behind(eighth, step) for step in range(1, lax.axis_size("tp"))])


def share_eighths(fetched, ready):
    count = lax.axis_size("seq")
    far = lambda flip: lax.ppermute(fetched, "seq", [(k, k ^ flip) for k in range(count)])
    pieces = []
    for piece in [fetched] + after([far(2), far(4), far(6)], *ready):
        pieces += [piece, swapped(piece, "seq", 0)]
    return pieces


def token_block(values, place):
    count = lax.axis_size("tp")
    size = values.shape[0] // count
    return lax.dynamic_slice_in_dim(values, (place % count) * size, size, 0)


def own_rows(values):
    rows = values.shape[0] // lax.axis_size("tp")
    return pl.BlockSpec((rows, values.shape[1]), lambda i, t: (t[TP_PLACE], 0))


def placed_blocks(blocks):
    count = len(blocks)
    place = lax.axis_index("tp")
    result = jnp.zeros((count,) + blocks[0].shape, blocks[0].dtype)
    for step in range(count):
        result = lax.dynamic_update_index_in_dim(result, blocks[step], (place - step) % count, 0)
    return result.reshape((count * blocks[0].shape[0],) + blocks[0].shape[1:])


def all_blocks(block):
    return [block] + [from_behind(block, step) for step in range(1, lax.axis_size("tp"))]


def product(left, right):
    count = lax.axis_size("tp")
    return dot(left, right).astype(LOW).reshape(count, left.shape[0] // count, right.shape[1])


def spread(blocks):
    count = lax.axis_size("tp")
    place = lax.axis_index("tp")
    return [
        from_behind(
            lax.dynamic_index_in_dim(blocks, (place + step) % count, 0, keepdims=False), step
        )
        for step in range(1, count)
    ]


def own_block(blocks):
    return pl.BlockSpec((1,) + blocks.shape[1:], lambda i, t: (t[TP_PLACE], 0, 0))


def with_own(own, *others):
    result = own[0].astype(WIDE)
    for other in others:
        result += other[...].astype(WIDE)
    return result


def total(parts):
    result = parts[0].astype(WIDE)
    for place in range(1, parts.shape[0]):
        result += parts[place].astype(WIDE)
    return result


def turned(table, step, count):
    return lax.rem(table[TP_PLACE] + count - step, count)


def same_everywhere(block):
    count = lax.axis_size("tp")
    flipped = lambda flip: lax.ppermute(block, "tp", [(k, k ^ flip) for k in range(count)])
    return (block + flipped(1)) + (flipped(2) + flipped(3))


def sum_rows(grad):
    return lax.optimization_barrier(
        lax.psum_scatter(grad.astype(LOW), "seq", scatter_dimension=0, tiled=True)
    )


def square_body(table, dyc, text, x1, dqc, dy1, att, kv_mine, kv_theirs, out, kv_out):
    kv_out[...] = (kv_mine[...].astype(WIDE) + kv_theirs[...].astype(WIDE)).astype(LOW)
    parts = [
        over_tokens(left[...], right[0]) for left, right in ((dyc, text), (x1, dqc), (dy1, att))
    ]
    rest = out.shape[1] - sum(part.shape[1] for part in parts)
    if rest:
        parts.append(jnp.zeros((out.shape[0], rest), WIDE))
    out[...] = jnp.concatenate(parts, axis=1).astype(LOW)


def square_parts(table, lefts, rights, kv_mine, kv_theirs):
    rows, width = lefts[0].shape
    count, _, columns = rights[0].shape
    block = -(-3 * columns // LANES) * LANES
    whole = pl.BlockSpec((rows, width), lambda i, t: (0, 0))
    one = pl.BlockSpec((1, rows, columns), lambda i, t: (turned(t, i, count), 0, 0))
    still = pl.BlockSpec((1, rows, columns), lambda i, t: (i, 0, 0))
    kv = pl.BlockSpec((1,) + kv_mine.shape[1:], lambda i, t: (i, 0, 0))
    return call(
        square_body,
        "square_parts",
        [((width, count * block), LOW), (kv_mine.shape, LOW)],
        [array for pair in zip(lefts, rights) for array in pair] + [kv_mine, kv_theirs],
        grid=(count,),
        in_specs=[whole, one, whole, one, whole, still, kv, kv],
        out_specs=[pl.BlockSpec((width, block), lambda i, t: (0, i)), kv],
        table=table,
    )


def ffn_body(table, grad_ffn, hidden, normed, grad_up, out):
    step = pl.program_id(0)

    @pl.when(step == 0)
    def _():
        out[...] = over_tokens(grad_ffn[...], hidden[...]).astype(LOW)

    @pl.when(step > 0)
    def _():
        out[...] = over_tokens(normed[...], grad_up[...]).astype(LOW)


def ffn_parts_of(table, grad_ffn, hidden, normed, grad_up):
    tokens, width = normed.shape
    columns = hidden.shape[1]
    whole = pl.BlockSpec((tokens, width), lambda i, t: (0, 0))
    return call(
        ffn_body,
        "ffn_parts",
        [((width, 3 * columns), LOW)],
        (grad_ffn, hidden, normed, grad_up),
        grid=(3,),
        in_specs=[
            whole,
            pl.BlockSpec((tokens, columns), lambda i, t: (0, 0)),
            whole,
            pl.BlockSpec((tokens, columns), lambda i, t: (0, jnp.maximum(i - 1, 0))),
        ],
        out_specs=[pl.BlockSpec((width, columns), lambda i, t: (0, i))],
        table=table,
    )[0]


def late_body(table, normed, grad_projected, text, kv_grads, out):
    first = over_tokens(normed[...], grad_projected[...]).astype(LOW)
    second = over_tokens(text[...], total(kv_grads).astype(LOW)).astype(LOW)
    out[...] = jnp.concatenate([first, second], axis=1)


def shards(
    hidden_in,
    cotangent,
    modulation,
    text_states,
    image_shapes,
    text_lengths,
    qkv_weight,
    attn_out_weight,
    cross_q_weight,
    cross_kv_weight,
    cross_out_weight,
    up_weight,
    conv_weight,
    down_weight,
):
    tokens_here, width = hidden_in.shape
    context = text_states.shape[1]
    keys = -(-context // 16) * 16
    self_cols = qkv_weight.shape[2]
    cross_cols = cross_q_weight.shape[1]
    ffn_cols = up_weight.shape[2]
    ffn_pad = -(-ffn_cols // LANES) * LANES
    count = lax.axis_size("tp")
    tp_index = lax.axis_index("tp")
    block_size = tokens_here // count
    seq_index = lax.axis_index("seq")
    side = seq_index % 2
    first_half = side == 0
    pair = seq_index - side
    pair_shapes = lax.dynamic_slice_in_dim(image_shapes, pair, 2, 0)
    row_width = pair_shapes[0, 1]
    lengths = lax.dynamic_slice_in_dim(text_lengths, pair, 2, 0)
    first_place = side * tokens_here
    table = jnp.stack(
        [
            first_place,
            pair_shapes[0, 0] * row_width,
            side,
            row_width,
            jnp.where(first_half, lengths[0], lengths[1]),
            jnp.where(first_half, lengths[1], lengths[0]),
            first_place + tp_index * block_size,
            jnp.int32(2 * tokens_here),
            tp_index,
            seq_index % 8,
        ]
    ).astype(jnp.int32)

    mod_own = modulation[0]
    mod_other = swapped(mod_own, "seq", 0).astype(WIDE)
    mod_own = mod_own.astype(WIDE)
    weights = [attn_out_weight.T, cross_q_weight.T, cross_out_weight.T]
    fetched = fetch_eighths(weights)
    qkv_flat = qkv_weight.transpose(1, 2, 0).reshape(3 * self_cols, width)
    text_rows = jnp.pad(text_states[0], ((0, keys - context), (0, 0)))
    kv_here = times_transposed(
        text_rows, cross_kv_weight.transpose(1, 2, 0).reshape(2 * cross_cols, width)
    ).astype(LOW)
    kv_sent_first = jnp.broadcast_to(kv_here[None], (count,) + kv_here.shape)
    normed_low, raw, q, k, v, part_own, part_other = self_project(
        table, after(hidden_in, kv_sent_first), mod_own, mod_other, qkv_flat, self_cols
    )
    theirs = swapped(jnp.stack([part_own, part_other]), "seq", 0)
    fetched = after(fetched, q)
    kernel_own, kernel_other = part_own + theirs[1], part_other + theirs[0]
    attended, attended_wide, denominator = self_attend(
        table, after(q, kv_here), kernel_own, kernel_other
    )

    whole = pl.BlockSpec(memory_space=pltpu.VMEM)
    x_rows, upstream_rows = own_rows(hidden_in), own_rows(cotangent)
    up_flat = jnp.pad(
        after(up_weight.transpose(1, 2, 0), attended), ((0, 0), (0, ffn_pad - ffn_cols), (0, 0))
    ).reshape(2 * ffn_pad, width)
    down_flat = jnp.pad(after(down_weight.T, attended), ((0, ffn_pad - ffn_cols), (0, 0)))
    taps = (
        jnp.pad(conv_weight, ((0, 7), (0, 0), (0, ffn_pad - ffn_cols)))
        .reshape(16, 2 * ffn_pad)
        .astype(WIDE)
    )
    gate_rows = jnp.where(
        (first_place + jnp.arange(tokens_here, dtype=jnp.int32) >= table[CUT])[:, None] == (side == 1),
        mod_own[5:6],
        mod_other[5:6],
    )
    grad_ffn = (cotangent.astype(WIDE) * gate_rows).astype(LOW)
    grad_hidden = times_transposed(grad_ffn, down_flat)
    ready = (up_flat, down_flat, taps, grad_hidden)
    split_tokens = lambda values: values.reshape(count, block_size, values.shape[1])
    kv_own = exchanged(kv_sent_first)
    attended_blocks = exchanged(after(split_tokens(attended), kv_own))
    kv_own = after(kv_own, *ready)
    kv_other = swapped(kv_own, "seq", 0)
    pieces = share_eighths(fetched, (*ready, attended_blocks))
    all_heads = count * cross_cols // CROSS_HEAD
    branch, after_low, queries, probs, text_low, after_cross, normed_two, rest = call(
        middle_body,
        "middle",
        [
            ((block_size, width), WIDE),
            ((block_size, width), LOW),
            ((count, block_size, cross_cols), LOW),
            ((all_heads, block_size, keys), WIDE),
            ((count, block_size, cross_cols), LOW),
            ((block_size, width), WIDE),
            ((block_size, width), LOW),
            ((count - 1, 8 * fetched.shape[1], width), LOW),
        ],
        (attended_blocks, hidden_in, mod_own, mod_other, *weights, *pieces, kv_own, kv_other),
        in_specs=[whole, x_rows] + [whole] * 15,
        flops=60 * block_size * width * width,
        table=table,
    )

    up_wide, activated, normed_two_low = up_project(table, all_blocks(normed_two), up_flat)
    rim = swapped(jnp.where(first_half, activated[-MAXW:], activated[:MAXW]), "seq", 0)
    hidden, grads = mix(table, activated, rim, taps, grad_hidden)
    grads_rim = swapped(jnp.where(first_half, grads[:, -MAXW:], grads[:, :MAXW]), "seq", 0)
    branch_sent = product(hidden, down_flat)
    grad_up, tap_part = mix_back(
        table, grads, grads_rim, activated, rim, taps, after(up_wide, branch_sent)
    )
    branches = exchanged(branch_sent)
    norm_two_sent = product(grad_up, up_flat)
    grad_norm_two = spread(norm_two_sent)
    output_block, output_sums = call(
        output_body,
        "output",
        [((block_size, width), LOW), ((8, width), WIDE)],
        (branches, after_cross, cotangent, mod_own, mod_other),
        in_specs=[whole, whole, upstream_rows, whole, whole],
        table=table,
    )
    ffn_parts = ffn_parts_of(
        table, grad_ffn, after(hidden, norm_two_sent, output_block), normed_two_low, grad_up
    )
    ffn_rows = sum_rows(after(ffn_parts, grad_norm_two))
    output_blocks = all_blocks(after(output_block, grad_norm_two))

    (
        cross_grad,
        query_grad,
        attn_grad,
        attended_grad,
        after_grad,
        middle_sums,
        kv_own_grad,
        kv_other_grad,
    ) = call(
        middle_back_body,
        "middle_back",
        [
            ((block_size, width), LOW),
            ((count, block_size, cross_cols), LOW),
            ((block_size, width), LOW),
            ((count, block_size, self_cols), LOW),
            ((block_size, width), WIDE),
            ((8, width), WIDE),
            ((count, keys, 2 * cross_cols), LOW),
            ((count, keys, 2 * cross_cols), LOW),
        ],
        (
            after(norm_two_sent, ffn_parts, output_block),
            *grad_norm_two,
            after_cross,
            cotangent,
            branch,
            mod_own,
            mod_other,
            *weights,
            rest,
            kv_own,
            kv_other,
            probs,
            queries,
        ),
        in_specs=[own_block(norm_two_sent)] + [whole] * 4 + [upstream_rows] + [whole] * 11,
        flops=120 * block_size * width * width,
        table=table,
    )

    grad_blocks = exchanged(after(attended_grad, output_blocks))
    kv_theirs = swapped(after(kv_other_grad, output_blocks), "seq", 0)
    squares, kv_sent = square_parts(
        table,
        (cross_grad, after_low, attn_grad),
        (text_low, query_grad, after(attended_blocks, attended_grad)),
        kv_own_grad,
        kv_theirs,
    )
    square_rows = sum_rows(after(squares, grad_blocks))
    kv_sent = after(kv_sent, grad_blocks)
    kv_parts = exchanged(kv_sent)
    grad_blocks = after(grad_blocks, squares, kv_sent, ffn_rows)
    grad_q, back_own, back_other = self_back(
        table, grad_blocks, q, attended_wide, denominator, kernel_own, kernel_other
    )
    back_theirs = swapped(jnp.stack([back_own, back_other]), "seq", 0)
    grad_projected = self_project_back(
        table,
        grad_q,
        k,
        v,
        raw,
        back_own + back_theirs[1],
        back_other + back_theirs[0],
    )
    normed_sent = product(grad_projected, qkv_flat)
    grad_normed = spread(normed_sent)
    late_parts = call(
        late_body,
        "late_parts",
        [((width, 3 * self_cols + 2 * cross_cols), LOW)],
        (normed_low, after(grad_projected, normed_sent), text_rows, kv_parts),
        table=table,
    )[0]
    late_rows = sum_rows(after(late_parts, square_rows, grad_normed))
    conv_sum = after(tap_part[:9], normed_sent)
    for place in range(lax.axis_size("seq").bit_length() - 1):
        conv_sum = conv_sum + swapped(conv_sum, "seq", place)
    square_sent = square_rows.reshape(square_rows.shape[0], count, -1).transpose(1, 0, 2)
    input_block, first_sums = call(
        first_norm_back_body,
        "first_norm_back",
        [((block_size, width), LOW), ((8, width), WIDE)],
        (
            after(normed_sent, late_parts, square_sent),
            *grad_normed,
            after_grad,
            hidden_in,
            mod_own,
            mod_other,
        ),
        in_specs=[own_block(normed_sent)] + [whole] * 4 + [x_rows, whole, whole],
        table=table,
    )
    square_parts_here = exchanged(square_sent)
    square_grads = total(square_parts_here)[:, : 3 * self_cols]
    pairs = jnp.concatenate([first_sums[:4], middle_sums[4:6], middle_sums[:4], output_sums[:2]])
    pairs = pairs.reshape(6, 2, width)
    pairs = pairs[:, 0] + swapped(pairs[:, 1], "seq", 0)
    input_block = after(input_block, square_parts_here)
    late_rows = late_rows.astype(WIDE)
    qkv_grad = late_rows[:, : 3 * self_cols].reshape(-1, 3, self_cols)
    ckv_grad = late_rows[:, 3 * self_cols :].reshape(-1, 2, cross_cols)
    output = placed_blocks(output_blocks)
    input_blocks = after(all_blocks(input_block), qkv_grad, ckv_grad, square_grads, output)
    modulation_grad = same_everywhere(after(pairs, input_blocks))
    input_grad = placed_blocks(input_blocks).astype(WIDE)

    return (
        output,
        input_grad,
        modulation_grad[None],
        qkv_grad,
        square_grads[:, 2 * self_cols :],
        square_grads[:, self_cols : 2 * self_cols],
        ckv_grad,
        square_grads[:, :self_cols],
        ffn_rows[:, ffn_pad:].astype(WIDE).reshape(-1, 2, ffn_pad)[:, :, :ffn_cols],
        conv_sum.reshape(9, 2, ffn_pad)[:, :, :ffn_cols],
        ffn_rows[:, :ffn_cols].astype(WIDE),
    )


def solution(mesh):
    placed = (
        P("seq", None),
        P("seq", None),
        P("seq", None, None),
        P("seq", None, None),
        P(),
        P(),
        P(None, None, "tp"),
        P(None, "tp"),
        P(None, "tp"),
        P(None, None, "tp"),
        P(None, "tp"),
        P(None, None, "tp"),
        P(None, None, "tp"),
        P(None, "tp"),
    )
    return jax.shard_map(
        shards,
        mesh=mesh,
        in_specs=placed,
        out_specs=(
            P("seq", None),
            P("seq", None),
            P("seq", None, None),
            P("seq", None, "tp"),
            P("seq", "tp"),
            P("seq", "tp"),
            P("seq", None, "tp"),
            P("seq", "tp"),
            P("seq", None, "tp"),
            P(None, None, "tp"),
            P("seq", "tp"),
        ),
        check_vma=False,
    )
```

```python
import functools
import math

import jax
import jax.numpy as jnp
from jax import lax
from jax.experimental import pallas as pl
from jax.experimental.pallas import tpu as pltpu
from jax.sharding import PartitionSpec as P

HEAD = 32
CROSS_HEAD = 72
MAXW = 32
LANES = 128
GRANT = 56 * 1024 * 1024

EPSILON = 1e-06
MASKED_OUT = -1e30
LOW = jnp.bfloat16
WIDE = jnp.float32

FIRST, CUT, SIDE, WIDTH, OWN_LENGTH, OTHER_LENGTH, BLOCK_FIRST, SEQ_TOKENS, TP_PLACE, ROW_PLACE = range(10)


def swapped(block, axis, apart):
    count = lax.axis_size(axis)
    route = [(low, low ^ (1 << apart)) for low in range(count)]
    return lax.ppermute(block, axis, route)


def from_behind(block, step):
    count = lax.axis_size("tp")
    return lax.ppermute(block, "tp", [(k, (k + step) % count) for k in range(count)])


def exchanged(blocks):
    return lax.all_to_all(blocks, "tp", 0, 0, tiled=True)


def dot(left, right):
    return jnp.dot(left, right, preferred_element_type=WIDE)


def times_transposed(left, right):
    return lax.dot_general(left, right, (((1,), (1,)), ((), ())), preferred_element_type=WIDE)


def over_tokens(left, right):
    return lax.dot_general(left, right, (((0,), (0,)), ((), ())), preferred_element_type=WIDE)


def split(wide):
    high = wide.astype(LOW)
    return high, (wide - high.astype(WIDE)).astype(LOW)


def call(body, name, outs, arrays, *, grid=None, in_specs=None, out_specs=None, scratch=(), flops=0, table=None):
    shapes = tuple(jax.ShapeDtypeStruct(*out) for out in outs)
    size = sum(math.prod(a.shape) * a.dtype.itemsize for a in (*arrays, *shapes))
    whole = pl.BlockSpec(memory_space=pltpu.VMEM)
    return pl.pallas_call(
        body,
        out_shape=shapes,
        grid_spec=pltpu.PrefetchScalarGridSpec(
            num_scalar_prefetch=1,
            grid=grid or (1,),
            in_specs=in_specs or [whole] * len(arrays),
            out_specs=out_specs or [whole] * len(shapes),
            scratch_shapes=list(scratch),
        ),
        compiler_params=pltpu.CompilerParams(vmem_limit_bytes=GRANT),
        cost_estimate=pl.CostEstimate(flops=0, bytes_accessed=size // 100, transcendentals=0),
        name=name,
    )(table, *arrays)


def own_image(table, start, rows):
    place = start + lax.broadcasted_iota(jnp.int32, (rows, 1), 0)
    return (place >= table[CUT]).astype(jnp.int32) == table[SIDE]


def pick(own, own_rows, other_rows, row):
    return jnp.where(
        own, own_rows[row : row + 1, :].astype(WIDE), other_rows[row : row + 1, :].astype(WIDE)
    )


def inverse_size(wide):
    return lax.rsqrt(jnp.mean(wide * wide, axis=-1, keepdims=True) + EPSILON)


def both_sums(own, values):
    mine = jnp.sum(jnp.where(own, values, 0.0), axis=0, keepdims=True)
    return mine, jnp.sum(jnp.where(own, 0.0, values), axis=0, keepdims=True)


def same_head(rows, columns):
    row_head = lax.broadcasted_iota(jnp.int32, (rows, columns), 0) // HEAD
    return row_head == lax.broadcasted_iota(jnp.int32, (rows, columns), 1) // HEAD


def fold(square):
    size = square.shape[1]
    total = None
    for low in range(0, size, LANES):
        part = square[:, low : min(low + LANES, size)]
        if part.shape[1] < LANES:
            part = jnp.concatenate(
                [part, jnp.zeros((part.shape[0], LANES - part.shape[1]), part.dtype)], axis=1
            )
        total = part if total is None else total + part
    return total


def unfold(folded):
    size = folded.shape[0]
    parts = [folded[:, : min(LANES, size - low)] for low in range(0, size, LANES)]
    return jnp.where(same_head(size, size), jnp.concatenate(parts, axis=1), 0.0)


def packed(square, totals):
    keep = same_head(square.shape[0], square.shape[1])
    return fold(jnp.where(keep, square, 0.0)) + pltpu.roll(
        fold(jnp.where(keep, totals, 0.0)), HEAD, 1
    )


def unpacked(folded):
    return unfold(folded), unfold(pltpu.roll(folded, LANES - HEAD, 1))


def log_exp(wide):
    return jnp.maximum(wide, 0.0) + jnp.log1p(jnp.exp(-jnp.abs(wide)))


def logistic(wide):
    return 0.5 + 0.5 * jnp.tanh(0.5 * wide)


def self_project_body(table, x, mod_own, mod_other, weight, normed, raw, q, k, v, own_out, other_out, squares, totals):
    step = pl.program_id(0)
    rows, columns = q.shape
    own = own_image(table, table[FIRST] + step * rows, rows)
    wide = x[...].astype(WIDE)
    low = (
        wide * inverse_size(wide) * (1.0 + pick(own, mod_own, mod_other, 1))
        + pick(own, mod_own, mod_other, 0)
    ).astype(LOW)
    normed[...] = low
    out = times_transposed(low, weight[...])
    raw[...] = out[:, : 2 * columns]
    q[...] = log_exp(out[:, :columns]).astype(LOW)
    keys = log_exp(out[:, columns : 2 * columns]).astype(LOW)
    values = out[:, 2 * columns :].astype(LOW)
    k[...] = keys
    v[...] = values

    @pl.when(step == 0)
    def _():
        squares[...] = jnp.zeros_like(squares)
        totals[...] = jnp.zeros_like(totals)

    ones = jnp.ones((rows, columns), LOW)
    for image in range(2):
        zero = jnp.zeros_like(keys)
        masked = jnp.where(own, keys, zero) if image == 0 else jnp.where(own, zero, keys)
        squares[image] += over_tokens(masked, values)
        totals[image] += over_tokens(masked, ones)

    @pl.when(step == pl.num_programs(0) - 1)
    def _():
        own_out[...] = packed(squares[0], totals[0])
        other_out[...] = packed(squares[1], totals[1])


def self_project(table, x, mod_own, mod_other, weight, columns):
    tokens, width = x.shape
    rows = 128
    row = lambda c: pl.BlockSpec((rows, c), lambda i, t: (i, 0))
    fixed = lambda *s: pl.BlockSpec(s, lambda i, t: (0,) * len(s))
    return call(
        self_project_body,
        "self_project",
        [((tokens, width), LOW), ((tokens, 2 * columns), WIDE)]
        + [((tokens, columns), LOW)] * 3
        + [((columns, LANES), WIDE)] * 2,
        (x, mod_own, mod_other, weight),
        grid=(tokens // rows,),
        in_specs=[row(width), fixed(*mod_own.shape), fixed(*mod_own.shape), fixed(*weight.shape)],
        out_specs=[row(width), row(2 * columns)]
        + [row(columns)] * 3
        + [fixed(columns, LANES)] * 2,
        scratch=[pltpu.VMEM((2, columns, columns), WIDE)] * 2,
        flops=4 * tokens * width * 3 * columns,
        table=table,
    )


def keep_squares(kernels, key_totals, own_fold, other_fold):
    for image, folded in enumerate((own_fold, other_fold)):
        square, total = unpacked(folded[...])
        kernels[image, 0], kernels[image, 1] = split(square)
        key_totals[image, 0], key_totals[image, 1] = split(total)


def self_attend_body(table, q, own_fold, other_fold, attended, wide_out, denominator, kernels, key_totals):
    step = pl.program_id(0)
    rows = q.shape[0]

    @pl.when(step == 0)
    def _():
        keep_squares(kernels, key_totals, own_fold, other_fold)

    own = own_image(table, table[FIRST] + step * rows, rows)
    queries = q[...]

    def both(pair):
        own_part = dot(queries, pair[0, 0]) + dot(queries, pair[0, 1])
        return jnp.where(own, own_part, dot(queries, pair[1, 0]) + dot(queries, pair[1, 1]))

    under = both(key_totals) + 1.0
    out = both(kernels) / under
    attended[...] = out.astype(LOW)
    wide_out[...] = out
    denominator[...] = under


def self_attend(table, q, own_fold, other_fold):
    tokens, columns = q.shape
    rows = 128
    row = pl.BlockSpec((rows, columns), lambda i, t: (i, 0))
    fixed = pl.BlockSpec((columns, LANES), lambda i, t: (0, 0))
    return call(
        self_attend_body,
        "self_attend",
        [((tokens, columns), LOW), ((tokens, columns), WIDE), ((tokens, columns), WIDE)],
        (q, own_fold, other_fold),
        grid=(tokens // rows,),
        in_specs=[row, fixed, fixed],
        out_specs=[row, row, row],
        scratch=[pltpu.VMEM((2, 2, columns, columns), LOW)] * 2,
        flops=16 * tokens * columns * columns,
        table=table,
    )


def self_back_body(table, grad, q, wide_out, denominator, own_fold, other_fold, grad_q, own_out, other_out, kernels, key_totals, squares, totals):
    step = pl.program_id(0)
    rows, columns = q.shape

    @pl.when(step == 0)
    def _():
        keep_squares(kernels, key_totals, own_fold, other_fold)
        squares[...] = jnp.zeros_like(squares)
        totals[...] = jnp.zeros_like(totals)

    own = own_image(table, table[FIRST] + step * rows, rows)
    wide = grad[0].astype(WIDE)
    over = 1.0 / denominator[...]
    numer_high, numer_low = split(wide * over)
    ones = jnp.where(same_head(columns, columns), 1.0, 0.0).astype(LOW)
    high, low = split(wide * wide_out[...])
    denom = -(dot(high, ones) + dot(low, ones)) * over
    denom_high, denom_low = split(denom)

    def back(image):
        square, total = kernels[image, 0], key_totals[image, 0]
        through = (
            times_transposed(numer_high, square)
            + times_transposed(numer_low, square)
            + times_transposed(numer_high, kernels[image, 1])
        )
        totals_part = (
            times_transposed(denom_high, total)
            + times_transposed(denom_low, total)
            + times_transposed(denom_high, key_totals[image, 1])
        )
        return through + totals_part * (1.0 / HEAD)

    grad_q[...] = jnp.where(own, back(0), back(1))
    queries = q[...]
    zero = jnp.zeros_like(queries)
    for image in range(2):
        masked = jnp.where(own, queries, zero) if image == 0 else jnp.where(own, zero, queries)
        squares[image] += over_tokens(masked, numer_high) + over_tokens(masked, numer_low)
        totals[image] += over_tokens(masked, denom_high) + over_tokens(masked, denom_low)

    @pl.when(step == pl.num_programs(0) - 1)
    def _():
        own_out[...] = packed(squares[0], totals[0])
        other_out[...] = packed(squares[1], totals[1])


def self_back(table, grad, q, wide_out, denominator, own_fold, other_fold):
    count, rows, columns = grad.shape
    tokens = q.shape[0]
    row = pl.BlockSpec((rows, columns), lambda i, t: (i, 0))
    fixed = pl.BlockSpec((columns, LANES), lambda i, t: (0, 0))
    return call(
        self_back_body,
        "self_back",
        [((tokens, columns), WIDE)] + [((columns, LANES), WIDE)] * 2,
        (grad, q, wide_out, denominator, own_fold, other_fold),
        grid=(count,),
        in_specs=[pl.BlockSpec((1, rows, columns), lambda i, t: (i, 0, 0)), row, row, row, fixed, fixed],
        out_specs=[row, fixed, fixed],
        scratch=[pltpu.VMEM((2, 2, columns, columns), LOW)] * 2
        + [pltpu.VMEM((2, columns, columns), WIDE)] * 2,
        flops=48 * tokens * columns * columns,
        table=table,
    )


def self_project_back_body(table, grad_q, k, v, raw, own_fold, other_fold, grad_out, kernels, key_totals):
    step = pl.program_id(0)
    rows, columns = k.shape

    @pl.when(step == 0)
    def _():
        keep_squares(kernels, key_totals, own_fold, other_fold)

    own = own_image(table, table[FIRST] + step * rows, rows)
    keys, values = k[...], v[...]
    ones = jnp.ones((16, columns), LOW)

    def grad_k(image):
        total = times_transposed(ones, key_totals[image, 0]) + times_transposed(
            ones, key_totals[image, 1]
        )
        return (
            times_transposed(values, kernels[image, 0])
            + times_transposed(values, kernels[image, 1])
            + total[:1] * (1.0 / HEAD)
        )

    def grad_v(image):
        return dot(keys, kernels[image, 0]) + dot(keys, kernels[image, 1])

    given = raw[...]
    q_part = grad_q[...] * logistic(given[:, :columns])
    k_part = jnp.where(own, grad_k(0), grad_k(1)) * logistic(given[:, columns:])
    v_part = jnp.where(own, grad_v(0), grad_v(1))
    grad_out[...] = jnp.concatenate([q_part, k_part, v_part], axis=1).astype(LOW)


def self_project_back(table, grad_q, k, v, raw, own_fold, other_fold):
    tokens, columns = k.shape
    rows = 128
    row = lambda c: pl.BlockSpec((rows, c), lambda i, t: (i, 0))
    fixed = pl.BlockSpec((columns, LANES), lambda i, t: (0, 0))
    return call(
        self_project_back_body,
        "self_project_back",
        [((tokens, 3 * columns), LOW)],
        (grad_q, k, v, raw, own_fold, other_fold),
        grid=(tokens // rows,),
        in_specs=[row(columns), row(columns), row(columns), row(2 * columns), fixed, fixed],
        out_specs=[row(3 * columns)],
        scratch=[pltpu.VMEM((2, 2, columns, columns), LOW)] * 2,
        flops=16 * tokens * columns * columns,
        table=table,
    )[0]


def live_keys(table, own, keys):
    place = lax.broadcasted_iota(jnp.int32, (1, keys), 1)
    return place < jnp.where(own, table[OWN_LENGTH], table[OTHER_LENGTH])


def shard_of(first, rest, step, which):
    rows = first.shape[0]
    return first[...] if step == 0 else rest[step - 1, which * rows : (which + 1) * rows, :]


def middle_body(table, att, x, mod_own, mod_other, out_first, query_first, cross_first, *refs):
    pieces, (kv_own, kv_other) = refs[:8], refs[8:10]
    branch, after_low, queries_out, probs_out, text_out, after_cross, normed, rest = refs[10:]
    put_in_order(table, pieces, rest)
    count, rows, columns = att.shape
    keys = kv_own.shape[1]
    heads = columns // CROSS_HEAD
    own = own_image(table, table[BLOCK_FIRST], rows)
    y1 = jnp.zeros((rows, x.shape[1]), WIDE)
    for step in range(count):
        y1 += dot(att[turned(table, step, count)], shard_of(out_first, rest, step, 0))
    branch[...] = y1
    x1 = x[...].astype(WIDE) + pick(own, mod_own, mod_other, 2) * y1
    x1_low = x1.astype(LOW)
    after_low[...] = x1_low
    live = live_keys(table, own, keys)
    yc = jnp.zeros_like(x1)
    for step in range(count):
        queries = times_transposed(x1_low, shard_of(query_first, rest, step, 1)).astype(LOW)
        queries_out[step] = queries
        place = turned(table, step, count)
        mine, theirs = kv_own[place], kv_other[place]
        parts = []
        for head in range(heads):
            lanes = slice(head * CROSS_HEAD, (head + 1) * CROSS_HEAD)
            wide_lanes = slice(columns + head * CROSS_HEAD, columns + (head + 1) * CROSS_HEAD)
            q = queries[:, lanes]
            scores = jnp.where(
                own, times_transposed(q, mine[:, lanes]), times_transposed(q, theirs[:, lanes])
            ) * (1.0 / math.sqrt(CROSS_HEAD))
            scores = jnp.where(live, scores, MASKED_OUT)
            raised = jnp.exp(scores - jnp.max(scores, axis=-1, keepdims=True))
            probs = raised / jnp.sum(raised, axis=-1, keepdims=True)
            probs_out[step * heads + head] = probs
            low = probs.astype(LOW)
            parts.append(
                jnp.where(own, dot(low, mine[:, wide_lanes]), dot(low, theirs[:, wide_lanes]))
            )
        text = jnp.concatenate(parts, axis=1).astype(LOW)
        text_out[step] = text
        yc += dot(text, shard_of(cross_first, rest, step, 2))
    x2 = x1 + yc
    after_cross[...] = x2
    normed[...] = (
        x2 * inverse_size(x2) * (1.0 + pick(own, mod_own, mod_other, 4))
        + pick(own, mod_own, mod_other, 3)
    ).astype(LOW)


def middle_back_body(table, grad_own, grad_1, grad_2, grad_3, x2_in, upstream, branch, mod_own, mod_other, out_first, query_first, cross_first, rest, kv_own, kv_other, probs_in, queries_in, cross_grad, query_grad, attn_grad, attended_grad, after_grad, sums, kv_own_grad, kv_other_grad):
    count, rows, columns = queries_in.shape
    keys = kv_own.shape[1]
    heads = columns // CROSS_HEAD
    scale = 1.0 / math.sqrt(CROSS_HEAD)
    own = own_image(table, table[BLOCK_FIRST], rows)
    grad = with_own(grad_own, grad_1, grad_2, grad_3)
    x2 = x2_in[...]
    inverse = inverse_size(x2)
    xh = x2 * inverse
    sums[0:1], sums[1:2] = both_sums(own, grad)
    sums[2:3], sums[3:4] = both_sums(own, grad * xh)
    e = grad * (1.0 + pick(own, mod_own, mod_other, 4))
    dx2 = upstream[...].astype(WIDE) + inverse * (
        e - xh * jnp.mean(e * xh, axis=-1, keepdims=True)
    )
    dyc = dx2.astype(LOW)
    cross_grad[...] = dyc
    dx1 = dx2
    for step in range(count):
        doc = times_transposed(dyc, shard_of(cross_first, rest, step, 2)).astype(LOW)
        place = turned(table, step, count)
        mine, theirs = kv_own[place], kv_other[place]
        queries = queries_in[step]
        query_parts = []
        key_parts = ([], [])
        value_parts = ([], [])
        for head in range(heads):
            lanes = slice(head * CROSS_HEAD, (head + 1) * CROSS_HEAD)
            wide_lanes = slice(columns + head * CROSS_HEAD, columns + (head + 1) * CROSS_HEAD)
            do, q = doc[:, lanes], queries[:, lanes]
            probs = probs_in[step * heads + head]
            dp = jnp.where(
                own,
                times_transposed(do, mine[:, wide_lanes]),
                times_transposed(do, theirs[:, wide_lanes]),
            )
            ds = (probs * (dp - jnp.sum(probs * dp, axis=-1, keepdims=True))).astype(LOW)
            low = probs.astype(LOW)
            zero = jnp.zeros_like(ds)
            query_parts.append(
                jnp.where(own, dot(ds, mine[:, lanes]), dot(ds, theirs[:, lanes])) * scale
            )
            for image in range(2):
                mask = (lambda a: jnp.where(own, a, zero)) if image == 0 else (
                    lambda a: jnp.where(own, zero, a)
                )
                key_parts[image].append(over_tokens(mask(ds), q) * scale)
                value_parts[image].append(over_tokens(mask(low), do))
        dqc = jnp.concatenate(query_parts, axis=1).astype(LOW)
        query_grad[step] = dqc
        kv_own_grad[place] = jnp.concatenate(key_parts[0] + value_parts[0], axis=1).astype(LOW)
        kv_other_grad[place] = jnp.concatenate(key_parts[1] + value_parts[1], axis=1).astype(LOW)
        dx1 = dx1 + dot(dqc, shard_of(query_first, rest, step, 1))
    after_grad[...] = dx1
    sums[4:5], sums[5:6] = both_sums(own, dx1 * branch[...])
    sums[6:8] = jnp.zeros((2, sums.shape[1]), WIDE)
    dy1 = (dx1 * pick(own, mod_own, mod_other, 2)).astype(LOW)
    attn_grad[...] = dy1
    for step in range(count):
        attended_grad[turned(table, step, count)] = times_transposed(
            dy1, shard_of(out_first, rest, step, 0)
        ).astype(LOW)


def first_norm_back_body(table, grad_own, grad_1, grad_2, grad_3, after_grad, x, mod_own, mod_other, input_grad, sums):
    rows = x.shape[0]
    own = own_image(table, table[BLOCK_FIRST], rows)
    grad = with_own(grad_own, grad_1, grad_2, grad_3)
    wide = x[...].astype(WIDE)
    inverse = inverse_size(wide)
    xh = wide * inverse
    sums[0:1], sums[1:2] = both_sums(own, grad)
    sums[2:3], sums[3:4] = both_sums(own, grad * xh)
    sums[4:8] = jnp.zeros((4, sums.shape[1]), WIDE)
    e = grad * (1.0 + pick(own, mod_own, mod_other, 1))
    input_grad[...] = (
        after_grad[...] + inverse * (e - xh * jnp.mean(e * xh, axis=-1, keepdims=True))
    ).astype(LOW)


def output_body(table, branches, x2, upstream, mod_own, mod_other, output, sums):
    rows = x2.shape[0]
    own = own_image(table, table[BLOCK_FIRST], rows)
    branch = total(branches)
    sums[0:1], sums[1:2] = both_sums(own, upstream[...].astype(WIDE) * branch)
    sums[2:8] = jnp.zeros((6, sums.shape[1]), WIDE)
    output[...] = (x2[...] + pick(own, mod_own, mod_other, 5) * branch).astype(LOW)


def up_body(table, *refs):
    blocks, weight, (wide_out, low_out, ordered) = refs[:-4], refs[-4], refs[-3:]
    rows = blocks[0].shape[0]

    @pl.when(pl.program_id(0) == 0)
    def _():
        for step, block in enumerate(blocks):
            low = turned(table, step, len(blocks)) * rows
            ordered[pl.ds(pl.multiple_of(low, 16), rows), :] = block[...]

    up = times_transposed(ordered[...], weight[...])
    wide_out[...] = up
    low_out[...] = (up * logistic(up)).astype(LOW)


def up_project(table, blocks, weight):
    rows, width = blocks[0].shape
    tokens = len(blocks) * rows
    columns = 3 * LANES
    whole = lambda *shape: pl.BlockSpec(shape, lambda i, t: (0, 0))
    column = pl.BlockSpec((tokens, columns), lambda i, t: (0, i))
    return call(
        up_body,
        "up_project",
        [((tokens, weight.shape[0]), WIDE), ((tokens, weight.shape[0]), LOW), ((tokens, width), LOW)],
        (*blocks, weight),
        grid=(weight.shape[0] // columns,),
        in_specs=[whole(rows, width)] * len(blocks)
        + [pl.BlockSpec((columns, width), lambda i, t: (i, 0))],
        out_specs=[column, column, whole(tokens, width)],
        table=table,
    )


def fill(padded, block, rim):
    tokens = block.shape[0]
    edge = rim[...].astype(WIDE)
    padded[0:MAXW, :] = edge
    padded[MAXW : MAXW + tokens, :] = block.astype(WIDE)
    padded[MAXW + tokens : 2 * MAXW + tokens, :] = edge


def fill_masks(table, masks):
    tokens = masks.shape[1]
    place = table[FIRST] + lax.broadcasted_iota(jnp.int32, (tokens, LANES), 0)
    width = table[WIDTH]
    cut = table[CUT]
    late = place >= cut
    start = jnp.where(late, cut, 0)
    end = jnp.where(late, table[SEQ_TOKENS], cut)
    column = lax.bitwise_and(place, width - 1)
    one, none = jnp.ones((tokens, LANES), WIDE), jnp.zeros((tokens, LANES), WIDE)
    masks[0] = jnp.where(place - width >= start, one, none)
    masks[1] = jnp.where(place + width < end, one, none)
    masks[2] = jnp.where(column > 0, one, none)
    masks[3] = jnp.where(column < width - 1, one, none)


CHUNK = 64


def three_rows(table, padded, masks, low):
    width = table[WIDTH]
    above = padded[pl.ds(pl.multiple_of(MAXW + low - width, 16), CHUNK), :]
    below = padded[pl.ds(pl.multiple_of(MAXW + low + width, 16), CHUNK), :]
    own = padded[pl.ds(pl.multiple_of(MAXW + low, 16), CHUNK), :]
    rows = pl.ds(pl.multiple_of(low, 16), CHUNK)
    return above * masks[0, rows, :], own, below * masks[1, rows, :]


def nine_taps(rows, taps, left_mask, right_mask):
    mixed = [sum(rows[a] * taps[a][b] for a in range(3)) for b in range(3)]
    return (
        mixed[1]
        + left_mask * pltpu.roll(mixed[0], 1, 0)
        + right_mask * pltpu.roll(mixed[2], CHUNK - 1, 0)
    )


def taps_of(taps, flip):
    read = lambda a, b: taps[3 * a + b : 3 * a + b + 1, :]
    return [[read(2 - a, 2 - b) if flip else read(a, b) for b in range(3)] for a in range(3)]


def mix_body(table, value, gate, value_rim, gate_rim, value_taps, gate_taps, grad_hidden, hidden, grads, value_pad, gate_pad, masks):
    @pl.when(pl.program_id(0) == 0)
    def _():
        fill_masks(table, masks)

    fill(value_pad, value[...], value_rim)
    fill(gate_pad, gate[...], gate_rim)
    value_weights, gate_weights = taps_of(value_taps, False), taps_of(gate_taps, False)

    @pl.loop(0, value.shape[0] // CHUNK)
    def _(index):
        low = index * CHUNK
        rows = pl.ds(pl.multiple_of(low, CHUNK), CHUNK)
        left, right = masks[2, rows, :], masks[3, rows, :]
        mv = nine_taps(three_rows(table, value_pad, masks, low), value_weights, left, right)
        mg = nine_taps(three_rows(table, gate_pad, masks, low), gate_weights, left, right)
        sigma = logistic(mg)
        gated = mg * sigma
        hidden[rows, :] = (mv * gated).astype(LOW)
        dh = grad_hidden[rows, :]
        grads[0, rows, :] = (dh * gated).astype(LOW)
        grads[1, rows, :] = (dh * mv * (sigma * (1.0 + mg * (1.0 - sigma)))).astype(LOW)


def mix(table, activated, rim, taps, grad_hidden):
    tokens, wide = activated.shape
    columns = wide // 2
    tiles = columns // LANES
    block = lambda r, shift: pl.BlockSpec((r, LANES), lambda i, t: (0, i + shift))
    pad = pltpu.VMEM((tokens + 2 * MAXW, LANES), WIDE)
    return call(
        mix_body,
        "mix",
        [((tokens, columns), LOW), ((2, tokens, columns), LOW)],
        (activated, activated, rim, rim, taps, taps, grad_hidden),
        grid=(tiles,),
        in_specs=[
            block(tokens, 0),
            block(tokens, tiles),
            block(MAXW, 0),
            block(MAXW, tiles),
            block(taps.shape[0], 0),
            block(taps.shape[0], tiles),
            block(tokens, 0),
        ],
        out_specs=[
            block(tokens, 0),
            pl.BlockSpec((2, tokens, LANES), lambda i, t: (0, 0, i)),
        ],
        scratch=[pad, pad, pltpu.VMEM((4, tokens, LANES), WIDE)],
        flops=6000 * tokens * columns // 2,
        table=table,
    )


def mix_back_body(table, grads, grads_rim, activated, rim, taps, up, grad_up, tap_grads, grad_pad, act_pad, masks):
    @pl.when(pl.program_id(0) == 0)
    def _():
        fill_masks(table, masks)

    fill(grad_pad, grads[0], grads_rim.at[0])
    fill(act_pad, activated[...], rim)
    weights = taps_of(taps, True)

    def step(index, sums):
        low = index * CHUNK
        rows = pl.ds(pl.multiple_of(low, CHUNK), CHUNK)
        left, right = masks[2, rows, :], masks[3, rows, :]
        mine = three_rows(table, grad_pad, masks, low)
        dact = nine_taps(mine, weights, left, right)
        given = up[rows, :]
        sigma = logistic(given)
        grad_up[rows, :] = (dact * (sigma * (1.0 + given * (1.0 - sigma)))).astype(LOW)
        acts = three_rows(table, act_pad, masks, low)
        turned = (
            right * pltpu.roll(mine[1], CHUNK - 1, 0),
            mine[1],
            left * pltpu.roll(mine[1], 1, 0),
        )
        return tuple(
            sums[3 * a + b]
            + jnp.sum((acts[a] * turned[b]).reshape(CHUNK // 8, 8, LANES), axis=0)
            for a in range(3)
            for b in range(3)
        )

    zero = jnp.zeros((8, LANES), WIDE)
    sums = lax.fori_loop(0, activated.shape[0] // CHUNK, step, (zero,) * 9)
    for tap in range(9):
        tap_grads[tap : tap + 1, :] = jnp.sum(sums[tap], axis=0, keepdims=True)
    tap_grads[9:16, :] = jnp.zeros((7, LANES), WIDE)


def mix_back(table, grads, grads_rim, activated, rim, taps, up):
    tokens, wide = activated.shape
    columns = wide // 2
    tiles = columns // LANES
    block = lambda r: pl.BlockSpec((r, LANES), lambda i, t: (0, i))
    half = lambda r: pl.BlockSpec(
        (1, r, LANES), lambda i, t: (lax.div(i, tiles), 0, lax.rem(i, tiles))
    )
    pad = pltpu.VMEM((tokens + 2 * MAXW, LANES), WIDE)
    return call(
        mix_back_body,
        "mix_back",
        [((tokens, wide), LOW), ((16, wide), WIDE)],
        (grads, grads_rim, activated, rim, taps, up),
        grid=(2 * tiles,),
        in_specs=[half(tokens), half(MAXW), block(tokens), block(MAXW), block(taps.shape[0]), block(tokens)],
        out_specs=[block(tokens), block(16)],
        scratch=[pad, pad, pltpu.VMEM((4, tokens, LANES), WIDE)],
        flops=6000 * tokens * columns,
        table=table,
    )


def eighth_body(table, *refs):
    weights, out, joined = refs[:-2], refs[-2], refs[-1]
    low = 0
    for weight in weights:
        joined[low : low + weight.shape[0], :] = weight[...]
        low += weight.shape[0]
    rows = out.shape[0]
    out[...] = joined[pl.ds(pl.multiple_of(table[0] * rows, 16), rows), :]


def put_in_order(table, pieces, out):
    steps, rows = pieces[0].shape[0], pieces[0].shape[1]
    for place, piece in enumerate(pieces):
        block = lax.bitwise_xor(table[ROW_PLACE], place)
        for step in range(steps):
            out[step, pl.ds(pl.multiple_of(block * rows, 16), rows), :] = piece[step]


def after(value, *others):
    return lax.optimization_barrier((value, others))[0]


def fetch_eighths(weights):
    columns = weights[0].shape[1]
    rows = -(-sum(weight.shape[0] for weight in weights) // LANES) * 16
    eighth = call(
        eighth_body,
        "eighth",
        [((rows, columns), weights[0].dtype)],
        weights,
        scratch=[pltpu.VMEM((8 * rows, columns), weights[0].dtype)],
        table=(lax.axis_index("seq") % 8).reshape(1).astype(jnp.int32),
    )[0]
    return jnp.stack([from_behind(eighth, step) for step in range(1, lax.axis_size("tp"))])


def share_eighths(fetched, ready):
    count = lax.axis_size("seq")
    far = lambda flip: lax.ppermute(fetched, "seq", [(k, k ^ flip) for k in range(count)])
    pieces = []
    for piece in [fetched] + after([far(2), far(4), far(6)], *ready):
        pieces += [piece, swapped(piece, "seq", 0)]
    return pieces


def token_block(values, place):
    count = lax.axis_size("tp")
    size = values.shape[0] // count
    return lax.dynamic_slice_in_dim(values, (place % count) * size, size, 0)


def own_rows(values):
    rows = values.shape[0] // lax.axis_size("tp")
    return pl.BlockSpec((rows, values.shape[1]), lambda i, t: (t[TP_PLACE], 0))


def placed_blocks(blocks):
    count = len(blocks)
    place = lax.axis_index("tp")
    result = jnp.zeros((count,) + blocks[0].shape, blocks[0].dtype)
    for step in range(count):
        result = lax.dynamic_update_index_in_dim(result, blocks[step], (place - step) % count, 0)
    return result.reshape((count * blocks[0].shape[0],) + blocks[0].shape[1:])


def all_blocks(block):
    return [block] + [from_behind(block, step) for step in range(1, lax.axis_size("tp"))]


def product(left, right):
    count = lax.axis_size("tp")
    return dot(left, right).astype(LOW).reshape(count, left.shape[0] // count, right.shape[1])


def spread(blocks):
    count = lax.axis_size("tp")
    place = lax.axis_index("tp")
    return [
        from_behind(
            lax.dynamic_index_in_dim(blocks, (place + step) % count, 0, keepdims=False), step
        )
        for step in range(1, count)
    ]


def own_block(blocks):
    return pl.BlockSpec((1,) + blocks.shape[1:], lambda i, t: (t[TP_PLACE], 0, 0))


def with_own(own, *others):
    result = own[0].astype(WIDE)
    for other in others:
        result += other[...].astype(WIDE)
    return result


def total(parts):
    result = parts[0].astype(WIDE)
    for place in range(1, parts.shape[0]):
        result += parts[place].astype(WIDE)
    return result


def turned(table, step, count):
    return lax.rem(table[TP_PLACE] + count - step, count)


def same_everywhere(block):
    count = lax.axis_size("tp")
    flipped = lambda flip: lax.ppermute(block, "tp", [(k, k ^ flip) for k in range(count)])
    return (block + flipped(1)) + (flipped(2) + flipped(3))


def sum_rows(grad):
    return lax.optimization_barrier(
        lax.psum_scatter(grad.astype(LOW), "seq", scatter_dimension=0, tiled=True)
    )


def square_body(table, dyc, text, x1, dqc, dy1, att, kv_mine, kv_theirs, out, kv_out):
    kv_out[...] = (kv_mine[...].astype(WIDE) + kv_theirs[...].astype(WIDE)).astype(LOW)
    parts = [
        over_tokens(left[...], right[0]) for left, right in ((dyc, text), (x1, dqc), (dy1, att))
    ]
    rest = out.shape[1] - sum(part.shape[1] for part in parts)
    if rest:
        parts.append(jnp.zeros((out.shape[0], rest), WIDE))
    out[...] = jnp.concatenate(parts, axis=1).astype(LOW)


def square_parts(table, lefts, rights, kv_mine, kv_theirs):
    rows, width = lefts[0].shape
    count, _, columns = rights[0].shape
    block = -(-3 * columns // LANES) * LANES
    whole = pl.BlockSpec((rows, width), lambda i, t: (0, 0))
    one = pl.BlockSpec((1, rows, columns), lambda i, t: (turned(t, i, count), 0, 0))
    still = pl.BlockSpec((1, rows, columns), lambda i, t: (i, 0, 0))
    kv = pl.BlockSpec((1,) + kv_mine.shape[1:], lambda i, t: (i, 0, 0))
    return call(
        square_body,
        "square_parts",
        [((width, count * block), LOW), (kv_mine.shape, LOW)],
        [array for pair in zip(lefts, rights) for array in pair] + [kv_mine, kv_theirs],
        grid=(count,),
        in_specs=[whole, one, whole, one, whole, still, kv, kv],
        out_specs=[pl.BlockSpec((width, block), lambda i, t: (0, i)), kv],
        table=table,
    )


def ffn_body(table, grad_ffn, hidden, normed, grad_up, out):
    step = pl.program_id(0)

    @pl.when(step == 0)
    def _():
        out[...] = over_tokens(grad_ffn[...], hidden[...]).astype(LOW)

    @pl.when(step > 0)
    def _():
        out[...] = over_tokens(normed[...], grad_up[...]).astype(LOW)


def ffn_parts_of(table, grad_ffn, hidden, normed, grad_up):
    tokens, width = normed.shape
    columns = hidden.shape[1]
    whole = pl.BlockSpec((tokens, width), lambda i, t: (0, 0))
    return call(
        ffn_body,
        "ffn_parts",
        [((width, 3 * columns), LOW)],
        (grad_ffn, hidden, normed, grad_up),
        grid=(3,),
        in_specs=[
            whole,
            pl.BlockSpec((tokens, columns), lambda i, t: (0, 0)),
            whole,
            pl.BlockSpec((tokens, columns), lambda i, t: (0, jnp.maximum(i - 1, 0))),
        ],
        out_specs=[pl.BlockSpec((width, columns), lambda i, t: (0, i))],
        table=table,
    )[0]


def late_body(table, normed, grad_projected, text, kv_grads, out):
    first = over_tokens(normed[...], grad_projected[...]).astype(LOW)
    second = over_tokens(text[...], total(kv_grads).astype(LOW)).astype(LOW)
    out[...] = jnp.concatenate([first, second], axis=1)


def shards(
    hidden_in,
    cotangent,
    modulation,
    text_states,
    image_shapes,
    text_lengths,
    qkv_weight,
    attn_out_weight,
    cross_q_weight,
    cross_kv_weight,
    cross_out_weight,
    up_weight,
    conv_weight,
    down_weight,
):
    tokens_here, width = hidden_in.shape
    context = text_states.shape[1]
    keys = -(-context // 16) * 16
    self_cols = qkv_weight.shape[2]
    cross_cols = cross_q_weight.shape[1]
    ffn_cols = up_weight.shape[2]
    ffn_pad = -(-ffn_cols // LANES) * LANES
    count = lax.axis_size("tp")
    tp_index = lax.axis_index("tp")
    block_size = tokens_here // count
    seq_index = lax.axis_index("seq")
    side = seq_index % 2
    first_half = side == 0
    pair = seq_index - side
    pair_shapes = lax.dynamic_slice_in_dim(image_shapes, pair, 2, 0)
    row_width = pair_shapes[0, 1]
    lengths = lax.dynamic_slice_in_dim(text_lengths, pair, 2, 0)
    first_place = side * tokens_here
    table = jnp.stack(
        [
            first_place,
            pair_shapes[0, 0] * row_width,
            side,
            row_width,
            jnp.where(first_half, lengths[0], lengths[1]),
            jnp.where(first_half, lengths[1], lengths[0]),
            first_place + tp_index * block_size,
            jnp.int32(2 * tokens_here),
            tp_index,
            seq_index % 8,
        ]
    ).astype(jnp.int32)

    mod_own = modulation[0]
    mod_other = swapped(mod_own, "seq", 0).astype(WIDE)
    mod_own = mod_own.astype(WIDE)
    weights = [attn_out_weight.T, cross_q_weight.T, cross_out_weight.T]
    fetched = fetch_eighths(weights)
    qkv_flat = qkv_weight.transpose(1, 2, 0).reshape(3 * self_cols, width)
    text_rows = jnp.pad(text_states[0], ((0, keys - context), (0, 0)))
    kv_here = times_transposed(
        text_rows, cross_kv_weight.transpose(1, 2, 0).reshape(2 * cross_cols, width)
    ).astype(LOW)
    kv_sent_first = jnp.broadcast_to(kv_here[None], (count,) + kv_here.shape)
    normed_low, raw, q, k, v, part_own, part_other = self_project(
        table, after(hidden_in, kv_sent_first), mod_own, mod_other, qkv_flat, self_cols
    )
    theirs = swapped(jnp.stack([part_own, part_other]), "seq", 0)
    fetched = after(fetched, q)
    kernel_own, kernel_other = part_own + theirs[1], part_other + theirs[0]
    attended, attended_wide, denominator = self_attend(
        table, after(q, kv_here), kernel_own, kernel_other
    )

    whole = pl.BlockSpec(memory_space=pltpu.VMEM)
    x_rows, upstream_rows = own_rows(hidden_in), own_rows(cotangent)
    up_flat = jnp.pad(
        after(up_weight.transpose(1, 2, 0), attended), ((0, 0), (0, ffn_pad - ffn_cols), (0, 0))
    ).reshape(2 * ffn_pad, width)
    down_flat = jnp.pad(after(down_weight.T, attended), ((0, ffn_pad - ffn_cols), (0, 0)))
    taps = (
        jnp.pad(conv_weight, ((0, 7), (0, 0), (0, ffn_pad - ffn_cols)))
        .reshape(16, 2 * ffn_pad)
        .astype(WIDE)
    )
    gate_rows = jnp.where(
        (first_place + jnp.arange(tokens_here, dtype=jnp.int32) >= table[CUT])[:, None] == (side == 1),
        mod_own[5:6],
        mod_other[5:6],
    )
    grad_ffn = (cotangent.astype(WIDE) * gate_rows).astype(LOW)
    grad_hidden = times_transposed(grad_ffn, down_flat)
    ready = (up_flat, down_flat, taps, grad_hidden)
    split_tokens = lambda values: values.reshape(count, block_size, values.shape[1])
    kv_own = exchanged(kv_sent_first)
    attended_blocks = exchanged(after(split_tokens(attended), kv_own))
    kv_own = after(kv_own, *ready)
    kv_other = swapped(kv_own, "seq", 0)
    pieces = share_eighths(fetched, (*ready, attended_blocks))
    all_heads = count * cross_cols // CROSS_HEAD
    branch, after_low, queries, probs, text_low, after_cross, normed_two, rest = call(
        middle_body,
        "middle",
        [
            ((block_size, width), WIDE),
            ((block_size, width), LOW),
            ((count, block_size, cross_cols), LOW),
            ((all_heads, block_size, keys), WIDE),
            ((count, block_size, cross_cols), LOW),
            ((block_size, width), WIDE),
            ((block_size, width), LOW),
            ((count - 1, 8 * fetched.shape[1], width), LOW),
        ],
        (attended_blocks, hidden_in, mod_own, mod_other, *weights, *pieces, kv_own, kv_other),
        in_specs=[whole, x_rows] + [whole] * 15,
        flops=60 * block_size * width * width,
        table=table,
    )

    up_wide, activated, normed_two_low = up_project(table, all_blocks(normed_two), up_flat)
    rim = swapped(jnp.where(first_half, activated[-MAXW:], activated[:MAXW]), "seq", 0)
    hidden, grads = mix(table, activated, rim, taps, grad_hidden)
    grads_rim = swapped(jnp.where(first_half, grads[:, -MAXW:], grads[:, :MAXW]), "seq", 0)
    branch_sent = product(hidden, down_flat)
    grad_up, tap_part = mix_back(
        table, grads, grads_rim, activated, rim, taps, after(up_wide, branch_sent)
    )
    branches = exchanged(branch_sent)
    norm_two_sent = product(grad_up, up_flat)
    grad_norm_two = spread(norm_two_sent)
    output_block, output_sums = call(
        output_body,
        "output",
        [((block_size, width), LOW), ((8, width), WIDE)],
        (branches, after_cross, cotangent, mod_own, mod_other),
        in_specs=[whole, whole, upstream_rows, whole, whole],
        table=table,
    )
    ffn_parts = ffn_parts_of(
        table, grad_ffn, after(hidden, norm_two_sent, output_block), normed_two_low, grad_up
    )
    ffn_rows = sum_rows(after(ffn_parts, grad_norm_two))
    output_blocks = all_blocks(after(output_block, grad_norm_two))

    (
        cross_grad,
        query_grad,
        attn_grad,
        attended_grad,
        after_grad,
        middle_sums,
        kv_own_grad,
        kv_other_grad,
    ) = call(
        middle_back_body,
        "middle_back",
        [
            ((block_size, width), LOW),
            ((count, block_size, cross_cols), LOW),
            ((block_size, width), LOW),
            ((count, block_size, self_cols), LOW),
            ((block_size, width), WIDE),
            ((8, width), WIDE),
            ((count, keys, 2 * cross_cols), LOW),
            ((count, keys, 2 * cross_cols), LOW),
        ],
        (
            after(norm_two_sent, ffn_parts, output_block),
            *grad_norm_two,
            after_cross,
            cotangent,
            branch,
            mod_own,
            mod_other,
            *weights,
            rest,
            kv_own,
            kv_other,
            probs,
            queries,
        ),
        in_specs=[own_block(norm_two_sent)] + [whole] * 4 + [upstream_rows] + [whole] * 11,
        flops=120 * block_size * width * width,
        table=table,
    )

    grad_blocks = exchanged(after(attended_grad, output_blocks))
    kv_theirs = swapped(after(kv_other_grad, output_blocks), "seq", 0)
    squares, kv_sent = square_parts(
        table,
        (cross_grad, after_low, attn_grad),
        (text_low, query_grad, after(attended_blocks, attended_grad)),
        kv_own_grad,
        kv_theirs,
    )
    square_rows = sum_rows(after(squares, grad_blocks))
    kv_sent = after(kv_sent, grad_blocks)
    kv_parts = exchanged(kv_sent)
    grad_blocks = after(grad_blocks, squares, kv_sent, ffn_rows)
    grad_q, back_own, back_other = self_back(
        table, grad_blocks, q, attended_wide, denominator, kernel_own, kernel_other
    )
    back_theirs = swapped(jnp.stack([back_own, back_other]), "seq", 0)
    grad_projected = self_project_back(
        table,
        grad_q,
        k,
        v,
        raw,
        back_own + back_theirs[1],
        back_other + back_theirs[0],
    )
    normed_sent = product(grad_projected, qkv_flat)
    grad_normed = spread(normed_sent)
    late_parts = call(
        late_body,
        "late_parts",
        [((width, 3 * self_cols + 2 * cross_cols), LOW)],
        (normed_low, after(grad_projected, normed_sent), text_rows, kv_parts),
        table=table,
    )[0]
    late_rows = sum_rows(after(late_parts, square_rows, grad_normed))
    conv_sum = after(tap_part[:9], normed_sent)
    for place in range(lax.axis_size("seq").bit_length() - 1):
        conv_sum = conv_sum + swapped(conv_sum, "seq", place)
    square_sent = square_rows.reshape(square_rows.shape[0], count, -1).transpose(1, 0, 2)
    input_block, first_sums = call(
        first_norm_back_body,
        "first_norm_back",
        [((block_size, width), LOW), ((8, width), WIDE)],
        (
            after(normed_sent, late_parts, square_sent),
            *grad_normed,
            after_grad,
            hidden_in,
            mod_own,
            mod_other,
        ),
        in_specs=[own_block(normed_sent)] + [whole] * 4 + [x_rows, whole, whole],
        table=table,
    )
    square_parts_here = exchanged(square_sent)
    square_grads = total(square_parts_here)[:, : 3 * self_cols]
    pairs = jnp.concatenate([first_sums[:4], middle_sums[4:6], middle_sums[:4], output_sums[:2]])
    pairs = pairs.reshape(6, 2, width)
    pairs = pairs[:, 0] + swapped(pairs[:, 1], "seq", 0)
    modulation_grad = same_everywhere(pairs)
    input_block = after(input_block, square_parts_here, modulation_grad)
    late_rows = late_rows.astype(WIDE)
    qkv_grad = late_rows[:, : 3 * self_cols].reshape(-1, 3, self_cols)
    ckv_grad = late_rows[:, 3 * self_cols :].reshape(-1, 2, cross_cols)
    output = placed_blocks(output_blocks)
    input_blocks = after(all_blocks(input_block), qkv_grad, ckv_grad, square_grads, output)
    input_grad = placed_blocks(input_blocks).astype(WIDE)

    return (
        output,
        input_grad,
        modulation_grad[None],
        qkv_grad,
        square_grads[:, 2 * self_cols :],
        square_grads[:, self_cols : 2 * self_cols],
        ckv_grad,
        square_grads[:, :self_cols],
        ffn_rows[:, ffn_pad:].astype(WIDE).reshape(-1, 2, ffn_pad)[:, :, :ffn_cols],
        conv_sum.reshape(9, 2, ffn_pad)[:, :, :ffn_cols],
        ffn_rows[:, :ffn_cols].astype(WIDE),
    )


def solution(mesh):
    placed = (
        P("seq", None),
        P("seq", None),
        P("seq", None, None),
        P("seq", None, None),
        P(),
        P(),
        P(None, None, "tp"),
        P(None, "tp"),
        P(None, "tp"),
        P(None, None, "tp"),
        P(None, "tp"),
        P(None, None, "tp"),
        P(None, None, "tp"),
        P(None, "tp"),
    )
    return jax.shard_map(
        shards,
        mesh=mesh,
        in_specs=placed,
        out_specs=(
            P("seq", None),
            P("seq", None),
            P("seq", None, None),
            P("seq", None, "tp"),
            P("seq", "tp"),
            P("seq", "tp"),
            P("seq", None, "tp"),
            P("seq", "tp"),
            P("seq", None, "tp"),
            P(None, None, "tp"),
            P("seq", "tp"),
        ),
        check_vma=False,
    )
```

```python
import functools
import math

import jax
import jax.numpy as jnp
from jax import lax
from jax.experimental import pallas as pl
from jax.experimental.pallas import tpu as pltpu
from jax.sharding import PartitionSpec as P

HEAD = 32
CROSS_HEAD = 72
MAXW = 32
LANES = 128
GRANT = 56 * 1024 * 1024

EPSILON = 1e-06
MASKED_OUT = -1e30
LOW = jnp.bfloat16
WIDE = jnp.float32

FIRST, CUT, SIDE, WIDTH, OWN_LENGTH, OTHER_LENGTH, BLOCK_FIRST, SEQ_TOKENS, TP_PLACE, ROW_PLACE = range(10)


def swapped(block, axis, apart):
    count = lax.axis_size(axis)
    route = [(low, low ^ (1 << apart)) for low in range(count)]
    return lax.ppermute(block, axis, route)


def from_behind(block, step):
    count = lax.axis_size("tp")
    return lax.ppermute(block, "tp", [(k, (k + step) % count) for k in range(count)])


def exchanged(blocks):
    return lax.all_to_all(blocks, "tp", 0, 0, tiled=True)


def dot(left, right):
    return jnp.dot(left, right, preferred_element_type=WIDE)


def times_transposed(left, right):
    return lax.dot_general(left, right, (((1,), (1,)), ((), ())), preferred_element_type=WIDE)


def over_tokens(left, right):
    return lax.dot_general(left, right, (((0,), (0,)), ((), ())), preferred_element_type=WIDE)


def split(wide):
    high = wide.astype(LOW)
    return high, (wide - high.astype(WIDE)).astype(LOW)


def call(body, name, outs, arrays, *, grid=None, in_specs=None, out_specs=None, scratch=(), flops=0, table=None):
    shapes = tuple(jax.ShapeDtypeStruct(*out) for out in outs)
    size = sum(math.prod(a.shape) * a.dtype.itemsize for a in (*arrays, *shapes))
    whole = pl.BlockSpec(memory_space=pltpu.VMEM)
    return pl.pallas_call(
        body,
        out_shape=shapes,
        grid_spec=pltpu.PrefetchScalarGridSpec(
            num_scalar_prefetch=1,
            grid=grid or (1,),
            in_specs=in_specs or [whole] * len(arrays),
            out_specs=out_specs or [whole] * len(shapes),
            scratch_shapes=list(scratch),
        ),
        compiler_params=pltpu.CompilerParams(vmem_limit_bytes=GRANT),
        cost_estimate=pl.CostEstimate(flops=0, bytes_accessed=size // 100, transcendentals=0),
        name=name,
    )(table, *arrays)


def own_image(table, start, rows):
    place = start + lax.broadcasted_iota(jnp.int32, (rows, 1), 0)
    return (place >= table[CUT]).astype(jnp.int32) == table[SIDE]


def pick(own, own_rows, other_rows, row):
    return jnp.where(
        own, own_rows[row : row + 1, :].astype(WIDE), other_rows[row : row + 1, :].astype(WIDE)
    )


def inverse_size(wide):
    return lax.rsqrt(jnp.mean(wide * wide, axis=-1, keepdims=True) + EPSILON)


def both_sums(own, values):
    mine = jnp.sum(jnp.where(own, values, 0.0), axis=0, keepdims=True)
    return mine, jnp.sum(jnp.where(own, 0.0, values), axis=0, keepdims=True)


def same_head(rows, columns):
    row_head = lax.broadcasted_iota(jnp.int32, (rows, columns), 0) // HEAD
    return row_head == lax.broadcasted_iota(jnp.int32, (rows, columns), 1) // HEAD


def fold(square):
    size = square.shape[1]
    total = None
    for low in range(0, size, LANES):
        part = square[:, low : min(low + LANES, size)]
        if part.shape[1] < LANES:
            part = jnp.concatenate(
                [part, jnp.zeros((part.shape[0], LANES - part.shape[1]), part.dtype)], axis=1
            )
        total = part if total is None else total + part
    return total


def unfold(folded):
    size = folded.shape[0]
    parts = [folded[:, : min(LANES, size - low)] for low in range(0, size, LANES)]
    return jnp.where(same_head(size, size), jnp.concatenate(parts, axis=1), 0.0)


def packed(square, totals):
    keep = same_head(square.shape[0], square.shape[1])
    return fold(jnp.where(keep, square, 0.0)) + pltpu.roll(
        fold(jnp.where(keep, totals, 0.0)), HEAD, 1
    )


def unpacked(folded):
    return unfold(folded), unfold(pltpu.roll(folded, LANES - HEAD, 1))


def log_exp(wide):
    return jnp.maximum(wide, 0.0) + jnp.log1p(jnp.exp(-jnp.abs(wide)))


def logistic(wide):
    return 0.5 + 0.5 * jnp.tanh(0.5 * wide)


def self_project_body(table, x, mod_own, mod_other, weight, normed, raw, q, k, v, own_out, other_out, squares, totals):
    step = pl.program_id(0)
    rows, columns = q.shape
    own = own_image(table, table[FIRST] + step * rows, rows)
    wide = x[...].astype(WIDE)
    low = (
        wide * inverse_size(wide) * (1.0 + pick(own, mod_own, mod_other, 1))
        + pick(own, mod_own, mod_other, 0)
    ).astype(LOW)
    normed[...] = low
    out = times_transposed(low, weight[...])
    raw[...] = out[:, : 2 * columns]
    q[...] = log_exp(out[:, :columns]).astype(LOW)
    keys = log_exp(out[:, columns : 2 * columns]).astype(LOW)
    values = out[:, 2 * columns :].astype(LOW)
    k[...] = keys
    v[...] = values

    @pl.when(step == 0)
    def _():
        squares[...] = jnp.zeros_like(squares)
        totals[...] = jnp.zeros_like(totals)

    ones = jnp.ones((rows, columns), LOW)
    for image in range(2):
        zero = jnp.zeros_like(keys)
        masked = jnp.where(own, keys, zero) if image == 0 else jnp.where(own, zero, keys)
        squares[image] += over_tokens(masked, values)
        totals[image] += over_tokens(masked, ones)

    @pl.when(step == pl.num_programs(0) - 1)
    def _():
        own_out[...] = packed(squares[0], totals[0])
        other_out[...] = packed(squares[1], totals[1])


def self_project(table, x, mod_own, mod_other, weight, columns):
    tokens, width = x.shape
    rows = tokens // 2
    row = lambda c: pl.BlockSpec((rows, c), lambda i, t: (i, 0))
    fixed = lambda *s: pl.BlockSpec(s, lambda i, t: (0,) * len(s))
    return call(
        self_project_body,
        "self_project",
        [((tokens, width), LOW), ((tokens, 2 * columns), WIDE)]
        + [((tokens, columns), LOW)] * 3
        + [((columns, LANES), WIDE)] * 2,
        (x, mod_own, mod_other, weight),
        grid=(tokens // rows,),
        in_specs=[row(width), fixed(*mod_own.shape), fixed(*mod_own.shape), fixed(*weight.shape)],
        out_specs=[row(width), row(2 * columns)]
        + [row(columns)] * 3
        + [fixed(columns, LANES)] * 2,
        scratch=[pltpu.VMEM((2, columns, columns), WIDE)] * 2,
        flops=4 * tokens * width * 3 * columns,
        table=table,
    )


def keep_squares(kernels, key_totals, own_fold, other_fold):
    for image, folded in enumerate((own_fold, other_fold)):
        square, total = unpacked(folded[...])
        kernels[image, 0], kernels[image, 1] = split(square)
        key_totals[image, 0], key_totals[image, 1] = split(total)


def self_attend_body(table, q, own_fold, other_fold, attended, wide_out, denominator, kernels, key_totals):
    step = pl.program_id(0)
    rows = q.shape[0]

    @pl.when(step == 0)
    def _():
        keep_squares(kernels, key_totals, own_fold, other_fold)

    own = own_image(table, table[FIRST] + step * rows, rows)
    queries = q[...]

    def both(pair):
        own_part = dot(queries, pair[0, 0]) + dot(queries, pair[0, 1])
        return jnp.where(own, own_part, dot(queries, pair[1, 0]) + dot(queries, pair[1, 1]))

    under = both(key_totals) + 1.0
    out = both(kernels) / under
    attended[...] = out.astype(LOW)
    wide_out[...] = out
    denominator[...] = under


def self_attend(table, q, own_fold, other_fold):
    tokens, columns = q.shape
    rows = tokens // 2
    row = pl.BlockSpec((rows, columns), lambda i, t: (i, 0))
    fixed = pl.BlockSpec((columns, LANES), lambda i, t: (0, 0))
    return call(
        self_attend_body,
        "self_attend",
        [((tokens, columns), LOW), ((tokens, columns), WIDE), ((tokens, columns), WIDE)],
        (q, own_fold, other_fold),
        grid=(tokens // rows,),
        in_specs=[row, fixed, fixed],
        out_specs=[row, row, row],
        scratch=[pltpu.VMEM((2, 2, columns, columns), LOW)] * 2,
        flops=16 * tokens * columns * columns,
        table=table,
    )


def self_back_body(table, grad, q, wide_out, denominator, own_fold, other_fold, grad_q, own_out, other_out, kernels, key_totals, squares, totals):
    step = pl.program_id(0)
    rows, columns = q.shape

    @pl.when(step == 0)
    def _():
        keep_squares(kernels, key_totals, own_fold, other_fold)
        squares[...] = jnp.zeros_like(squares)
        totals[...] = jnp.zeros_like(totals)

    own = own_image(table, table[FIRST] + step * rows, rows)
    wide = grad[0].astype(WIDE)
    over = 1.0 / denominator[...]
    numer_high, numer_low = split(wide * over)
    ones = jnp.where(same_head(columns, columns), 1.0, 0.0).astype(LOW)
    high, low = split(wide * wide_out[...])
    denom = -(dot(high, ones) + dot(low, ones)) * over
    denom_high, denom_low = split(denom)

    def back(image):
        square, total = kernels[image, 0], key_totals[image, 0]
        through = (
            times_transposed(numer_high, square)
            + times_transposed(numer_low, square)
            + times_transposed(numer_high, kernels[image, 1])
        )
        totals_part = (
            times_transposed(denom_high, total)
            + times_transposed(denom_low, total)
            + times_transposed(denom_high, key_totals[image, 1])
        )
        return through + totals_part * (1.0 / HEAD)

    grad_q[...] = jnp.where(own, back(0), back(1))
    queries = q[...]
    zero = jnp.zeros_like(queries)
    for image in range(2):
        masked = jnp.where(own, queries, zero) if image == 0 else jnp.where(own, zero, queries)
        squares[image] += over_tokens(masked, numer_high) + over_tokens(masked, numer_low)
        totals[image] += over_tokens(masked, denom_high) + over_tokens(masked, denom_low)

    @pl.when(step == pl.num_programs(0) - 1)
    def _():
        own_out[...] = packed(squares[0], totals[0])
        other_out[...] = packed(squares[1], totals[1])


def self_back(table, grad, q, wide_out, denominator, own_fold, other_fold):
    count, rows, columns = grad.shape
    tokens = q.shape[0]
    row = pl.BlockSpec((rows, columns), lambda i, t: (i, 0))
    fixed = pl.BlockSpec((columns, LANES), lambda i, t: (0, 0))
    return call(
        self_back_body,
        "self_back",
        [((tokens, columns), WIDE)] + [((columns, LANES), WIDE)] * 2,
        (grad, q, wide_out, denominator, own_fold, other_fold),
        grid=(count,),
        in_specs=[pl.BlockSpec((1, rows, columns), lambda i, t: (i, 0, 0)), row, row, row, fixed, fixed],
        out_specs=[row, fixed, fixed],
        scratch=[pltpu.VMEM((2, 2, columns, columns), LOW)] * 2
        + [pltpu.VMEM((2, columns, columns), WIDE)] * 2,
        flops=48 * tokens * columns * columns,
        table=table,
    )


def self_project_back_body(table, grad_q, k, v, raw, own_fold, other_fold, grad_out, kernels, key_totals):
    step = pl.program_id(0)
    rows, columns = k.shape

    @pl.when(step == 0)
    def _():
        keep_squares(kernels, key_totals, own_fold, other_fold)

    own = own_image(table, table[FIRST] + step * rows, rows)
    keys, values = k[...], v[...]
    ones = jnp.ones((16, columns), LOW)

    def grad_k(image):
        total = times_transposed(ones, key_totals[image, 0]) + times_transposed(
            ones, key_totals[image, 1]
        )
        return (
            times_transposed(values, kernels[image, 0])
            + times_transposed(values, kernels[image, 1])
            + total[:1] * (1.0 / HEAD)
        )

    def grad_v(image):
        return dot(keys, kernels[image, 0]) + dot(keys, kernels[image, 1])

    given = raw[...]
    q_part = grad_q[...] * logistic(given[:, :columns])
    k_part = jnp.where(own, grad_k(0), grad_k(1)) * logistic(given[:, columns:])
    v_part = jnp.where(own, grad_v(0), grad_v(1))
    grad_out[...] = jnp.concatenate([q_part, k_part, v_part], axis=1).astype(LOW)


def self_project_back(table, grad_q, k, v, raw, own_fold, other_fold):
    tokens, columns = k.shape
    rows = tokens // 2
    row = lambda c: pl.BlockSpec((rows, c), lambda i, t: (i, 0))
    fixed = pl.BlockSpec((columns, LANES), lambda i, t: (0, 0))
    return call(
        self_project_back_body,
        "self_project_back",
        [((tokens, 3 * columns), LOW)],
        (grad_q, k, v, raw, own_fold, other_fold),
        grid=(tokens // rows,),
        in_specs=[row(columns), row(columns), row(columns), row(2 * columns), fixed, fixed],
        out_specs=[row(3 * columns)],
        scratch=[pltpu.VMEM((2, 2, columns, columns), LOW)] * 2,
        flops=16 * tokens * columns * columns,
        table=table,
    )[0]


def live_keys(table, own, keys):
    place = lax.broadcasted_iota(jnp.int32, (1, keys), 1)
    return place < jnp.where(own, table[OWN_LENGTH], table[OTHER_LENGTH])


def shard_of(first, rest, step, which):
    rows = first.shape[0]
    return first[...] if step == 0 else rest[step - 1, which * rows : (which + 1) * rows, :]


def middle_body(table, att, x, mod_own, mod_other, out_first, query_first, cross_first, *refs):
    pieces, (kv_own, kv_other) = refs[:8], refs[8:10]
    branch, after_low, queries_out, probs_out, text_out, after_cross, normed, rest = refs[10:]
    put_in_order(table, pieces, rest)
    count, rows, columns = att.shape
    keys = kv_own.shape[1]
    heads = columns // CROSS_HEAD
    own = own_image(table, table[BLOCK_FIRST], rows)
    y1 = jnp.zeros((rows, x.shape[1]), WIDE)
    for step in range(count):
        y1 += dot(att[turned(table, step, count)], shard_of(out_first, rest, step, 0))
    branch[...] = y1
    x1 = x[...].astype(WIDE) + pick(own, mod_own, mod_other, 2) * y1
    x1_low = x1.astype(LOW)
    after_low[...] = x1_low
    live = live_keys(table, own, keys)
    yc = jnp.zeros_like(x1)
    for step in range(count):
        queries = times_transposed(x1_low, shard_of(query_first, rest, step, 1)).astype(LOW)
        queries_out[step] = queries
        place = turned(table, step, count)
        mine, theirs = kv_own[place], kv_other[place]
        parts = []
        for head in range(heads):
            lanes = slice(head * CROSS_HEAD, (head + 1) * CROSS_HEAD)
            wide_lanes = slice(columns + head * CROSS_HEAD, columns + (head + 1) * CROSS_HEAD)
            q = queries[:, lanes]
            scores = jnp.where(
                own, times_transposed(q, mine[:, lanes]), times_transposed(q, theirs[:, lanes])
            ) * (1.0 / math.sqrt(CROSS_HEAD))
            scores = jnp.where(live, scores, MASKED_OUT)
            raised = jnp.exp(scores - jnp.max(scores, axis=-1, keepdims=True))
            probs = raised / jnp.sum(raised, axis=-1, keepdims=True)
            probs_out[step * heads + head] = probs
            low = probs.astype(LOW)
            parts.append(
                jnp.where(own, dot(low, mine[:, wide_lanes]), dot(low, theirs[:, wide_lanes]))
            )
        text = jnp.concatenate(parts, axis=1).astype(LOW)
        text_out[step] = text
        yc += dot(text, shard_of(cross_first, rest, step, 2))
    x2 = x1 + yc
    after_cross[...] = x2
    normed[...] = (
        x2 * inverse_size(x2) * (1.0 + pick(own, mod_own, mod_other, 4))
        + pick(own, mod_own, mod_other, 3)
    ).astype(LOW)


def middle_back_body(table, grad_own, grad_1, grad_2, grad_3, x2_in, upstream, branch, mod_own, mod_other, out_first, query_first, cross_first, rest, kv_own, kv_other, probs_in, queries_in, cross_grad, query_grad, attn_grad, attended_grad, after_grad, sums, kv_own_grad, kv_other_grad):
    count, rows, columns = queries_in.shape
    keys = kv_own.shape[1]
    heads = columns // CROSS_HEAD
    scale = 1.0 / math.sqrt(CROSS_HEAD)
    own = own_image(table, table[BLOCK_FIRST], rows)
    grad = with_own(grad_own, grad_1, grad_2, grad_3)
    x2 = x2_in[...]
    inverse = inverse_size(x2)
    xh = x2 * inverse
    sums[0:1], sums[1:2] = both_sums(own, grad)
    sums[2:3], sums[3:4] = both_sums(own, grad * xh)
    e = grad * (1.0 + pick(own, mod_own, mod_other, 4))
    dx2 = upstream[...].astype(WIDE) + inverse * (
        e - xh * jnp.mean(e * xh, axis=-1, keepdims=True)
    )
    dyc = dx2.astype(LOW)
    cross_grad[...] = dyc
    dx1 = dx2
    for step in range(count):
        doc = times_transposed(dyc, shard_of(cross_first, rest, step, 2)).astype(LOW)
        place = turned(table, step, count)
        mine, theirs = kv_own[place], kv_other[place]
        queries = queries_in[step]
        query_parts = []
        key_parts = ([], [])
        value_parts = ([], [])
        for head in range(heads):
            lanes = slice(head * CROSS_HEAD, (head + 1) * CROSS_HEAD)
            wide_lanes = slice(columns + head * CROSS_HEAD, columns + (head + 1) * CROSS_HEAD)
            do, q = doc[:, lanes], queries[:, lanes]
            probs = probs_in[step * heads + head]
            dp = jnp.where(
                own,
                times_transposed(do, mine[:, wide_lanes]),
                times_transposed(do, theirs[:, wide_lanes]),
            )
            ds = (probs * (dp - jnp.sum(probs * dp, axis=-1, keepdims=True))).astype(LOW)
            low = probs.astype(LOW)
            zero = jnp.zeros_like(ds)
            query_parts.append(
                jnp.where(own, dot(ds, mine[:, lanes]), dot(ds, theirs[:, lanes])) * scale
            )
            for image in range(2):
                mask = (lambda a: jnp.where(own, a, zero)) if image == 0 else (
                    lambda a: jnp.where(own, zero, a)
                )
                key_parts[image].append(over_tokens(mask(ds), q) * scale)
                value_parts[image].append(over_tokens(mask(low), do))
        dqc = jnp.concatenate(query_parts, axis=1).astype(LOW)
        query_grad[step] = dqc
        kv_own_grad[place] = jnp.concatenate(key_parts[0] + value_parts[0], axis=1).astype(LOW)
        kv_other_grad[place] = jnp.concatenate(key_parts[1] + value_parts[1], axis=1).astype(LOW)
        dx1 = dx1 + dot(dqc, shard_of(query_first, rest, step, 1))
    after_grad[...] = dx1
    sums[4:5], sums[5:6] = both_sums(own, dx1 * branch[...])
    sums[6:8] = jnp.zeros((2, sums.shape[1]), WIDE)
    dy1 = (dx1 * pick(own, mod_own, mod_other, 2)).astype(LOW)
    attn_grad[...] = dy1
    for step in range(count):
        attended_grad[turned(table, step, count)] = times_transposed(
            dy1, shard_of(out_first, rest, step, 0)
        ).astype(LOW)


def first_norm_back_body(table, grad_own, grad_1, grad_2, grad_3, after_grad, x, mod_own, mod_other, input_grad, sums):
    rows = x.shape[0]
    own = own_image(table, table[BLOCK_FIRST], rows)
    grad = with_own(grad_own, grad_1, grad_2, grad_3)
    wide = x[...].astype(WIDE)
    inverse = inverse_size(wide)
    xh = wide * inverse
    sums[0:1], sums[1:2] = both_sums(own, grad)
    sums[2:3], sums[3:4] = both_sums(own, grad * xh)
    sums[4:8] = jnp.zeros((4, sums.shape[1]), WIDE)
    e = grad * (1.0 + pick(own, mod_own, mod_other, 1))
    input_grad[...] = (
        after_grad[...] + inverse * (e - xh * jnp.mean(e * xh, axis=-1, keepdims=True))
    ).astype(LOW)


def output_body(table, branches, x2, upstream, mod_own, mod_other, output, sums):
    rows = x2.shape[0]
    own = own_image(table, table[BLOCK_FIRST], rows)
    branch = total(branches)
    sums[0:1], sums[1:2] = both_sums(own, upstream[...].astype(WIDE) * branch)
    sums[2:8] = jnp.zeros((6, sums.shape[1]), WIDE)
    output[...] = (x2[...] + pick(own, mod_own, mod_other, 5) * branch).astype(LOW)


def up_body(table, *refs):
    blocks, weight, (wide_out, low_out, ordered) = refs[:-4], refs[-4], refs[-3:]
    rows = blocks[0].shape[0]

    @pl.when(pl.program_id(0) == 0)
    def _():
        for step, block in enumerate(blocks):
            low = turned(table, step, len(blocks)) * rows
            ordered[pl.ds(pl.multiple_of(low, 16), rows), :] = block[...]

    up = times_transposed(ordered[...], weight[...])
    wide_out[...] = up
    low_out[...] = (up * logistic(up)).astype(LOW)


def up_project(table, blocks, weight):
    rows, width = blocks[0].shape
    tokens = len(blocks) * rows
    columns = 3 * LANES
    whole = lambda *shape: pl.BlockSpec(shape, lambda i, t: (0, 0))
    column = pl.BlockSpec((tokens, columns), lambda i, t: (0, i))
    return call(
        up_body,
        "up_project",
        [((tokens, weight.shape[0]), WIDE), ((tokens, weight.shape[0]), LOW), ((tokens, width), LOW)],
        (*blocks, weight),
        grid=(weight.shape[0] // columns,),
        in_specs=[whole(rows, width)] * len(blocks)
        + [pl.BlockSpec((columns, width), lambda i, t: (i, 0))],
        out_specs=[column, column, whole(tokens, width)],
        table=table,
    )


def fill(padded, block, rim):
    tokens = block.shape[0]
    edge = rim[...].astype(WIDE)
    padded[0:MAXW, :] = edge
    padded[MAXW : MAXW + tokens, :] = block.astype(WIDE)
    padded[MAXW + tokens : 2 * MAXW + tokens, :] = edge


def fill_masks(table, masks):
    tokens = masks.shape[1]
    place = table[FIRST] + lax.broadcasted_iota(jnp.int32, (tokens, LANES), 0)
    width = table[WIDTH]
    cut = table[CUT]
    late = place >= cut
    start = jnp.where(late, cut, 0)
    end = jnp.where(late, table[SEQ_TOKENS], cut)
    column = lax.bitwise_and(place, width - 1)
    one, none = jnp.ones((tokens, LANES), WIDE), jnp.zeros((tokens, LANES), WIDE)
    masks[0] = jnp.where(place - width >= start, one, none)
    masks[1] = jnp.where(place + width < end, one, none)
    masks[2] = jnp.where(column > 0, one, none)
    masks[3] = jnp.where(column < width - 1, one, none)


CHUNK = 64


def three_rows(table, padded, masks, low):
    width = table[WIDTH]
    above = padded[pl.ds(pl.multiple_of(MAXW + low - width, 16), CHUNK), :]
    below = padded[pl.ds(pl.multiple_of(MAXW + low + width, 16), CHUNK), :]
    own = padded[pl.ds(pl.multiple_of(MAXW + low, 16), CHUNK), :]
    rows = pl.ds(pl.multiple_of(low, 16), CHUNK)
    return above * masks[0, rows, :], own, below * masks[1, rows, :]


def nine_taps(rows, taps, left_mask, right_mask):
    mixed = [sum(rows[a] * taps[a][b] for a in range(3)) for b in range(3)]
    return (
        mixed[1]
        + left_mask * pltpu.roll(mixed[0], 1, 0)
        + right_mask * pltpu.roll(mixed[2], CHUNK - 1, 0)
    )


def taps_of(taps, flip):
    read = lambda a, b: taps[3 * a + b : 3 * a + b + 1, :]
    return [[read(2 - a, 2 - b) if flip else read(a, b) for b in range(3)] for a in range(3)]


def mix_body(table, value, gate, value_rim, gate_rim, value_taps, gate_taps, grad_hidden, hidden, grads, value_pad, gate_pad, masks):
    @pl.when(pl.program_id(0) == 0)
    def _():
        fill_masks(table, masks)

    fill(value_pad, value[...], value_rim)
    fill(gate_pad, gate[...], gate_rim)
    value_weights, gate_weights = taps_of(value_taps, False), taps_of(gate_taps, False)

    @pl.loop(0, value.shape[0] // CHUNK)
    def _(index):
        low = index * CHUNK
        rows = pl.ds(pl.multiple_of(low, CHUNK), CHUNK)
        left, right = masks[2, rows, :], masks[3, rows, :]
        mv = nine_taps(three_rows(table, value_pad, masks, low), value_weights, left, right)
        mg = nine_taps(three_rows(table, gate_pad, masks, low), gate_weights, left, right)
        sigma = logistic(mg)
        gated = mg * sigma
        hidden[rows, :] = (mv * gated).astype(LOW)
        dh = grad_hidden[rows, :]
        grads[0, rows, :] = (dh * gated).astype(LOW)
        grads[1, rows, :] = (dh * mv * (sigma * (1.0 + mg * (1.0 - sigma)))).astype(LOW)


def mix(table, activated, rim, taps, grad_hidden):
    tokens, wide = activated.shape
    columns = wide // 2
    tiles = columns // LANES
    block = lambda r, shift: pl.BlockSpec((r, LANES), lambda i, t: (0, i + shift))
    pad = pltpu.VMEM((tokens + 2 * MAXW, LANES), WIDE)
    return call(
        mix_body,
        "mix",
        [((tokens, columns), LOW), ((2, tokens, columns), LOW)],
        (activated, activated, rim, rim, taps, taps, grad_hidden),
        grid=(tiles,),
        in_specs=[
            block(tokens, 0),
            block(tokens, tiles),
            block(MAXW, 0),
            block(MAXW, tiles),
            block(taps.shape[0], 0),
            block(taps.shape[0], tiles),
            block(tokens, 0),
        ],
        out_specs=[
            block(tokens, 0),
            pl.BlockSpec((2, tokens, LANES), lambda i, t: (0, 0, i)),
        ],
        scratch=[pad, pad, pltpu.VMEM((4, tokens, LANES), WIDE)],
        flops=6000 * tokens * columns // 2,
        table=table,
    )


def mix_back_body(table, grads, grads_rim, activated, rim, taps, up, grad_up, tap_grads, grad_pad, act_pad, masks):
    @pl.when(pl.program_id(0) == 0)
    def _():
        fill_masks(table, masks)

    fill(grad_pad, grads[0], grads_rim.at[0])
    fill(act_pad, activated[...], rim)
    weights = taps_of(taps, True)

    def step(index, sums):
        low = index * CHUNK
        rows = pl.ds(pl.multiple_of(low, CHUNK), CHUNK)
        left, right = masks[2, rows, :], masks[3, rows, :]
        mine = three_rows(table, grad_pad, masks, low)
        dact = nine_taps(mine, weights, left, right)
        given = up[rows, :]
        sigma = logistic(given)
        grad_up[rows, :] = (dact * (sigma * (1.0 + given * (1.0 - sigma)))).astype(LOW)
        acts = three_rows(table, act_pad, masks, low)
        turned = (
            right * pltpu.roll(mine[1], CHUNK - 1, 0),
            mine[1],
            left * pltpu.roll(mine[1], 1, 0),
        )
        return tuple(
            sums[3 * a + b]
            + jnp.sum((acts[a] * turned[b]).reshape(CHUNK // 8, 8, LANES), axis=0)
            for a in range(3)
            for b in range(3)
        )

    zero = jnp.zeros((8, LANES), WIDE)
    sums = lax.fori_loop(0, activated.shape[0] // CHUNK, step, (zero,) * 9)
    for tap in range(9):
        tap_grads[tap : tap + 1, :] = jnp.sum(sums[tap], axis=0, keepdims=True)
    tap_grads[9:16, :] = jnp.zeros((7, LANES), WIDE)


def mix_back(table, grads, grads_rim, activated, rim, taps, up):
    tokens, wide = activated.shape
    columns = wide // 2
    tiles = columns // LANES
    block = lambda r: pl.BlockSpec((r, LANES), lambda i, t: (0, i))
    half = lambda r: pl.BlockSpec(
        (1, r, LANES), lambda i, t: (lax.div(i, tiles), 0, lax.rem(i, tiles))
    )
    pad = pltpu.VMEM((tokens + 2 * MAXW, LANES), WIDE)
    return call(
        mix_back_body,
        "mix_back",
        [((tokens, wide), LOW), ((16, wide), WIDE)],
        (grads, grads_rim, activated, rim, taps, up),
        grid=(2 * tiles,),
        in_specs=[half(tokens), half(MAXW), block(tokens), block(MAXW), block(taps.shape[0]), block(tokens)],
        out_specs=[block(tokens), block(16)],
        scratch=[pad, pad, pltpu.VMEM((4, tokens, LANES), WIDE)],
        flops=6000 * tokens * columns,
        table=table,
    )


def eighth_body(table, *refs):
    weights, out, joined = refs[:-2], refs[-2], refs[-1]
    low = 0
    for weight in weights:
        joined[low : low + weight.shape[0], :] = weight[...]
        low += weight.shape[0]
    rows = out.shape[0]
    out[...] = joined[pl.ds(pl.multiple_of(table[0] * rows, 16), rows), :]


def put_in_order(table, pieces, out):
    steps, rows = pieces[0].shape[0], pieces[0].shape[1]
    for place, piece in enumerate(pieces):
        block = lax.bitwise_xor(table[ROW_PLACE], place)
        for step in range(steps):
            out[step, pl.ds(pl.multiple_of(block * rows, 16), rows), :] = piece[step]


def after(value, *others):
    return lax.optimization_barrier((value, others))[0]


def fetch_eighths(weights):
    columns = weights[0].shape[1]
    rows = -(-sum(weight.shape[0] for weight in weights) // LANES) * 16
    eighth = call(
        eighth_body,
        "eighth",
        [((rows, columns), weights[0].dtype)],
        weights,
        scratch=[pltpu.VMEM((8 * rows, columns), weights[0].dtype)],
        table=(lax.axis_index("seq") % 8).reshape(1).astype(jnp.int32),
    )[0]
    return jnp.stack([from_behind(eighth, step) for step in range(1, lax.axis_size("tp"))])


def share_eighths(fetched, ready):
    count = lax.axis_size("seq")
    far = lambda flip: lax.ppermute(fetched, "seq", [(k, k ^ flip) for k in range(count)])
    pieces = []
    for piece in [fetched] + after([far(2), far(4), far(6)], *ready):
        pieces += [piece, swapped(piece, "seq", 0)]
    return pieces


def token_block(values, place):
    count = lax.axis_size("tp")
    size = values.shape[0] // count
    return lax.dynamic_slice_in_dim(values, (place % count) * size, size, 0)


def own_rows(values):
    rows = values.shape[0] // lax.axis_size("tp")
    return pl.BlockSpec((rows, values.shape[1]), lambda i, t: (t[TP_PLACE], 0))


def placed_blocks(blocks):
    count = len(blocks)
    place = lax.axis_index("tp")
    result = jnp.zeros((count,) + blocks[0].shape, blocks[0].dtype)
    for step in range(count):
        result = lax.dynamic_update_index_in_dim(result, blocks[step], (place - step) % count, 0)
    return result.reshape((count * blocks[0].shape[0],) + blocks[0].shape[1:])


def all_blocks(block):
    return [block] + [from_behind(block, step) for step in range(1, lax.axis_size("tp"))]


def product(left, right):
    count = lax.axis_size("tp")
    return dot(left, right).astype(LOW).reshape(count, left.shape[0] // count, right.shape[1])


def spread(blocks):
    count = lax.axis_size("tp")
    place = lax.axis_index("tp")
    return [
        from_behind(
            lax.dynamic_index_in_dim(blocks, (place + step) % count, 0, keepdims=False), step
        )
        for step in range(1, count)
    ]


def own_block(blocks):
    return pl.BlockSpec((1,) + blocks.shape[1:], lambda i, t: (t[TP_PLACE], 0, 0))


def with_own(own, *others):
    result = own[0].astype(WIDE)
    for other in others:
        result += other[...].astype(WIDE)
    return result


def total(parts):
    result = parts[0].astype(WIDE)
    for place in range(1, parts.shape[0]):
        result += parts[place].astype(WIDE)
    return result


def turned(table, step, count):
    return lax.rem(table[TP_PLACE] + count - step, count)


def same_everywhere(block):
    count = lax.axis_size("tp")
    flipped = lambda flip: lax.ppermute(block, "tp", [(k, k ^ flip) for k in range(count)])
    return (block + flipped(1)) + (flipped(2) + flipped(3))


def sum_rows(grad):
    return lax.optimization_barrier(
        lax.psum_scatter(grad.astype(LOW), "seq", scatter_dimension=0, tiled=True)
    )


def square_body(table, dyc, text, x1, dqc, dy1, att, kv_mine, kv_theirs, out, kv_out):
    kv_out[...] = (kv_mine[...].astype(WIDE) + kv_theirs[...].astype(WIDE)).astype(LOW)
    parts = [
        over_tokens(left[...], right[0]) for left, right in ((dyc, text), (x1, dqc), (dy1, att))
    ]
    rest = out.shape[1] - sum(part.shape[1] for part in parts)
    if rest:
        parts.append(jnp.zeros((out.shape[0], rest), WIDE))
    out[...] = jnp.concatenate(parts, axis=1).astype(LOW)


def square_parts(table, lefts, rights, kv_mine, kv_theirs):
    rows, width = lefts[0].shape
    count, _, columns = rights[0].shape
    block = -(-3 * columns // LANES) * LANES
    whole = pl.BlockSpec((rows, width), lambda i, t: (0, 0))
    one = pl.BlockSpec((1, rows, columns), lambda i, t: (turned(t, i, count), 0, 0))
    still = pl.BlockSpec((1, rows, columns), lambda i, t: (i, 0, 0))
    kv = pl.BlockSpec((1,) + kv_mine.shape[1:], lambda i, t: (i, 0, 0))
    return call(
        square_body,
        "square_parts",
        [((width, count * block), LOW), (kv_mine.shape, LOW)],
        [array for pair in zip(lefts, rights) for array in pair] + [kv_mine, kv_theirs],
        grid=(count,),
        in_specs=[whole, one, whole, one, whole, still, kv, kv],
        out_specs=[pl.BlockSpec((width, block), lambda i, t: (0, i)), kv],
        table=table,
    )


def ffn_body(table, grad_ffn, hidden, normed, grad_up, out):
    step = pl.program_id(0)

    @pl.when(step == 0)
    def _():
        out[...] = over_tokens(grad_ffn[...], hidden[...]).astype(LOW)

    @pl.when(step > 0)
    def _():
        out[...] = over_tokens(normed[...], grad_up[...]).astype(LOW)


def ffn_parts_of(table, grad_ffn, hidden, normed, grad_up):
    tokens, width = normed.shape
    columns = hidden.shape[1]
    whole = pl.BlockSpec((tokens, width), lambda i, t: (0, 0))
    return call(
        ffn_body,
        "ffn_parts",
        [((width, 3 * columns), LOW)],
        (grad_ffn, hidden, normed, grad_up),
        grid=(3,),
        in_specs=[
            whole,
            pl.BlockSpec((tokens, columns), lambda i, t: (0, 0)),
            whole,
            pl.BlockSpec((tokens, columns), lambda i, t: (0, jnp.maximum(i - 1, 0))),
        ],
        out_specs=[pl.BlockSpec((width, columns), lambda i, t: (0, i))],
        table=table,
    )[0]


def late_body(table, normed, grad_projected, text, kv_grads, out):
    first = over_tokens(normed[...], grad_projected[...]).astype(LOW)
    second = over_tokens(text[...], total(kv_grads).astype(LOW)).astype(LOW)
    out[...] = jnp.concatenate([first, second], axis=1)


def shards(
    hidden_in,
    cotangent,
    modulation,
    text_states,
    image_shapes,
    text_lengths,
    qkv_weight,
    attn_out_weight,
    cross_q_weight,
    cross_kv_weight,
    cross_out_weight,
    up_weight,
    conv_weight,
    down_weight,
):
    tokens_here, width = hidden_in.shape
    context = text_states.shape[1]
    keys = -(-context // 16) * 16
    self_cols = qkv_weight.shape[2]
    cross_cols = cross_q_weight.shape[1]
    ffn_cols = up_weight.shape[2]
    ffn_pad = -(-ffn_cols // LANES) * LANES
    count = lax.axis_size("tp")
    tp_index = lax.axis_index("tp")
    block_size = tokens_here // count
    seq_index = lax.axis_index("seq")
    side = seq_index % 2
    first_half = side == 0
    pair = seq_index - side
    pair_shapes = lax.dynamic_slice_in_dim(image_shapes, pair, 2, 0)
    row_width = pair_shapes[0, 1]
    lengths = lax.dynamic_slice_in_dim(text_lengths, pair, 2, 0)
    first_place = side * tokens_here
    table = jnp.stack(
        [
            first_place,
            pair_shapes[0, 0] * row_width,
            side,
            row_width,
            jnp.where(first_half, lengths[0], lengths[1]),
            jnp.where(first_half, lengths[1], lengths[0]),
            first_place + tp_index * block_size,
            jnp.int32(2 * tokens_here),
            tp_index,
            seq_index % 8,
        ]
    ).astype(jnp.int32)

    mod_own = modulation[0]
    mod_other = swapped(mod_own, "seq", 0).astype(WIDE)
    mod_own = mod_own.astype(WIDE)
    weights = [attn_out_weight.T, cross_q_weight.T, cross_out_weight.T]
    fetched = fetch_eighths(weights)
    qkv_flat = qkv_weight.transpose(1, 2, 0).reshape(3 * self_cols, width)
    text_rows = jnp.pad(text_states[0], ((0, keys - context), (0, 0)))
    kv_here = times_transposed(
        text_rows, cross_kv_weight.transpose(1, 2, 0).reshape(2 * cross_cols, width)
    ).astype(LOW)
    kv_sent_first = jnp.broadcast_to(kv_here[None], (count,) + kv_here.shape)
    normed_low, raw, q, k, v, part_own, part_other = self_project(
        table, after(hidden_in, kv_sent_first), mod_own, mod_other, qkv_flat, self_cols
    )
    theirs = swapped(jnp.stack([part_own, part_other]), "seq", 0)
    fetched = after(fetched, q)
    kernel_own, kernel_other = part_own + theirs[1], part_other + theirs[0]
    attended, attended_wide, denominator = self_attend(
        table, after(q, kv_here), kernel_own, kernel_other
    )

    whole = pl.BlockSpec(memory_space=pltpu.VMEM)
    x_rows, upstream_rows = own_rows(hidden_in), own_rows(cotangent)
    up_flat = jnp.pad(
        after(up_weight.transpose(1, 2, 0), attended), ((0, 0), (0, ffn_pad - ffn_cols), (0, 0))
    ).reshape(2 * ffn_pad, width)
    down_flat = jnp.pad(after(down_weight.T, attended), ((0, ffn_pad - ffn_cols), (0, 0)))
    taps = (
        jnp.pad(conv_weight, ((0, 7), (0, 0), (0, ffn_pad - ffn_cols)))
        .reshape(16, 2 * ffn_pad)
        .astype(WIDE)
    )
    gate_rows = jnp.where(
        (first_place + jnp.arange(tokens_here, dtype=jnp.int32) >= table[CUT])[:, None] == (side == 1),
        mod_own[5:6],
        mod_other[5:6],
    )
    grad_ffn = (cotangent.astype(WIDE) * gate_rows).astype(LOW)
    grad_hidden = times_transposed(grad_ffn, down_flat)
    ready = (up_flat, down_flat, taps, grad_hidden)
    split_tokens = lambda values: values.reshape(count, block_size, values.shape[1])
    kv_own = exchanged(kv_sent_first)
    attended_blocks = exchanged(after(split_tokens(attended), kv_own))
    kv_own = after(kv_own, *ready)
    kv_other = swapped(kv_own, "seq", 0)
    pieces = share_eighths(fetched, (*ready, attended_blocks))
    all_heads = count * cross_cols // CROSS_HEAD
    branch, after_low, queries, probs, text_low, after_cross, normed_two, rest = call(
        middle_body,
        "middle",
        [
            ((block_size, width), WIDE),
            ((block_size, width), LOW),
            ((count, block_size, cross_cols), LOW),
            ((all_heads, block_size, keys), WIDE),
            ((count, block_size, cross_cols), LOW),
            ((block_size, width), WIDE),
            ((block_size, width), LOW),
            ((count - 1, 8 * fetched.shape[1], width), LOW),
        ],
        (attended_blocks, hidden_in, mod_own, mod_other, *weights, *pieces, kv_own, kv_other),
        in_specs=[whole, x_rows] + [whole] * 15,
        flops=60 * block_size * width * width,
        table=table,
    )

    up_wide, activated, normed_two_low = up_project(table, all_blocks(normed_two), up_flat)
    rim = swapped(jnp.where(first_half, activated[-MAXW:], activated[:MAXW]), "seq", 0)
    hidden, grads = mix(table, activated, rim, taps, grad_hidden)
    grads_rim = swapped(jnp.where(first_half, grads[:, -MAXW:], grads[:, :MAXW]), "seq", 0)
    branch_sent = product(hidden, down_flat)
    grad_up, tap_part = mix_back(
        table, grads, grads_rim, activated, rim, taps, after(up_wide, branch_sent)
    )
    branches = exchanged(branch_sent)
    norm_two_sent = product(grad_up, up_flat)
    grad_norm_two = spread(norm_two_sent)
    output_block, output_sums = call(
        output_body,
        "output",
        [((block_size, width), LOW), ((8, width), WIDE)],
        (branches, after_cross, cotangent, mod_own, mod_other),
        in_specs=[whole, whole, upstream_rows, whole, whole],
        table=table,
    )
    ffn_parts = ffn_parts_of(
        table, grad_ffn, after(hidden, norm_two_sent, output_block), normed_two_low, grad_up
    )
    ffn_rows = sum_rows(after(ffn_parts, grad_norm_two))
    output_blocks = all_blocks(after(output_block, grad_norm_two))

    (
        cross_grad,
        query_grad,
        attn_grad,
        attended_grad,
        after_grad,
        middle_sums,
        kv_own_grad,
        kv_other_grad,
    ) = call(
        middle_back_body,
        "middle_back",
        [
            ((block_size, width), LOW),
            ((count, block_size, cross_cols), LOW),
            ((block_size, width), LOW),
            ((count, block_size, self_cols), LOW),
            ((block_size, width), WIDE),
            ((8, width), WIDE),
            ((count, keys, 2 * cross_cols), LOW),
            ((count, keys, 2 * cross_cols), LOW),
        ],
        (
            after(norm_two_sent, ffn_parts, output_block),
            *grad_norm_two,
            after_cross,
            cotangent,
            branch,
            mod_own,
            mod_other,
            *weights,
            rest,
            kv_own,
            kv_other,
            probs,
            queries,
        ),
        in_specs=[own_block(norm_two_sent)] + [whole] * 4 + [upstream_rows] + [whole] * 11,
        flops=120 * block_size * width * width,
        table=table,
    )

    grad_blocks = exchanged(after(attended_grad, output_blocks))
    kv_theirs = swapped(after(kv_other_grad, output_blocks), "seq", 0)
    squares, kv_sent = square_parts(
        table,
        (cross_grad, after_low, attn_grad),
        (text_low, query_grad, after(attended_blocks, attended_grad)),
        kv_own_grad,
        kv_theirs,
    )
    square_rows = sum_rows(after(squares, grad_blocks))
    kv_sent = after(kv_sent, grad_blocks)
    kv_parts = exchanged(kv_sent)
    grad_blocks = after(grad_blocks, squares, kv_sent, ffn_rows)
    grad_q, back_own, back_other = self_back(
        table, grad_blocks, q, attended_wide, denominator, kernel_own, kernel_other
    )
    back_theirs = swapped(jnp.stack([back_own, back_other]), "seq", 0)
    grad_projected = self_project_back(
        table,
        grad_q,
        k,
        v,
        raw,
        back_own + back_theirs[1],
        back_other + back_theirs[0],
    )
    normed_sent = product(grad_projected, qkv_flat)
    grad_normed = spread(normed_sent)
    late_parts = call(
        late_body,
        "late_parts",
        [((width, 3 * self_cols + 2 * cross_cols), LOW)],
        (normed_low, after(grad_projected, normed_sent), text_rows, kv_parts),
        table=table,
    )[0]
    late_rows = sum_rows(after(late_parts, square_rows, grad_normed))
    conv_sum = after(tap_part[:9], normed_sent)
    for place in range(lax.axis_size("seq").bit_length() - 1):
        conv_sum = conv_sum + swapped(conv_sum, "seq", place)
    square_sent = square_rows.reshape(square_rows.shape[0], count, -1).transpose(1, 0, 2)
    input_block, first_sums = call(
        first_norm_back_body,
        "first_norm_back",
        [((block_size, width), LOW), ((8, width), WIDE)],
        (
            after(normed_sent, late_parts, square_sent),
            *grad_normed,
            after_grad,
            hidden_in,
            mod_own,
            mod_other,
        ),
        in_specs=[own_block(normed_sent)] + [whole] * 4 + [x_rows, whole, whole],
        table=table,
    )
    square_parts_here = exchanged(square_sent)
    square_grads = total(square_parts_here)[:, : 3 * self_cols]
    pairs = jnp.concatenate([first_sums[:4], middle_sums[4:6], middle_sums[:4], output_sums[:2]])
    pairs = pairs.reshape(6, 2, width)
    pairs = pairs[:, 0] + swapped(pairs[:, 1], "seq", 0)
    modulation_grad = same_everywhere(pairs)
    input_block = after(input_block, square_parts_here, modulation_grad)
    late_rows = late_rows.astype(WIDE)
    qkv_grad = late_rows[:, : 3 * self_cols].reshape(-1, 3, self_cols)
    ckv_grad = late_rows[:, 3 * self_cols :].reshape(-1, 2, cross_cols)
    output = placed_blocks(output_blocks)
    input_blocks = after(all_blocks(input_block), qkv_grad, ckv_grad, square_grads, output)
    input_grad = placed_blocks(input_blocks).astype(WIDE)

    return (
        output,
        input_grad,
        modulation_grad[None],
        qkv_grad,
        square_grads[:, 2 * self_cols :],
        square_grads[:, self_cols : 2 * self_cols],
        ckv_grad,
        square_grads[:, :self_cols],
        ffn_rows[:, ffn_pad:].astype(WIDE).reshape(-1, 2, ffn_pad)[:, :, :ffn_cols],
        conv_sum.reshape(9, 2, ffn_pad)[:, :, :ffn_cols],
        ffn_rows[:, :ffn_cols].astype(WIDE),
    )


def solution(mesh):
    placed = (
        P("seq", None),
        P("seq", None),
        P("seq", None, None),
        P("seq", None, None),
        P(),
        P(),
        P(None, None, "tp"),
        P(None, "tp"),
        P(None, "tp"),
        P(None, None, "tp"),
        P(None, "tp"),
        P(None, None, "tp"),
        P(None, None, "tp"),
        P(None, "tp"),
    )
    return jax.shard_map(
        shards,
        mesh=mesh,
        in_specs=placed,
        out_specs=(
            P("seq", None),
            P("seq", None),
            P("seq", None, None),
            P("seq", None, "tp"),
            P("seq", "tp"),
            P("seq", "tp"),
            P("seq", None, "tp"),
            P("seq", "tp"),
            P("seq", None, "tp"),
            P(None, None, "tp"),
            P("seq", "tp"),
        ),
        check_vma=False,
    )
```

```python
import functools
import math

import jax
import jax.numpy as jnp
from jax import lax
from jax.experimental import pallas as pl
from jax.experimental.pallas import tpu as pltpu
from jax.sharding import PartitionSpec as P

HEAD = 32
CROSS_HEAD = 72
MAXW = 32
LANES = 128
GRANT = 56 * 1024 * 1024

EPSILON = 1e-06
MASKED_OUT = -1e30
LOW = jnp.bfloat16
WIDE = jnp.float32

FIRST, CUT, SIDE, WIDTH, OWN_LENGTH, OTHER_LENGTH, BLOCK_FIRST, SEQ_TOKENS, TP_PLACE, ROW_PLACE = range(10)


def swapped(block, axis, apart):
    count = lax.axis_size(axis)
    route = [(low, low ^ (1 << apart)) for low in range(count)]
    return lax.ppermute(block, axis, route)


def from_behind(block, step):
    count = lax.axis_size("tp")
    return lax.ppermute(block, "tp", [(k, (k + step) % count) for k in range(count)])


def exchanged(blocks):
    return lax.all_to_all(blocks, "tp", 0, 0, tiled=True)


def dot(left, right):
    return jnp.dot(left, right, preferred_element_type=WIDE)


def times_transposed(left, right):
    return lax.dot_general(left, right, (((1,), (1,)), ((), ())), preferred_element_type=WIDE)


def over_tokens(left, right):
    return lax.dot_general(left, right, (((0,), (0,)), ((), ())), preferred_element_type=WIDE)


def split(wide):
    high = wide.astype(LOW)
    return high, (wide - high.astype(WIDE)).astype(LOW)


def call(body, name, outs, arrays, *, grid=None, in_specs=None, out_specs=None, scratch=(), flops=0, table=None):
    shapes = tuple(jax.ShapeDtypeStruct(*out) for out in outs)
    size = sum(math.prod(a.shape) * a.dtype.itemsize for a in (*arrays, *shapes))
    whole = pl.BlockSpec(memory_space=pltpu.VMEM)
    return pl.pallas_call(
        body,
        out_shape=shapes,
        grid_spec=pltpu.PrefetchScalarGridSpec(
            num_scalar_prefetch=1,
            grid=grid or (1,),
            in_specs=in_specs or [whole] * len(arrays),
            out_specs=out_specs or [whole] * len(shapes),
            scratch_shapes=list(scratch),
        ),
        compiler_params=pltpu.CompilerParams(vmem_limit_bytes=GRANT),
        cost_estimate=pl.CostEstimate(flops=0, bytes_accessed=size // 100, transcendentals=0),
        name=name,
    )(table, *arrays)


def own_image(table, start, rows):
    place = start + lax.broadcasted_iota(jnp.int32, (rows, 1), 0)
    return (place >= table[CUT]).astype(jnp.int32) == table[SIDE]


def pick(own, own_rows, other_rows, row):
    return jnp.where(
        own, own_rows[row : row + 1, :].astype(WIDE), other_rows[row : row + 1, :].astype(WIDE)
    )


def inverse_size(wide):
    return lax.rsqrt(jnp.mean(wide * wide, axis=-1, keepdims=True) + EPSILON)


def both_sums(own, values):
    mine = jnp.sum(jnp.where(own, values, 0.0), axis=0, keepdims=True)
    return mine, jnp.sum(jnp.where(own, 0.0, values), axis=0, keepdims=True)


def same_head(rows, columns):
    row_head = lax.broadcasted_iota(jnp.int32, (rows, columns), 0) // HEAD
    return row_head == lax.broadcasted_iota(jnp.int32, (rows, columns), 1) // HEAD


def fold(square):
    size = square.shape[1]
    total = None
    for low in range(0, size, LANES):
        part = square[:, low : min(low + LANES, size)]
        if part.shape[1] < LANES:
            part = jnp.concatenate(
                [part, jnp.zeros((part.shape[0], LANES - part.shape[1]), part.dtype)], axis=1
            )
        total = part if total is None else total + part
    return total


def unfold(folded):
    size = folded.shape[0]
    parts = [folded[:, : min(LANES, size - low)] for low in range(0, size, LANES)]
    return jnp.where(same_head(size, size), jnp.concatenate(parts, axis=1), 0.0)


def packed(square, totals):
    keep = same_head(square.shape[0], square.shape[1])
    return fold(jnp.where(keep, square, 0.0)) + pltpu.roll(
        fold(jnp.where(keep, totals, 0.0)), HEAD, 1
    )


def unpacked(folded):
    return unfold(folded), unfold(pltpu.roll(folded, LANES - HEAD, 1))


def log_exp(wide):
    return jnp.maximum(wide, 0.0) + jnp.log1p(jnp.exp(-jnp.abs(wide)))


def logistic(wide):
    return 0.5 + 0.5 * jnp.tanh(0.5 * wide)


def self_project_body(table, x, mod_own, mod_other, weight, normed, raw, q, k, v, own_out, other_out, squares, totals):
    step = pl.program_id(0)
    rows, columns = q.shape
    own = own_image(table, table[FIRST] + step * rows, rows)
    wide = x[...].astype(WIDE)
    low = (
        wide * inverse_size(wide) * (1.0 + pick(own, mod_own, mod_other, 1))
        + pick(own, mod_own, mod_other, 0)
    ).astype(LOW)
    normed[...] = low
    out = times_transposed(low, weight[...])
    raw[...] = out[:, : 2 * columns]
    q[...] = log_exp(out[:, :columns]).astype(LOW)
    keys = log_exp(out[:, columns : 2 * columns]).astype(LOW)
    values = out[:, 2 * columns :].astype(LOW)
    k[...] = keys
    v[...] = values

    @pl.when(step == 0)
    def _():
        squares[...] = jnp.zeros_like(squares)
        totals[...] = jnp.zeros_like(totals)

    ones = jnp.ones((rows, columns), LOW)
    for image in range(2):
        zero = jnp.zeros_like(keys)
        masked = jnp.where(own, keys, zero) if image == 0 else jnp.where(own, zero, keys)
        squares[image] += over_tokens(masked, values)
        totals[image] += over_tokens(masked, ones)

    @pl.when(step == pl.num_programs(0) - 1)
    def _():
        own_out[...] = packed(squares[0], totals[0])
        other_out[...] = packed(squares[1], totals[1])


def self_project(table, x, mod_own, mod_other, weight, columns):
    tokens, width = x.shape
    rows = 128
    row = lambda c: pl.BlockSpec((rows, c), lambda i, t: (i, 0))
    fixed = lambda *s: pl.BlockSpec(s, lambda i, t: (0,) * len(s))
    return call(
        self_project_body,
        "self_project",
        [((tokens, width), LOW), ((tokens, 2 * columns), WIDE)]
        + [((tokens, columns), LOW)] * 3
        + [((columns, LANES), WIDE)] * 2,
        (x, mod_own, mod_other, weight),
        grid=(tokens // rows,),
        in_specs=[row(width), fixed(*mod_own.shape), fixed(*mod_own.shape), fixed(*weight.shape)],
        out_specs=[row(width), row(2 * columns)]
        + [row(columns)] * 3
        + [fixed(columns, LANES)] * 2,
        scratch=[pltpu.VMEM((2, columns, columns), WIDE)] * 2,
        flops=4 * tokens * width * 3 * columns,
        table=table,
    )


def keep_squares(kernels, key_totals, own_fold, other_fold):
    for image, folded in enumerate((own_fold, other_fold)):
        square, total = unpacked(folded[...])
        kernels[image, 0], kernels[image, 1] = split(square)
        key_totals[image, 0], key_totals[image, 1] = split(total)


def self_attend_body(table, q, own_fold, other_fold, attended, wide_out, denominator, kernels, key_totals):
    step = pl.program_id(0)
    rows = q.shape[0]

    @pl.when(step == 0)
    def _():
        keep_squares(kernels, key_totals, own_fold, other_fold)

    own = own_image(table, table[FIRST] + step * rows, rows)
    queries = q[...]

    def both(pair):
        own_part = dot(queries, pair[0, 0]) + dot(queries, pair[0, 1])
        return jnp.where(own, own_part, dot(queries, pair[1, 0]) + dot(queries, pair[1, 1]))

    under = both(key_totals) + 1.0
    out = both(kernels) / under
    attended[...] = out.astype(LOW)
    wide_out[...] = out
    denominator[...] = under


def self_attend(table, q, own_fold, other_fold):
    tokens, columns = q.shape
    rows = 128
    row = pl.BlockSpec((rows, columns), lambda i, t: (i, 0))
    fixed = pl.BlockSpec((columns, LANES), lambda i, t: (0, 0))
    return call(
        self_attend_body,
        "self_attend",
        [((tokens, columns), LOW), ((tokens, columns), WIDE), ((tokens, columns), WIDE)],
        (q, own_fold, other_fold),
        grid=(tokens // rows,),
        in_specs=[row, fixed, fixed],
        out_specs=[row, row, row],
        scratch=[pltpu.VMEM((2, 2, columns, columns), LOW)] * 2,
        flops=16 * tokens * columns * columns,
        table=table,
    )


def self_back_body(table, grad, q, wide_out, denominator, own_fold, other_fold, grad_q, own_out, other_out, kernels, key_totals, squares, totals):
    step = pl.program_id(0)
    rows, columns = q.shape

    @pl.when(step == 0)
    def _():
        keep_squares(kernels, key_totals, own_fold, other_fold)
        squares[...] = jnp.zeros_like(squares)
        totals[...] = jnp.zeros_like(totals)

    own = own_image(table, table[FIRST] + step * rows, rows)
    wide = grad[0].astype(WIDE)
    over = 1.0 / denominator[...]
    numer_high, numer_low = split(wide * over)
    ones = jnp.where(same_head(columns, columns), 1.0, 0.0).astype(LOW)
    high, low = split(wide * wide_out[...])
    denom = -(dot(high, ones) + dot(low, ones)) * over
    denom_high, denom_low = split(denom)

    def back(image):
        square, total = kernels[image, 0], key_totals[image, 0]
        through = (
            times_transposed(numer_high, square)
            + times_transposed(numer_low, square)
            + times_transposed(numer_high, kernels[image, 1])
        )
        totals_part = (
            times_transposed(denom_high, total)
            + times_transposed(denom_low, total)
            + times_transposed(denom_high, key_totals[image, 1])
        )
        return through + totals_part * (1.0 / HEAD)

    grad_q[...] = jnp.where(own, back(0), back(1))
    queries = q[...]
    zero = jnp.zeros_like(queries)
    for image in range(2):
        masked = jnp.where(own, queries, zero) if image == 0 else jnp.where(own, zero, queries)
        squares[image] += over_tokens(masked, numer_high) + over_tokens(masked, numer_low)
        totals[image] += over_tokens(masked, denom_high) + over_tokens(masked, denom_low)

    @pl.when(step == pl.num_programs(0) - 1)
    def _():
        own_out[...] = packed(squares[0], totals[0])
        other_out[...] = packed(squares[1], totals[1])


def self_back(table, grad, q, wide_out, denominator, own_fold, other_fold):
    count, rows, columns = grad.shape
    tokens = q.shape[0]
    row = pl.BlockSpec((rows, columns), lambda i, t: (i, 0))
    fixed = pl.BlockSpec((columns, LANES), lambda i, t: (0, 0))
    return call(
        self_back_body,
        "self_back",
        [((tokens, columns), WIDE)] + [((columns, LANES), WIDE)] * 2,
        (grad, q, wide_out, denominator, own_fold, other_fold),
        grid=(count,),
        in_specs=[pl.BlockSpec((1, rows, columns), lambda i, t: (i, 0, 0)), row, row, row, fixed, fixed],
        out_specs=[row, fixed, fixed],
        scratch=[pltpu.VMEM((2, 2, columns, columns), LOW)] * 2
        + [pltpu.VMEM((2, columns, columns), WIDE)] * 2,
        flops=48 * tokens * columns * columns,
        table=table,
    )


def self_project_back_body(table, grad_q, k, v, raw, own_fold, other_fold, grad_out, kernels, key_totals):
    step = pl.program_id(0)
    rows, columns = k.shape

    @pl.when(step == 0)
    def _():
        keep_squares(kernels, key_totals, own_fold, other_fold)

    own = own_image(table, table[FIRST] + step * rows, rows)
    keys, values = k[...], v[...]
    ones = jnp.ones((16, columns), LOW)

    def grad_k(image):
        total = times_transposed(ones, key_totals[image, 0]) + times_transposed(
            ones, key_totals[image, 1]
        )
        return (
            times_transposed(values, kernels[image, 0])
            + times_transposed(values, kernels[image, 1])
            + total[:1] * (1.0 / HEAD)
        )

    def grad_v(image):
        return dot(keys, kernels[image, 0]) + dot(keys, kernels[image, 1])

    given = raw[...]
    q_part = grad_q[...] * logistic(given[:, :columns])
    k_part = jnp.where(own, grad_k(0), grad_k(1)) * logistic(given[:, columns:])
    v_part = jnp.where(own, grad_v(0), grad_v(1))
    grad_out[...] = jnp.concatenate([q_part, k_part, v_part], axis=1).astype(LOW)


def self_project_back(table, grad_q, k, v, raw, own_fold, other_fold):
    tokens, columns = k.shape
    rows = 128
    row = lambda c: pl.BlockSpec((rows, c), lambda i, t: (i, 0))
    fixed = pl.BlockSpec((columns, LANES), lambda i, t: (0, 0))
    return call(
        self_project_back_body,
        "self_project_back",
        [((tokens, 3 * columns), LOW)],
        (grad_q, k, v, raw, own_fold, other_fold),
        grid=(tokens // rows,),
        in_specs=[row(columns), row(columns), row(columns), row(2 * columns), fixed, fixed],
        out_specs=[row(3 * columns)],
        scratch=[pltpu.VMEM((2, 2, columns, columns), LOW)] * 2,
        flops=16 * tokens * columns * columns,
        table=table,
    )[0]


def live_keys(table, own, keys):
    place = lax.broadcasted_iota(jnp.int32, (1, keys), 1)
    return place < jnp.where(own, table[OWN_LENGTH], table[OTHER_LENGTH])


def shard_of(first, rest, step, which):
    rows = first.shape[0]
    return first[...] if step == 0 else rest[step - 1, which * rows : (which + 1) * rows, :]


def middle_body(table, att, x, mod_own, mod_other, out_first, query_first, cross_first, *refs):
    pieces, (kv_own, kv_other) = refs[:8], refs[8:10]
    branch, after_low, queries_out, probs_out, text_out, after_cross, normed, rest = refs[10:]
    put_in_order(table, pieces, rest)
    count, rows, columns = att.shape
    keys = kv_own.shape[1]
    heads = columns // CROSS_HEAD
    own = own_image(table, table[BLOCK_FIRST], rows)
    y1 = jnp.zeros((rows, x.shape[1]), WIDE)
    for step in range(count):
        y1 += dot(att[turned(table, step, count)], shard_of(out_first, rest, step, 0))
    branch[...] = y1
    x1 = x[...].astype(WIDE) + pick(own, mod_own, mod_other, 2) * y1
    x1_low = x1.astype(LOW)
    after_low[...] = x1_low
    live = live_keys(table, own, keys)
    yc = jnp.zeros_like(x1)
    for step in range(count):
        queries = times_transposed(x1_low, shard_of(query_first, rest, step, 1)).astype(LOW)
        queries_out[step] = queries
        place = turned(table, step, count)
        mine, theirs = kv_own[place], kv_other[place]
        parts = []
        for head in range(heads):
            lanes = slice(head * CROSS_HEAD, (head + 1) * CROSS_HEAD)
            wide_lanes = slice(columns + head * CROSS_HEAD, columns + (head + 1) * CROSS_HEAD)
            q = queries[:, lanes]
            scores = jnp.where(
                own, times_transposed(q, mine[:, lanes]), times_transposed(q, theirs[:, lanes])
            ) * (1.0 / math.sqrt(CROSS_HEAD))
            scores = jnp.where(live, scores, MASKED_OUT)
            raised = jnp.exp(scores - jnp.max(scores, axis=-1, keepdims=True))
            probs = raised / jnp.sum(raised, axis=-1, keepdims=True)
            probs_out[step * heads + head] = probs
            low = probs.astype(LOW)
            parts.append(
                jnp.where(own, dot(low, mine[:, wide_lanes]), dot(low, theirs[:, wide_lanes]))
            )
        text = jnp.concatenate(parts, axis=1).astype(LOW)
        text_out[step] = text
        yc += dot(text, shard_of(cross_first, rest, step, 2))
    x2 = x1 + yc
    after_cross[...] = x2
    normed[...] = (
        x2 * inverse_size(x2) * (1.0 + pick(own, mod_own, mod_other, 4))
        + pick(own, mod_own, mod_other, 3)
    ).astype(LOW)


def middle_back_body(table, grad_own, grad_1, grad_2, grad_3, x2_in, upstream, branch, mod_own, mod_other, out_first, query_first, cross_first, rest, kv_own, kv_other, probs_in, queries_in, cross_grad, query_grad, attn_grad, attended_grad, after_grad, sums, kv_own_grad, kv_other_grad):
    count, rows, columns = queries_in.shape
    keys = kv_own.shape[1]
    heads = columns // CROSS_HEAD
    scale = 1.0 / math.sqrt(CROSS_HEAD)
    own = own_image(table, table[BLOCK_FIRST], rows)
    grad = with_own(grad_own, grad_1, grad_2, grad_3)
    x2 = x2_in[...]
    inverse = inverse_size(x2)
    xh = x2 * inverse
    sums[0:1], sums[1:2] = both_sums(own, grad)
    sums[2:3], sums[3:4] = both_sums(own, grad * xh)
    e = grad * (1.0 + pick(own, mod_own, mod_other, 4))
    dx2 = upstream[...].astype(WIDE) + inverse * (
        e - xh * jnp.mean(e * xh, axis=-1, keepdims=True)
    )
    dyc = dx2.astype(LOW)
    cross_grad[...] = dyc
    dx1 = dx2
    for step in range(count):
        doc = times_transposed(dyc, shard_of(cross_first, rest, step, 2)).astype(LOW)
        place = turned(table, step, count)
        mine, theirs = kv_own[place], kv_other[place]
        queries = queries_in[step]
        query_parts = []
        key_parts = ([], [])
        value_parts = ([], [])
        for head in range(heads):
            lanes = slice(head * CROSS_HEAD, (head + 1) * CROSS_HEAD)
            wide_lanes = slice(columns + head * CROSS_HEAD, columns + (head + 1) * CROSS_HEAD)
            do, q = doc[:, lanes], queries[:, lanes]
            probs = probs_in[step * heads + head]
            dp = jnp.where(
                own,
                times_transposed(do, mine[:, wide_lanes]),
                times_transposed(do, theirs[:, wide_lanes]),
            )
            ds = (probs * (dp - jnp.sum(probs * dp, axis=-1, keepdims=True))).astype(LOW)
            low = probs.astype(LOW)
            zero = jnp.zeros_like(ds)
            query_parts.append(
                jnp.where(own, dot(ds, mine[:, lanes]), dot(ds, theirs[:, lanes])) * scale
            )
            for image in range(2):
                mask = (lambda a: jnp.where(own, a, zero)) if image == 0 else (
                    lambda a: jnp.where(own, zero, a)
                )
                key_parts[image].append(over_tokens(mask(ds), q) * scale)
                value_parts[image].append(over_tokens(mask(low), do))
        dqc = jnp.concatenate(query_parts, axis=1).astype(LOW)
        query_grad[step] = dqc
        kv_own_grad[place] = jnp.concatenate(key_parts[0] + value_parts[0], axis=1).astype(LOW)
        kv_other_grad[place] = jnp.concatenate(key_parts[1] + value_parts[1], axis=1).astype(LOW)
        dx1 = dx1 + dot(dqc, shard_of(query_first, rest, step, 1))
    after_grad[...] = dx1
    sums[4:5], sums[5:6] = both_sums(own, dx1 * branch[...])
    sums[6:8] = jnp.zeros((2, sums.shape[1]), WIDE)
    dy1 = (dx1 * pick(own, mod_own, mod_other, 2)).astype(LOW)
    attn_grad[...] = dy1
    for step in range(count):
        attended_grad[turned(table, step, count)] = times_transposed(
            dy1, shard_of(out_first, rest, step, 0)
        ).astype(LOW)


def first_norm_back_body(table, grad_own, grad_1, grad_2, grad_3, after_grad, x, mod_own, mod_other, input_grad, sums):
    rows = x.shape[0]
    own = own_image(table, table[BLOCK_FIRST], rows)
    grad = with_own(grad_own, grad_1, grad_2, grad_3)
    wide = x[...].astype(WIDE)
    inverse = inverse_size(wide)
    xh = wide * inverse
    sums[0:1], sums[1:2] = both_sums(own, grad)
    sums[2:3], sums[3:4] = both_sums(own, grad * xh)
    sums[4:8] = jnp.zeros((4, sums.shape[1]), WIDE)
    e = grad * (1.0 + pick(own, mod_own, mod_other, 1))
    input_grad[...] = (
        after_grad[...] + inverse * (e - xh * jnp.mean(e * xh, axis=-1, keepdims=True))
    ).astype(LOW)


def output_body(table, branches, x2, upstream, mod_own, mod_other, output, sums):
    rows = x2.shape[0]
    own = own_image(table, table[BLOCK_FIRST], rows)
    branch = total(branches)
    sums[0:1], sums[1:2] = both_sums(own, upstream[...].astype(WIDE) * branch)
    sums[2:8] = jnp.zeros((6, sums.shape[1]), WIDE)
    output[...] = (x2[...] + pick(own, mod_own, mod_other, 5) * branch).astype(LOW)


def up_body(table, *refs):
    blocks, weight, (wide_out, low_out, ordered) = refs[:-4], refs[-4], refs[-3:]
    rows = blocks[0].shape[0]

    @pl.when(pl.program_id(0) == 0)
    def _():
        for step, block in enumerate(blocks):
            low = turned(table, step, len(blocks)) * rows
            ordered[pl.ds(pl.multiple_of(low, 16), rows), :] = block[...]

    up = times_transposed(ordered[...], weight[...])
    wide_out[...] = up
    low_out[...] = (up * logistic(up)).astype(LOW)


def up_project(table, blocks, weight):
    rows, width = blocks[0].shape
    tokens = len(blocks) * rows
    columns = 3 * LANES
    whole = lambda *shape: pl.BlockSpec(shape, lambda i, t: (0, 0))
    column = pl.BlockSpec((tokens, columns), lambda i, t: (0, i))
    return call(
        up_body,
        "up_project",
        [((tokens, weight.shape[0]), WIDE), ((tokens, weight.shape[0]), LOW), ((tokens, width), LOW)],
        (*blocks, weight),
        grid=(weight.shape[0] // columns,),
        in_specs=[whole(rows, width)] * len(blocks)
        + [pl.BlockSpec((columns, width), lambda i, t: (i, 0))],
        out_specs=[column, column, whole(tokens, width)],
        table=table,
    )


def fill(padded, block, rim):
    tokens = block.shape[0]
    edge = rim[...].astype(WIDE)
    padded[0:MAXW, :] = edge
    padded[MAXW : MAXW + tokens, :] = block.astype(WIDE)
    padded[MAXW + tokens : 2 * MAXW + tokens, :] = edge


def fill_masks(table, masks):
    tokens = masks.shape[1]
    place = table[FIRST] + lax.broadcasted_iota(jnp.int32, (tokens, LANES), 0)
    width = table[WIDTH]
    cut = table[CUT]
    late = place >= cut
    start = jnp.where(late, cut, 0)
    end = jnp.where(late, table[SEQ_TOKENS], cut)
    column = lax.bitwise_and(place, width - 1)
    one, none = jnp.ones((tokens, LANES), WIDE), jnp.zeros((tokens, LANES), WIDE)
    masks[0] = jnp.where(place - width >= start, one, none)
    masks[1] = jnp.where(place + width < end, one, none)
    masks[2] = jnp.where(column > 0, one, none)
    masks[3] = jnp.where(column < width - 1, one, none)


CHUNK = 64


def three_rows(table, padded, masks, low):
    width = table[WIDTH]
    above = padded[pl.ds(pl.multiple_of(MAXW + low - width, 16), CHUNK), :]
    below = padded[pl.ds(pl.multiple_of(MAXW + low + width, 16), CHUNK), :]
    own = padded[pl.ds(pl.multiple_of(MAXW + low, 16), CHUNK), :]
    rows = pl.ds(pl.multiple_of(low, 16), CHUNK)
    return above * masks[0, rows, :], own, below * masks[1, rows, :]


def nine_taps(rows, taps, left_mask, right_mask):
    mixed = [sum(rows[a] * taps[a][b] for a in range(3)) for b in range(3)]
    return (
        mixed[1]
        + left_mask * pltpu.roll(mixed[0], 1, 0)
        + right_mask * pltpu.roll(mixed[2], CHUNK - 1, 0)
    )


def taps_of(taps, flip):
    read = lambda a, b: taps[3 * a + b : 3 * a + b + 1, :]
    return [[read(2 - a, 2 - b) if flip else read(a, b) for b in range(3)] for a in range(3)]


def mix_body(table, value, gate, value_rim, gate_rim, value_taps, gate_taps, grad_hidden, hidden, grads, value_pad, gate_pad, masks):
    @pl.when(pl.program_id(0) == 0)
    def _():
        fill_masks(table, masks)

    fill(value_pad, value[...], value_rim)
    fill(gate_pad, gate[...], gate_rim)
    value_weights, gate_weights = taps_of(value_taps, False), taps_of(gate_taps, False)

    @pl.loop(0, value.shape[0] // CHUNK)
    def _(index):
        low = index * CHUNK
        rows = pl.ds(pl.multiple_of(low, CHUNK), CHUNK)
        left, right = masks[2, rows, :], masks[3, rows, :]
        mv = nine_taps(three_rows(table, value_pad, masks, low), value_weights, left, right)
        mg = nine_taps(three_rows(table, gate_pad, masks, low), gate_weights, left, right)
        sigma = logistic(mg)
        gated = mg * sigma
        hidden[rows, :] = (mv * gated).astype(LOW)
        dh = grad_hidden[rows, :]
        grads[0, rows, :] = (dh * gated).astype(LOW)
        grads[1, rows, :] = (dh * mv * (sigma * (1.0 + mg * (1.0 - sigma)))).astype(LOW)


def mix(table, activated, rim, taps, grad_hidden):
    tokens, wide = activated.shape
    columns = wide // 2
    tiles = columns // LANES
    block = lambda r, shift: pl.BlockSpec((r, LANES), lambda i, t: (0, i + shift))
    pad = pltpu.VMEM((tokens + 2 * MAXW, LANES), WIDE)
    return call(
        mix_body,
        "mix",
        [((tokens, columns), LOW), ((2, tokens, columns), LOW)],
        (activated, activated, rim, rim, taps, taps, grad_hidden),
        grid=(tiles,),
        in_specs=[
            block(tokens, 0),
            block(tokens, tiles),
            block(MAXW, 0),
            block(MAXW, tiles),
            block(taps.shape[0], 0),
            block(taps.shape[0], tiles),
            block(tokens, 0),
        ],
        out_specs=[
            block(tokens, 0),
            pl.BlockSpec((2, tokens, LANES), lambda i, t: (0, 0, i)),
        ],
        scratch=[pad, pad, pltpu.VMEM((4, tokens, LANES), WIDE)],
        flops=6000 * tokens * columns // 2,
        table=table,
    )


def mix_back_body(table, grads, grads_rim, activated, rim, taps, up, grad_up, tap_grads, grad_pad, act_pad, masks):
    @pl.when(pl.program_id(0) == 0)
    def _():
        fill_masks(table, masks)

    fill(grad_pad, grads[0], grads_rim.at[0])
    fill(act_pad, activated[...], rim)
    weights = taps_of(taps, True)

    def step(index, sums):
        low = index * CHUNK
        rows = pl.ds(pl.multiple_of(low, CHUNK), CHUNK)
        left, right = masks[2, rows, :], masks[3, rows, :]
        mine = three_rows(table, grad_pad, masks, low)
        dact = nine_taps(mine, weights, left, right)
        given = up[rows, :]
        sigma = logistic(given)
        grad_up[rows, :] = (dact * (sigma * (1.0 + given * (1.0 - sigma)))).astype(LOW)
        acts = three_rows(table, act_pad, masks, low)
        turned = (
            right * pltpu.roll(mine[1], CHUNK - 1, 0),
            mine[1],
            left * pltpu.roll(mine[1], 1, 0),
        )
        return tuple(
            sums[3 * a + b]
            + jnp.sum((acts[a] * turned[b]).reshape(CHUNK // 8, 8, LANES), axis=0)
            for a in range(3)
            for b in range(3)
        )

    zero = jnp.zeros((8, LANES), WIDE)
    sums = lax.fori_loop(0, activated.shape[0] // CHUNK, step, (zero,) * 9)
    for tap in range(9):
        tap_grads[tap : tap + 1, :] = jnp.sum(sums[tap], axis=0, keepdims=True)
    tap_grads[9:16, :] = jnp.zeros((7, LANES), WIDE)


def mix_back(table, grads, grads_rim, activated, rim, taps, up):
    tokens, wide = activated.shape
    columns = wide // 2
    tiles = columns // LANES
    block = lambda r: pl.BlockSpec((r, LANES), lambda i, t: (0, i))
    half = lambda r: pl.BlockSpec(
        (1, r, LANES), lambda i, t: (lax.div(i, tiles), 0, lax.rem(i, tiles))
    )
    pad = pltpu.VMEM((tokens + 2 * MAXW, LANES), WIDE)
    return call(
        mix_back_body,
        "mix_back",
        [((tokens, wide), LOW), ((16, wide), WIDE)],
        (grads, grads_rim, activated, rim, taps, up),
        grid=(2 * tiles,),
        in_specs=[half(tokens), half(MAXW), block(tokens), block(MAXW), block(taps.shape[0]), block(tokens)],
        out_specs=[block(tokens), block(16)],
        scratch=[pad, pad, pltpu.VMEM((4, tokens, LANES), WIDE)],
        flops=6000 * tokens * columns,
        table=table,
    )


def eighth_body(table, *refs):
    weights, out, joined = refs[:-2], refs[-2], refs[-1]
    low = 0
    for weight in weights:
        joined[low : low + weight.shape[0], :] = weight[...]
        low += weight.shape[0]
    rows = out.shape[0]
    out[...] = joined[pl.ds(pl.multiple_of(table[0] * rows, 16), rows), :]


def put_in_order(table, pieces, out):
    steps, rows = pieces[0].shape[0], pieces[0].shape[1]
    for place, piece in enumerate(pieces):
        block = lax.bitwise_xor(table[ROW_PLACE], place)
        for step in range(steps):
            out[step, pl.ds(pl.multiple_of(block * rows, 16), rows), :] = piece[step]


def after(value, *others):
    return lax.optimization_barrier((value, others))[0]


def fetch_eighths(weights):
    columns = weights[0].shape[1]
    rows = -(-sum(weight.shape[0] for weight in weights) // LANES) * 16
    eighth = call(
        eighth_body,
        "eighth",
        [((rows, columns), weights[0].dtype)],
        weights,
        scratch=[pltpu.VMEM((8 * rows, columns), weights[0].dtype)],
        table=(lax.axis_index("seq") % 8).reshape(1).astype(jnp.int32),
    )[0]
    return jnp.stack([from_behind(eighth, step) for step in range(1, lax.axis_size("tp"))])


def share_eighths(fetched, ready):
    count = lax.axis_size("seq")
    far = lambda flip: lax.ppermute(fetched, "seq", [(k, k ^ flip) for k in range(count)])
    pieces = []
    for piece in [fetched] + after([far(2), far(4), far(6)], *ready):
        pieces += [piece, swapped(piece, "seq", 0)]
    return pieces


def token_block(values, place):
    count = lax.axis_size("tp")
    size = values.shape[0] // count
    return lax.dynamic_slice_in_dim(values, (place % count) * size, size, 0)


def own_rows(values):
    rows = values.shape[0] // lax.axis_size("tp")
    return pl.BlockSpec((rows, values.shape[1]), lambda i, t: (t[TP_PLACE], 0))


def placed_blocks(blocks):
    count = len(blocks)
    place = lax.axis_index("tp")
    result = jnp.zeros((count,) + blocks[0].shape, blocks[0].dtype)
    for step in range(count):
        result = lax.dynamic_update_index_in_dim(result, blocks[step], (place - step) % count, 0)
    return result.reshape((count * blocks[0].shape[0],) + blocks[0].shape[1:])


def all_blocks(block):
    return [block] + [from_behind(block, step) for step in range(1, lax.axis_size("tp"))]


def product(left, right):
    count = lax.axis_size("tp")
    return dot(left, right).astype(LOW).reshape(count, left.shape[0] // count, right.shape[1])


def spread(blocks):
    count = lax.axis_size("tp")
    place = lax.axis_index("tp")
    return [
        from_behind(
            lax.dynamic_index_in_dim(blocks, (place + step) % count, 0, keepdims=False), step
        )
        for step in range(1, count)
    ]


def own_block(blocks):
    return pl.BlockSpec((1,) + blocks.shape[1:], lambda i, t: (t[TP_PLACE], 0, 0))


def with_own(own, *others):
    result = own[0].astype(WIDE)
    for other in others:
        result += other[...].astype(WIDE)
    return result


def total(parts):
    result = parts[0].astype(WIDE)
    for place in range(1, parts.shape[0]):
        result += parts[place].astype(WIDE)
    return result


def turned(table, step, count):
    return lax.rem(table[TP_PLACE] + count - step, count)


def same_everywhere(block):
    count = lax.axis_size("tp")
    flipped = lambda flip: lax.ppermute(block, "tp", [(k, k ^ flip) for k in range(count)])
    return (block + flipped(1)) + (flipped(2) + flipped(3))


def sum_rows(grad):
    return lax.optimization_barrier(
        lax.psum_scatter(grad.astype(LOW), "seq", scatter_dimension=0, tiled=True)
    )


def square_body(table, dyc, text, x1, dqc, dy1, att, kv_mine, kv_theirs, out, kv_out):
    kv_out[...] = (kv_mine[...].astype(WIDE) + kv_theirs[...].astype(WIDE)).astype(LOW)
    parts = [
        over_tokens(left[...], right[0]) for left, right in ((dyc, text), (x1, dqc), (dy1, att))
    ]
    rest = out.shape[1] - sum(part.shape[1] for part in parts)
    if rest:
        parts.append(jnp.zeros((out.shape[0], rest), WIDE))
    out[...] = jnp.concatenate(parts, axis=1).astype(LOW)


def square_parts(table, lefts, rights, kv_mine, kv_theirs):
    rows, width = lefts[0].shape
    count, _, columns = rights[0].shape
    block = -(-3 * columns // LANES) * LANES
    whole = pl.BlockSpec((rows, width), lambda i, t: (0, 0))
    one = pl.BlockSpec((1, rows, columns), lambda i, t: (turned(t, i, count), 0, 0))
    still = pl.BlockSpec((1, rows, columns), lambda i, t: (i, 0, 0))
    kv = pl.BlockSpec((1,) + kv_mine.shape[1:], lambda i, t: (i, 0, 0))
    return call(
        square_body,
        "square_parts",
        [((width, count * block), LOW), (kv_mine.shape, LOW)],
        [array for pair in zip(lefts, rights) for array in pair] + [kv_mine, kv_theirs],
        grid=(count,),
        in_specs=[whole, one, whole, one, whole, still, kv, kv],
        out_specs=[pl.BlockSpec((width, block), lambda i, t: (0, i)), kv],
        table=table,
    )


def ffn_body(table, grad_ffn, hidden, normed, grad_up, out):
    step = pl.program_id(0)

    @pl.when(step == 0)
    def _():
        out[...] = over_tokens(grad_ffn[...], hidden[...]).astype(LOW)

    @pl.when(step > 0)
    def _():
        out[...] = over_tokens(normed[...], grad_up[...]).astype(LOW)


def ffn_parts_of(table, grad_ffn, hidden, normed, grad_up):
    tokens, width = normed.shape
    columns = hidden.shape[1]
    whole = pl.BlockSpec((tokens, width), lambda i, t: (0, 0))
    return call(
        ffn_body,
        "ffn_parts",
        [((width, 3 * columns), LOW)],
        (grad_ffn, hidden, normed, grad_up),
        grid=(3,),
        in_specs=[
            whole,
            pl.BlockSpec((tokens, columns), lambda i, t: (0, 0)),
            whole,
            pl.BlockSpec((tokens, columns), lambda i, t: (0, jnp.maximum(i - 1, 0))),
        ],
        out_specs=[pl.BlockSpec((width, columns), lambda i, t: (0, i))],
        table=table,
    )[0]


def late_body(table, normed, grad_projected, text, kv_grads, out):
    first = over_tokens(normed[...], grad_projected[...]).astype(LOW)
    second = over_tokens(text[...], total(kv_grads).astype(LOW)).astype(LOW)
    out[...] = jnp.concatenate([first, second], axis=1)


def shards(
    hidden_in,
    cotangent,
    modulation,
    text_states,
    image_shapes,
    text_lengths,
    qkv_weight,
    attn_out_weight,
    cross_q_weight,
    cross_kv_weight,
    cross_out_weight,
    up_weight,
    conv_weight,
    down_weight,
):
    tokens_here, width = hidden_in.shape
    context = text_states.shape[1]
    keys = -(-context // 16) * 16
    self_cols = qkv_weight.shape[2]
    cross_cols = cross_q_weight.shape[1]
    ffn_cols = up_weight.shape[2]
    ffn_pad = -(-ffn_cols // LANES) * LANES
    count = lax.axis_size("tp")
    tp_index = lax.axis_index("tp")
    block_size = tokens_here // count
    seq_index = lax.axis_index("seq")
    side = seq_index % 2
    first_half = side == 0
    pair = seq_index - side
    pair_shapes = lax.dynamic_slice_in_dim(image_shapes, pair, 2, 0)
    row_width = pair_shapes[0, 1]
    lengths = lax.dynamic_slice_in_dim(text_lengths, pair, 2, 0)
    first_place = side * tokens_here
    table = jnp.stack(
        [
            first_place,
            pair_shapes[0, 0] * row_width,
            side,
            row_width,
            jnp.where(first_half, lengths[0], lengths[1]),
            jnp.where(first_half, lengths[1], lengths[0]),
            first_place + tp_index * block_size,
            jnp.int32(2 * tokens_here),
            tp_index,
            seq_index % 8,
        ]
    ).astype(jnp.int32)

    mod_own = modulation[0]
    mod_other = swapped(mod_own, "seq", 0).astype(WIDE)
    mod_own = mod_own.astype(WIDE)
    weights = [attn_out_weight.T, cross_q_weight.T, cross_out_weight.T]
    fetched = fetch_eighths(weights)
    qkv_flat = qkv_weight.transpose(1, 2, 0).reshape(3 * self_cols, width)
    text_rows = jnp.pad(text_states[0], ((0, keys - context), (0, 0)))
    kv_here = times_transposed(
        text_rows, cross_kv_weight.transpose(1, 2, 0).reshape(2 * cross_cols, width)
    ).astype(LOW)
    kv_sent_first = jnp.broadcast_to(kv_here[None], (count,) + kv_here.shape)
    normed_low, raw, q, k, v, part_own, part_other = self_project(
        table, after(hidden_in, kv_sent_first), mod_own, mod_other, qkv_flat, self_cols
    )
    theirs = swapped(jnp.stack([part_own, part_other]), "seq", 0)
    fetched = after(fetched, q)
    kernel_own, kernel_other = part_own + theirs[1], part_other + theirs[0]
    attended, attended_wide, denominator = self_attend(
        table, after(q, kv_here), kernel_own, kernel_other
    )

    whole = pl.BlockSpec(memory_space=pltpu.VMEM)
    x_rows, upstream_rows = own_rows(hidden_in), own_rows(cotangent)
    up_flat = jnp.pad(
        after(up_weight.transpose(1, 2, 0), attended), ((0, 0), (0, ffn_pad - ffn_cols), (0, 0))
    ).reshape(2 * ffn_pad, width)
    down_flat = jnp.pad(after(down_weight.T, attended), ((0, ffn_pad - ffn_cols), (0, 0)))
    taps = (
        jnp.pad(conv_weight, ((0, 7), (0, 0), (0, ffn_pad - ffn_cols)))
        .reshape(16, 2 * ffn_pad)
        .astype(WIDE)
    )
    gate_rows = jnp.where(
        (first_place + jnp.arange(tokens_here, dtype=jnp.int32) >= table[CUT])[:, None] == (side == 1),
        mod_own[5:6],
        mod_other[5:6],
    )
    grad_ffn = (cotangent.astype(WIDE) * gate_rows).astype(LOW)
    grad_hidden = times_transposed(grad_ffn, down_flat)
    ready = (up_flat, down_flat, taps, grad_hidden)
    split_tokens = lambda values: values.reshape(count, block_size, values.shape[1])
    kv_own = exchanged(kv_sent_first)
    attended_blocks = exchanged(after(split_tokens(attended), kv_own))
    kv_own = after(kv_own, *ready)
    kv_other = swapped(kv_own, "seq", 0)
    pieces = share_eighths(fetched, (*ready, attended_blocks))
    all_heads = count * cross_cols // CROSS_HEAD
    branch, after_low, queries, probs, text_low, after_cross, normed_two, rest = call(
        middle_body,
        "middle",
        [
            ((block_size, width), WIDE),
            ((block_size, width), LOW),
            ((count, block_size, cross_cols), LOW),
            ((all_heads, block_size, keys), WIDE),
            ((count, block_size, cross_cols), LOW),
            ((block_size, width), WIDE),
            ((block_size, width), LOW),
            ((count - 1, 8 * fetched.shape[1], width), LOW),
        ],
        (attended_blocks, hidden_in, mod_own, mod_other, *weights, *pieces, kv_own, kv_other),
        in_specs=[whole, x_rows] + [whole] * 15,
        flops=60 * block_size * width * width,
        table=table,
    )

    up_wide, activated, normed_two_low = up_project(table, all_blocks(normed_two), up_flat)
    rim = swapped(jnp.where(first_half, activated[-MAXW:], activated[:MAXW]), "seq", 0)
    hidden, grads = mix(table, activated, rim, taps, grad_hidden)
    grads_rim = swapped(jnp.where(first_half, grads[:, -MAXW:], grads[:, :MAXW]), "seq", 0)
    branch_sent = product(hidden, down_flat)
    grad_up, tap_part = mix_back(
        table, grads, grads_rim, activated, rim, taps, after(up_wide, branch_sent)
    )
    branches = exchanged(branch_sent)
    norm_two_sent = product(grad_up, up_flat)
    grad_norm_two = spread(norm_two_sent)
    output_block, output_sums = call(
        output_body,
        "output",
        [((block_size, width), LOW), ((8, width), WIDE)],
        (branches, after_cross, cotangent, mod_own, mod_other),
        in_specs=[whole, whole, upstream_rows, whole, whole],
        table=table,
    )
    ffn_parts = ffn_parts_of(
        table, grad_ffn, after(hidden, norm_two_sent, output_block), normed_two_low, grad_up
    )
    ffn_rows = sum_rows(after(ffn_parts, grad_norm_two))
    output_blocks = all_blocks(after(output_block, grad_norm_two))

    (
        cross_grad,
        query_grad,
        attn_grad,
        attended_grad,
        after_grad,
        middle_sums,
        kv_own_grad,
        kv_other_grad,
    ) = call(
        middle_back_body,
        "middle_back",
        [
            ((block_size, width), LOW),
            ((count, block_size, cross_cols), LOW),
            ((block_size, width), LOW),
            ((count, block_size, self_cols), LOW),
            ((block_size, width), WIDE),
            ((8, width), WIDE),
            ((count, keys, 2 * cross_cols), LOW),
            ((count, keys, 2 * cross_cols), LOW),
        ],
        (
            after(norm_two_sent, ffn_parts, output_block),
            *grad_norm_two,
            after_cross,
            cotangent,
            branch,
            mod_own,
            mod_other,
            *weights,
            rest,
            kv_own,
            kv_other,
            probs,
            queries,
        ),
        in_specs=[own_block(norm_two_sent)] + [whole] * 4 + [upstream_rows] + [whole] * 11,
        flops=120 * block_size * width * width,
        table=table,
    )

    grad_blocks = exchanged(after(attended_grad, output_blocks))
    kv_theirs = swapped(after(kv_other_grad, output_blocks), "seq", 0)
    squares, kv_sent = square_parts(
        table,
        (cross_grad, after_low, attn_grad),
        (text_low, query_grad, after(attended_blocks, attended_grad)),
        kv_own_grad,
        kv_theirs,
    )
    square_rows = sum_rows(after(squares, grad_blocks))
    kv_sent = after(kv_sent, grad_blocks)
    kv_parts = exchanged(kv_sent)
    grad_blocks = after(grad_blocks, squares, kv_sent, ffn_rows)
    grad_q, back_own, back_other = self_back(
        table, grad_blocks, q, attended_wide, denominator, kernel_own, kernel_other
    )
    back_theirs = swapped(jnp.stack([back_own, back_other]), "seq", 0)
    grad_projected = self_project_back(
        table,
        grad_q,
        k,
        v,
        raw,
        back_own + back_theirs[1],
        back_other + back_theirs[0],
    )
    normed_sent = product(grad_projected, qkv_flat)
    grad_normed = spread(normed_sent)
    late_parts = call(
        late_body,
        "late_parts",
        [((width, 3 * self_cols + 2 * cross_cols), LOW)],
        (normed_low, after(grad_projected, normed_sent), text_rows, kv_parts),
        table=table,
    )[0]
    late_rows = sum_rows(after(late_parts, square_rows, grad_normed))
    square_sent = square_rows.reshape(square_rows.shape[0], count, -1).transpose(1, 0, 2)
    input_block, first_sums = call(
        first_norm_back_body,
        "first_norm_back",
        [((block_size, width), LOW), ((8, width), WIDE)],
        (
            after(normed_sent, late_parts, square_sent),
            *grad_normed,
            after_grad,
            hidden_in,
            mod_own,
            mod_other,
        ),
        in_specs=[own_block(normed_sent)] + [whole] * 4 + [x_rows, whole, whole],
        table=table,
    )
    square_parts_here = exchanged(square_sent)
    square_grads = total(square_parts_here)[:, : 3 * self_cols]
    pairs = jnp.concatenate([first_sums[:4], middle_sums[4:6], middle_sums[:4], output_sums[:2]])
    pairs = pairs.reshape(6, 2, width)
    pairs = pairs[:, 0] + swapped(pairs[:, 1], "seq", 0)
    modulation_grad = same_everywhere(pairs)
    input_block = after(input_block, square_parts_here, modulation_grad)
    conv_sum = after(tap_part[:9], input_block)
    for place in range(lax.axis_size("seq").bit_length() - 1):
        conv_sum = conv_sum + swapped(conv_sum, "seq", place)
    late_rows = late_rows.astype(WIDE)
    qkv_grad = late_rows[:, : 3 * self_cols].reshape(-1, 3, self_cols)
    ckv_grad = late_rows[:, 3 * self_cols :].reshape(-1, 2, cross_cols)
    output = placed_blocks(output_blocks)
    input_blocks = after(all_blocks(input_block), qkv_grad, ckv_grad, square_grads, output)
    input_grad = placed_blocks(input_blocks).astype(WIDE)

    return (
        output,
        input_grad,
        modulation_grad[None],
        qkv_grad,
        square_grads[:, 2 * self_cols :],
        square_grads[:, self_cols : 2 * self_cols],
        ckv_grad,
        square_grads[:, :self_cols],
        ffn_rows[:, ffn_pad:].astype(WIDE).reshape(-1, 2, ffn_pad)[:, :, :ffn_cols],
        conv_sum.reshape(9, 2, ffn_pad)[:, :, :ffn_cols],
        ffn_rows[:, :ffn_cols].astype(WIDE),
    )


def solution(mesh):
    placed = (
        P("seq", None),
        P("seq", None),
        P("seq", None, None),
        P("seq", None, None),
        P(),
        P(),
        P(None, None, "tp"),
        P(None, "tp"),
        P(None, "tp"),
        P(None, None, "tp"),
        P(None, "tp"),
        P(None, None, "tp"),
        P(None, None, "tp"),
        P(None, "tp"),
    )
    return jax.shard_map(
        shards,
        mesh=mesh,
        in_specs=placed,
        out_specs=(
            P("seq", None),
            P("seq", None),
            P("seq", None, None),
            P("seq", None, "tp"),
            P("seq", "tp"),
            P("seq", "tp"),
            P("seq", None, "tp"),
            P("seq", "tp"),
            P("seq", None, "tp"),
            P(None, None, "tp"),
            P("seq", "tp"),
        ),
        check_vma=False,
    )
```
